128 devices in a mesh: branch: 8 (over z, core), tensor: 16 (over x, y).
Axes of the slice: x: 4, y: 4, z: 4, core: 2. Of those that a mesh axis runs over, the one named last changes fastest.
Arguments:
- tokens: bfloat16 [4096, 8192], P('branch', 'tensor'), may hold values from -6 to 6
- gain: bfloat16 [8192], replicated, may hold values from 0.099609375 to 1.8984375
- w_query: bfloat16 [8192, 8192], P(None, 'tensor'), may hold values from -0.0625 to 0.0625
- w_keyvalue: bfloat16 [2, 8192, 1024], P(None, 'tensor'), may hold values from -0.0625 to 0.0625
- w_output: bfloat16 [8192, 8192], P('tensor'), may hold values from -0.0625 to 0.0625
- cache: bfloat16 [2, 128, 64, 1024], P(None, 'branch'), may hold values from -800 to 800
- parents: int32 [64, 4], replicated, may hold values from 0 to 127, as said below
- lengths: int32 [64], replicated, may hold values from 1 to 4
Outputs:
- attended: bfloat16 [4096, 8192], P('branch', 'tensor')
The draws below stay inside these ranges and needn't reach their ends.
Inputs may be any that keep to these rules, and one draw needn't show every extreme that they name: `parents`: block p lies with owner p // 16. The entries of one branch's list lie with different owners; entries at or past the branch's length are unused but follow the same rules. The branches of one index of branch name at most 4 distinct blocks of any one owner, and exactly 4 of some owner.
All inputs are finite; a program needn't handle non-finite values.
Results may differ from the reference program's by a relative error of at most 0.025.
Values may be sent and summed in bfloat16 or wider, within the bound.
No kernel may reach another device: no remote copies, remote signals or barrier semaphores. Data moves between devices by JAX's collectives and lax.ppermute only.
A program may use at most 128 MiB of HBM per device.

```python
import math
import jax
import jax.numpy as jnp
from jax import lax

D = 8192
HEADS = 64
KVH = 8
HD = 128
PB = 64
PDEPTH = 4
BR_DEV = 8
NB_DEV = 16
CAP = 4
BRANCHES = 64
NBLK = 128
ROWS = 4096
N_TENSOR = 16


def draw_parents(key, part):
    key = jax.random.fold_in(key, 11)
    groups = BRANCHES // BR_DEV
    key_owner, key_select, key_shift, key_pick = jax.random.split(key, 4)
    owner_scores = jax.random.randint(key_owner, (groups, groups), 0, 4096) * groups + jnp.arange(groups, dtype=jnp.int32)[None, :]
    owner_order = jnp.argsort(owner_scores, axis=1).astype(jnp.int32)
    select_scores = jax.random.randint(key_select, (groups, groups, NB_DEV), 0, 4096) * NB_DEV + jnp.arange(NB_DEV, dtype=jnp.int32)
    chosen = jnp.argsort(select_scores, axis=2).astype(jnp.int32)[:, :, :CAP]
    shifts = jax.random.randint(key_shift, (groups, PDEPTH), 0, CAP)
    picks = jax.random.randint(key_pick, (groups, BR_DEV, PDEPTH), 0, CAP)
    member = jnp.arange(BR_DEV, dtype=jnp.int32)[None, :, None]
    slots = jnp.where(member < CAP, (member + shifts[:, None, :]) % CAP, picks)
    owners = jnp.broadcast_to(owner_order[:, None, :PDEPTH], (groups, BR_DEV, PDEPTH))
    group_index = jnp.broadcast_to(jnp.arange(groups, dtype=jnp.int32)[:, None, None], (groups, BR_DEV, PDEPTH))
    local = chosen[group_index, owners, slots]
    return (owners * NB_DEV + local).reshape(groups * BR_DEV, PDEPTH).astype(jnp.int32)


def draw_lengths(key, part):
    key = jax.random.fold_in(key, 5)
    key_len, key_spot = jax.random.split(key)
    drawn = jax.random.randint(key_len, (BRANCHES,), 1, PDEPTH + 1)
    spot = jax.random.randint(key_spot, (), 0, BRANCHES)
    return jnp.where(jnp.arange(BRANCHES) == spot, PDEPTH, drawn).astype(jnp.int32)


def draw_cache(key, part):
    key = jax.random.fold_in(key, 7)
    key_base = jax.random.fold_in(key, 0)
    shape = (2, NBLK, PB, KVH * HD)
    return jnp.clip(jax.random.normal(key_base, shape, jnp.float32), -6.0, 6.0).astype(jnp.bfloat16)


def level_of(own_key, extent, pieces, low, high):
    def one(position, blocks):
        heights = jax.random.uniform(jax.random.fold_in(jax.random.fold_in(own_key, 6), position), (blocks,), jnp.float32, low / len(pieces), high / len(pieces))
        return jnp.repeat(jnp.exp(heights), extent[position] // blocks).reshape((-1,) + (1,) * (len(extent) - position - 1))

    level = one(*pieces[0])
    for cut in pieces[1:]:
        level = level * one(*cut)
    return level


def noise(stream_key, extent, deviation, bound, pieces=(), held_as=jnp.bfloat16):
    loudness = level_of(stream_key, extent, pieces, -0.22, 0.18) if pieces else 1.0
    result = jax.random.normal(stream_key, extent, jnp.float32) * deviation * loudness
    return jnp.minimum(jnp.maximum(result, -bound), bound).astype(held_as)


def setup_inputs(seed: int = 0) -> dict:
    streams_of = jax.random.split(jax.random.key(seed), 9)
    return {
        "tokens": noise(streams_of[0], (ROWS, D), 1.0, 6.0, ((0, 8), (1, 16))),
        "gain": jnp.clip(1.0 + 0.18 * jax.random.normal(streams_of[1], (D,), jnp.float32), 0.099609375, 1.8984375).astype(jnp.bfloat16),
        "w_query": noise(streams_of[2], (D, HEADS * HD), D ** -0.5, 0.0625, ((1, 16),)),
        "w_keyvalue": noise(streams_of[3], (2, D, KVH * HD), D ** -0.5, 0.0625, ((1, 16),)),
        "w_output": noise(streams_of[4], (HEADS * HD, D), (HEADS * HD) ** -0.5, 0.0625, ((0, 16),)),
        "cache": draw_cache(jax.random.fold_in(streams_of[8], 71), 0),
        "parents": draw_parents(jax.random.fold_in(streams_of[8], 71), 0),
        "lengths": draw_lengths(jax.random.fold_in(streams_of[8], 71), 0),
    }


def normalize(tokens, gain):
    values = tokens.astype(jnp.float32)
    meansq = lax.optimization_barrier(jnp.mean(values * values, axis=-1, keepdims=True))
    return (values * lax.rsqrt(meansq + 1e-06) * gain.astype(jnp.float32)).astype(jnp.bfloat16)

def rotate(values, positions, heads):
    halfway = HD // 2
    frequency = jnp.exp(jnp.arange(halfway, dtype=jnp.float32) * (-2.0 * math.log(1000000.0) / HD))
    angles = positions.astype(jnp.float32)[:, None] * frequency[None, :]
    cos_part = jnp.cos(angles)[:, None, :]
    sin_part = jnp.sin(angles)[:, None, :]
    shaped = values.reshape(values.shape[0], heads, HD)
    leading = shaped[..., :halfway]
    trailing = shaped[..., halfway:]
    joined = jnp.concatenate([leading * cos_part - trailing * sin_part, trailing * cos_part + leading * sin_part], axis=-1)
    return joined.reshape(values.shape[0], heads * HD)

def visible(lengths):
    span = PDEPTH * PB + PB
    column = jnp.arange(span, dtype=jnp.int32)
    within = jnp.arange(PB, dtype=jnp.int32)
    prefix_ok = (column[None, None, :] < PDEPTH * PB) & ((column // PB)[None, None, :] < lengths[:, None, None])
    own_ok = (column[None, None, :] >= PDEPTH * PB) & ((column - PDEPTH * PB)[None, None, :] <= within[None, :, None])
    return prefix_ok | own_ok

def reference(tokens, gain, w_query, w_keyvalue, w_output, cache, parents, lengths):
    normed = normalize(tokens, gain)
    positions = (jnp.repeat(lengths, PB) * PB + jnp.tile(jnp.arange(PB, dtype=jnp.int32), BRANCHES)).astype(jnp.int32)
    query = rotate(jnp.dot(normed, w_query, preferred_element_type=jnp.float32), positions, HEADS).astype(jnp.bfloat16)
    new_keys = rotate(jnp.dot(normed, w_keyvalue[0], preferred_element_type=jnp.float32), positions, KVH).astype(jnp.bfloat16)
    new_values = jnp.dot(normed, w_keyvalue[1], preferred_element_type=jnp.float32).astype(jnp.bfloat16)
    flat_ids = parents.reshape(-1).astype(jnp.int32)
    pre_keys = cache[0][flat_ids].reshape(BRANCHES, PDEPTH * PB, KVH, HD)
    pre_values = cache[1][flat_ids].reshape(BRANCHES, PDEPTH * PB, KVH, HD)
    keys = jnp.concatenate([pre_keys, new_keys.reshape(BRANCHES, PB, KVH, HD)], axis=1)
    values = jnp.concatenate([pre_values, new_values.reshape(BRANCHES, PB, KVH, HD)], axis=1)
    allowed = visible(lengths)
    group_size = HEADS // KVH
    queries = query.reshape(BRANCHES, PB, KVH, group_size, HD)
    scale = 1.0 / math.sqrt(HD)

    def per_head(items):
        q_group, k_group, v_group = items
        scores = jnp.einsum('bigd,bjd->bgij', q_group.astype(jnp.float32), k_group.astype(jnp.float32)) * scale
        scores = jnp.where(allowed[:, None], scores, -1e+30)
        highest = lax.optimization_barrier(jnp.max(scores, axis=-1, keepdims=True))
        expo = jnp.exp(scores - highest)
        probs = (expo / lax.optimization_barrier(jnp.sum(expo, axis=-1, keepdims=True))).astype(jnp.bfloat16)
        mixed = jnp.einsum('bgij,bjd->bigd', probs.astype(jnp.float32), v_group.astype(jnp.float32))
        return mixed.astype(jnp.bfloat16)
    mixed = lax.map(per_head, (jnp.moveaxis(queries, 2, 0), jnp.moveaxis(keys, 2, 0), jnp.moveaxis(values, 2, 0)))
    heads_out = jnp.moveaxis(mixed, 0, 2).reshape(ROWS, HEADS * HD)
    block = HEADS * HD // N_TENSOR
    total = jnp.zeros((ROWS, D), jnp.float32)
    for member in range(N_TENSOR):
        partial_term = jnp.dot(heads_out[:, member * block:(member + 1) * block], w_output[member * block:(member + 1) * block], preferred_element_type=jnp.float32)
        rounded = lax.optimization_barrier(partial_term.astype(jnp.bfloat16))
        total = total + rounded.astype(jnp.float32)
    return total.astype(jnp.bfloat16)
```

```python
import math

import jax
import jax.numpy as jnp
from jax import lax
from jax.experimental import pallas as pl
from jax.experimental.pallas import tpu as pltpu
from jax.sharding import PartitionSpec as P

HEADS = 64
KVH = 8
HD = 128
PB = 64
PDEPTH = 4
HALF = 256
AXES = ("branch", "tensor")
F32 = jnp.float32
BF16 = jnp.bfloat16
MIB = 1024 * 1024


def pairs(move):
    table = []
    for z in range(4):
        for c in range(2):
            for x in range(4):
                for y in range(4):
                    z2, c2, x2, y2 = move(z, c, x, y)
                    target = ((z2 % 4) * 2 + c2 % 2) * 16 + (x2 % 4) * 4 + y2 % 4
                    table.append(((z * 2 + c) * 16 + x * 4 + y, target))
    return table


HOPS = {}
for step in (1, -1):
    HOPS["first", step] = pairs(
        lambda z, c, x, y, s=step: (z, c, x, y + s) if c == 0 else (z, c, x + s, y)
    )
    HOPS["second", step] = pairs(
        lambda z, c, x, y, s=step: (z, c, x + s, y) if c == 0 else (z, c, x, y + s)
    )
HOPS["twin", 1] = pairs(lambda z, c, x, y: (z, c, x, y ^ 1))


def hop(value, axis, step):
    return lax.ppermute(value, AXES, HOPS[axis, step])


def both(forward, backward, axis):
    return hop(forward, axis, 1), hop(backward, axis, -1)


def stack_rows(*parts):
    return jnp.concatenate(parts, axis=0)


def plus(base, *terms):
    total = base.astype(F32)
    for term in terms:
        total = total + term.astype(F32)
    return total.astype(BF16)


def pack(block):
    quarter = block.shape[0] // 4
    return jnp.concatenate([block[k * quarter : (k + 1) * quarter] for k in range(4)], axis=1)


def unpack(block):
    return jnp.concatenate([block[:, k * HD : (k + 1) * HD] for k in range(4)], axis=0)


def params(mebibytes):
    return pltpu.CompilerParams(vmem_limit_bytes=mebibytes * MIB)


def kv_partial(tokens, gain_own, w_keyvalue, ids):
    count = ids.shape[0]
    rows, features = tokens.shape

    def body(ids_ref, t_ref, g_ref, w_ref, o_ref):
        scaled = (t_ref[...].astype(F32) * g_ref[...]).astype(BF16)
        o_ref[...] = jnp.dot(scaled, w_ref[0], preferred_element_type=F32).astype(BF16)

    return pl.pallas_call(
        body,
        out_shape=jax.ShapeDtypeStruct((rows, count * HD), BF16),
        grid_spec=pltpu.PrefetchScalarGridSpec(
            num_scalar_prefetch=1,
            grid=(count,),
            in_specs=[
                pl.BlockSpec((rows, features), lambda n, ids: (0, 0)),
                pl.BlockSpec((1, features), lambda n, ids: (0, 0)),
                pl.BlockSpec(
                    (1, features, HD), lambda n, ids: (lax.rem(ids[n], 2), 0, lax.div(ids[n], 2))
                ),
            ],
            out_specs=pl.BlockSpec((rows, HD), lambda n, ids: (0, n)),
        ),
        compiler_params=params(8),
        name="kv_partial",
    )(ids, tokens, gain_own, w_keyvalue)


def query_part(pieces, arrays, ids, gain, w_query, carry):
    rows, columns = 512, w_query.shape[1]
    count = len(pieces)
    first = carry is None
    n_arrays = len(arrays)

    def body(ids_ref, *refs):
        a_refs = refs[:n_arrays]
        g_ref, w_ref = refs[n_arrays : n_arrays + 2]
        q_ref, s_ref = refs[-2:]
        step = pl.program_id(0)

        @pl.when(step == 0)
        def _():
            if first:
                q_ref[...] = jnp.zeros_like(q_ref)
                s_ref[...] = jnp.zeros_like(s_ref)
            else:
                q_ref[...] = refs[n_arrays + 2][...]
                s_ref[...] = refs[n_arrays + 3][...]

        for number, parts in enumerate(pieces):

            @pl.when(step == number)
            def _(parts=parts):
                for which, start, target, size in parts:
                    values = a_refs[which][start : start + size, :].astype(F32)
                    squares = values * values
                    lanes = squares[:, :HD]
                    for k in range(1, 4):
                        lanes = lanes + squares[:, k * HD : (k + 1) * HD]
                    s_ref[target : target + size, :] += lanes
                    scaled = (values * g_ref[0]).astype(BF16)
                    q_ref[target : target + size, :] += jnp.dot(
                        scaled, w_ref[...], preferred_element_type=F32
                    )

    whole = pl.BlockSpec(memory_space=pltpu.VMEM)
    carried = [] if first else list(carry)
    return pl.pallas_call(
        body,
        out_shape=(
            jax.ShapeDtypeStruct((rows, columns), F32),
            jax.ShapeDtypeStruct((rows, HD), F32),
        ),
        grid_spec=pltpu.PrefetchScalarGridSpec(
            num_scalar_prefetch=1,
            grid=(count,),
            in_specs=[whole] * n_arrays
            + [
                pl.BlockSpec((1, 1, 512), lambda n, ids: (ids[n], 0, 0)),
                pl.BlockSpec((512, columns), lambda n, ids: (ids[n], 0)),
            ]
            + [whole] * len(carried),
            out_specs=[
                pl.BlockSpec((rows, columns), lambda n, ids: (0, 0)),
                pl.BlockSpec((rows, HD), lambda n, ids: (0, 0)),
            ],
        ),
        compiler_params=params(20),
        name="query_part",
    )(ids, *arrays, gain, w_query, *carried)


def attention(query, squares, keyvalue, cosine, sine, pool, parents, lengths):
    rows, columns = query.shape
    branches = rows // PB
    heads = columns // HD
    span = PDEPTH * PB + PB
    features = 8192.0
    scale = 1.0 / math.sqrt(HD)

    def body(par_ref, len_ref, q_ref, s_ref, k_ref, v_ref, c_ref, n_ref, p_ref, o_ref, qb, kb, vb):
        branch = pl.program_id(0)
        meansq = jnp.sum(s_ref[...], axis=1, keepdims=True) * (1.0 / features)
        factor = lax.rsqrt(meansq + 1e-06)
        cos_part = c_ref[...] * factor
        sin_part = n_ref[...] * factor

        def rope(v):
            return (v * cos_part + pltpu.roll(v, HD // 2, 1) * sin_part).astype(BF16)

        for h in range(heads):
            qb[h * PB : (h + 1) * PB, :] = rope(q_ref[:, h * HD : (h + 1) * HD])
        for d in range(PDEPTH):
            block = par_ref[branch, d]
            kb[d * PB : (d + 1) * PB, :] = p_ref[0, block]
            vb[d * PB : (d + 1) * PB, :] = p_ref[1, block]
        kb[PDEPTH * PB :, :] = rope(k_ref[...].astype(F32))
        vb[PDEPTH * PB :, :] = (v_ref[...].astype(F32) * factor).astype(BF16)
        scores = lax.dot_general(
            qb[...], kb[...], (((1,), (1,)), ((), ())), preferred_element_type=F32
        )
        column = lax.broadcasted_iota(jnp.int32, (heads * PB, span), 1)
        within = lax.broadcasted_iota(jnp.int32, (heads * PB, span), 0) % PB
        limit = len_ref[branch] * PB
        seen = (column < limit) | (
            (column >= PDEPTH * PB) & (column - PDEPTH * PB <= within)
        )
        scores = jnp.where(seen, scores * scale, -1e30)
        highest = jnp.max(scores, axis=1, keepdims=True)
        expo = jnp.exp(scores - highest)
        total = jnp.sum(expo, axis=1, keepdims=True)
        probs = (expo / total).astype(BF16)
        mixed = jnp.dot(probs, vb[...], preferred_element_type=F32).astype(BF16)
        for h in range(heads):
            o_ref[:, h * HD : (h + 1) * HD] = mixed[h * PB : (h + 1) * PB]

    def rows_of(width):
        return pl.BlockSpec((PB, width), lambda n, *_: (n, 0))

    return pl.pallas_call(
        body,
        out_shape=jax.ShapeDtypeStruct((rows, columns), BF16),
        grid_spec=pltpu.PrefetchScalarGridSpec(
            num_scalar_prefetch=2,
            grid=(branches,),
            in_specs=[
                rows_of(columns),
                rows_of(HD),
                rows_of(HD),
                rows_of(HD),
                rows_of(HD),
                rows_of(HD),
                pl.BlockSpec(memory_space=pltpu.VMEM),
            ],
            out_specs=rows_of(columns),
            scratch_shapes=[
                pltpu.VMEM((heads * PB, HD), BF16),
                pltpu.VMEM((span, HD), BF16),
                pltpu.VMEM((span, HD), BF16),
            ],
        ),
        compiler_params=params(16),
        name="attention",
    )(parents, lengths, query, squares, *keyvalue, cosine, sine, pool)


def output_part(heads_out, w_output, ids):
    rows, depth = heads_out.shape
    count = ids.shape[0]

    def body(ids_ref, h_ref, w_ref, o_ref):
        o_ref[0] = jnp.dot(h_ref[...], w_ref[...], preferred_element_type=F32).astype(BF16)

    return pl.pallas_call(
        body,
        out_shape=jax.ShapeDtypeStruct((count, rows, 512), BF16),
        grid_spec=pltpu.PrefetchScalarGridSpec(
            num_scalar_prefetch=1,
            grid=(count,),
            in_specs=[
                pl.BlockSpec((rows, depth), lambda n, ids: (0, 0)),
                pl.BlockSpec((depth, 512), lambda n, ids: (0, ids[n])),
            ],
            out_specs=pl.BlockSpec((1, rows, 512), lambda n, ids: (n, 0, 0)),
        ),
        compiler_params=params(12),
        name="output_part",
    )(ids, heads_out, w_output)


def local(tokens, gain, w_query, w_keyvalue, w_output, cache, parents, lengths):
    bar = lax.optimization_barrier
    group = lax.axis_index("branch")
    place = lax.axis_index("tensor")
    x, y = place // 4, place % 4
    core = group % 2
    row_count = tokens.shape[0]
    branch_count = row_count // PB

    ahead = jnp.arange(4, dtype=jnp.int32)
    i_step, j_step = ahead[:, None], ahead[None, :]
    dx = jnp.where(core == 0, j_step, i_step)
    dy = jnp.where(core == 0, i_step, j_step)
    order = ((x + dx) % 4) * 4 + (y + dy) % 4

    my_lengths = lax.dynamic_slice_in_dim(lengths, group * branch_count, branch_count, 0)
    my_parents = lax.dynamic_slice_in_dim(parents, group * branch_count, branch_count, 0)
    local_heads = w_query.shape[1] // HD
    kv_head = place * local_heads // (HEADS // KVH)
    cache_head = lax.dynamic_slice_in_dim(cache, kv_head * HD, HD, 3)
    pool = lax.all_gather(cache_head, "branch", axis=1, tiled=True)

    positions = jnp.repeat(my_lengths, PB) * PB + jnp.tile(
        jnp.arange(PB, dtype=jnp.int32), branch_count
    )
    halfway = HD // 2
    frequency = jnp.exp(jnp.arange(halfway, dtype=F32) * (-2.0 * math.log(1000000.0) / HD))
    angles = positions.astype(F32)[:, None] * frequency[None, :]
    cosine, sine = jnp.cos(angles), jnp.sin(angles)
    cosine = jnp.concatenate([cosine, cosine], axis=1)
    sine = jnp.concatenate([-sine, sine], axis=1)

    gain_all = gain.astype(F32).reshape(16, 1, 512)
    gain_own = lax.dynamic_slice_in_dim(gain, place * 512, 512, 0).astype(F32)[None, :]

    kv_far = kv_partial(tokens, gain_own, w_keyvalue, order[2])
    s1 = both(stack_rows(tokens, kv_far[:HALF]), stack_rows(tokens, kv_far[HALF:]), "first")
    s2 = both(tokens, tokens, "second")
    kv_near = kv_partial(
        tokens, gain_own, w_keyvalue, jnp.concatenate([order[0], order[1], order[3]])
    )
    (b1m, b1p) = bar(s1)
    k1 = kv_near[:, 512:1024]
    k3 = kv_near[:, 1024:]
    k1 = stack_rows(plus(k1[:HALF], b1m[512:]), k1[HALF:])
    k3 = stack_rows(k3[:HALF], plus(k3[HALF:], b1p[512:]))
    s3 = both(stack_rows(b1m[:HALF], k1), stack_rows(b1p[HALF:512], k3), "first")
    near = stack_rows(b1p[:512], b1m[:512])
    s4 = both(near, near, "second")
    b2m, b2p, b3m, b3p = bar((*s2, *s3))
    part = query_part(
        [[(0, 0, 0, 512)], [(1, 0, 0, 512)], [(2, 0, 0, 512)], [(3, 0, 0, 512)], [(4, 0, 0, 512)]],
        [tokens, b1p, b1m, b2p, b2m],
        jnp.stack([order[0, 0], order[1, 0], order[3, 0], order[0, 1], order[0, 3]]),
        gain_all,
        w_query,
        None,
    )
    ksum = plus(kv_near[:, :512], b3m[HALF:], b3p[HALF:])
    kfar = ksum[:, 2 * HD : 3 * HD]
    opposite = stack_rows(b3m[:HALF], b3p[:HALF])
    s5 = both(
        stack_rows(opposite, b2m[:HALF], pack(kfar[:HALF])),
        stack_rows(opposite, b2p[HALF:], pack(kfar[HALF:])),
        "second",
    )
    b4m, b4p = bar(s4)
    part = query_part(
        [
            [(0, 0, 0, HALF), (1, 0, HALF, HALF)],
            [(2, 0, 0, 512)],
            [(2, 512, 0, 512)],
            [(3, 0, 0, 512)],
            [(3, 512, 0, 512)],
        ],
        [b3m, b3p, b4p, b4m],
        jnp.stack([order[2, 0], order[1, 1], order[3, 1], order[1, 3], order[3, 3]]),
        gain_all,
        w_query,
        part,
    )
    s6 = both(
        stack_rows(b4m[:HALF], b4m[512 : 512 + HALF]),
        stack_rows(b4p[HALF:512], b4p[512 + HALF :]),
        "second",
    )
    b5m, b5p = bar(s5)
    k1 = ksum[:, HD : 2 * HD]
    k3 = ksum[:, 3 * HD :]
    k1 = stack_rows(plus(k1[:HALF], unpack(b5m[768:])), k1[HALF:])
    k3 = stack_rows(k3[:HALF], plus(k3[HALF:], unpack(b5p[768:])))
    s7 = both(
        stack_rows(b5m[:HALF], pack(k1)), stack_rows(b5p[HALF:512], pack(k3)), "second"
    )
    part = query_part(
        [[(0, 0, 0, 512)], [(1, 0, 0, 512)], [(1, 512, 0, HALF), (0, 512, HALF, HALF)]],
        [b5p, b5m],
        jnp.stack([order[2, 1], order[2, 3], order[0, 2]]),
        gain_all,
        w_query,
        part,
    )
    b6m, b6p, b7m, b7p = bar((*s6, *s7))
    mine = plus(ksum[:, :HD], unpack(b7m[HALF:]), unpack(b7p[HALF:]))
    other = hop(mine, "twin", 1)
    even = place % 2 == 0
    new_key = jnp.where(even, mine, other)
    new_value = jnp.where(even, other, mine)
    query, squares = query_part(
        [
            [(0, 0, 0, HALF), (1, 0, HALF, HALF)],
            [(0, HALF, 0, HALF), (1, HALF, HALF, HALF)],
            [(2, 0, 0, HALF), (3, 0, HALF, HALF)],
        ],
        [b6m, b6p, b7m, b7p],
        jnp.stack([order[1, 2], order[3, 2], order[2, 2]]),
        gain_all,
        w_query,
        part,
    )
    heads_out = attention(
        query, squares, (new_key, new_value), cosine, sine, pool, my_parents, my_lengths
    )

    far = output_part(
        heads_out, w_output, jnp.stack([order[2, 2], order[1, 2], order[3, 2], order[0, 2]])
    )
    r1 = both(far[0, :HALF], far[0, HALF:], "second")
    r2 = both(
        stack_rows(far[1, :HALF], far[2, :HALF]),
        stack_rows(far[1, HALF:], far[2, HALF:]),
        "second",
    )
    rest = output_part(
        heads_out,
        w_output,
        jnp.concatenate(
            [
                jnp.stack([order[2, 1], order[2, 3], order[1, 1], order[3, 1], order[1, 3]]),
                jnp.stack([order[3, 3], order[2, 0], order[0, 1], order[0, 3], order[1, 0]]),
                jnp.stack([order[3, 0], order[0, 0]]),
            ]
        ),
    )
    q21, q23, q11, q31, q13, q33, q20, q01, q03, q10, q30, q00 = [rest[n] for n in range(12)]
    r1m, r1p = bar(r1)
    r3 = both(
        stack_rows(plus(q21[:HALF], r1m), q21[HALF:], far[3, :HALF]),
        stack_rows(q23[:HALF], plus(q23[HALF:], r1p), far[3, HALF:]),
        "second",
    )
    r2m, r2p = bar(r2)
    r4 = both(
        stack_rows(plus(q11[:HALF], r2m[:HALF]), q11[HALF:], plus(q31[:HALF], r2m[HALF:]), q31[HALF:]),
        stack_rows(q13[:HALF], plus(q13[HALF:], r2p[:HALF]), q33[:HALF], plus(q33[HALF:], r2p[HALF:])),
        "second",
    )
    r3m, r3p = bar(r3)
    sum2 = plus(q20, r3m[:512], r3p[:512])
    r5 = both(sum2[:HALF], sum2[HALF:], "first")
    r6 = both(
        stack_rows(plus(q01[:HALF], r3m[512:]), q01[HALF:]),
        stack_rows(q03[:HALF], plus(q03[HALF:], r3p[512:])),
        "second",
    )
    r4m, r4p, r5m, r5p = bar((*r4, *r5))
    sum1 = stack_rows(
        plus(q10[:HALF], r4m[:HALF], r4p[:HALF], r5m), plus(q10[HALF:], r4m[HALF:512], r4p[HALF:512])
    )
    sum3 = stack_rows(
        plus(q30[:HALF], r4m[512 : 512 + HALF], r4p[512 : 512 + HALF]),
        plus(q30[HALF:], r4m[512 + HALF :], r4p[512 + HALF :], r5p),
    )
    r7 = both(sum1, sum3, "first")
    return plus(q00, *r6, *r7)


def solution(mesh):
    return jax.shard_map(
        local,
        mesh=mesh,
        in_specs=(
            P("branch", "tensor"),
            P(),
            P(None, "tensor"),
            P(None, "tensor", None),
            P("tensor", None),
            P(None, "branch", None, None),
            P(),
            P(),
        ),
        out_specs=P("branch", "tensor"),
        check_vma=False,
    )
```

```python
import math

import jax
import jax.numpy as jnp
from jax import lax
from jax.experimental import pallas as pl
from jax.experimental.pallas import tpu as pltpu
from jax.sharding import PartitionSpec as P

HEADS = 64
KVH = 8
HD = 128
PB = 64
PDEPTH = 4
HALF = 256
AXES = ("branch", "tensor")
F32 = jnp.float32
BF16 = jnp.bfloat16
MIB = 1024 * 1024


def pairs(move):
    table = []
    for z in range(4):
        for c in range(2):
            for x in range(4):
                for y in range(4):
                    z2, c2, x2, y2 = move(z, c, x, y)
                    target = ((z2 % 4) * 2 + c2 % 2) * 16 + (x2 % 4) * 4 + y2 % 4
                    table.append(((z * 2 + c) * 16 + x * 4 + y, target))
    return table


HOPS = {}
for step in (1, -1):
    HOPS["first", step] = pairs(
        lambda z, c, x, y, s=step: (z, c, x, y + s) if c == 0 else (z, c, x + s, y)
    )
    HOPS["second", step] = pairs(
        lambda z, c, x, y, s=step: (z, c, x + s, y) if c == 0 else (z, c, x, y + s)
    )
HOPS["twin", 1] = pairs(lambda z, c, x, y: (z, c, x, y ^ 1))
HOPS["z_one", 1] = pairs(lambda z, c, x, y: (z ^ 1 if c == 0 else 3 - z, c, x, y))
HOPS["z_two", 1] = pairs(lambda z, c, x, y: (3 - z if c == 0 else z ^ 1, c, x, y))
HOPS["core", 1] = pairs(lambda z, c, x, y: (z, c + 1, x, y))


def hop(value, axis, step):
    return lax.ppermute(value, AXES, HOPS[axis, step])


def both(forward, backward, axis):
    return hop(forward, axis, 1), hop(backward, axis, -1)


def stack_rows(*parts):
    return jnp.concatenate(parts, axis=0)


def plus(base, *terms):
    total = base.astype(F32)
    for term in terms:
        total = total + term.astype(F32)
    return total.astype(BF16)


def pack(block):
    quarter = block.shape[0] // 4
    return jnp.concatenate([block[k * quarter : (k + 1) * quarter] for k in range(4)], axis=1)


def unpack(block):
    return jnp.concatenate([block[:, k * HD : (k + 1) * HD] for k in range(4)], axis=0)


def params(mebibytes):
    return pltpu.CompilerParams(vmem_limit_bytes=mebibytes * MIB)


def estimate(flops, moved):
    return pl.CostEstimate(flops=flops, bytes_accessed=moved, transcendentals=0)


VMEM = pl.BlockSpec(memory_space=pltpu.VMEM)
SMEM = pl.BlockSpec(memory_space=pltpu.SMEM)
FIXED = pl.BlockSpec(memory_space=pltpu.HBM)
ANYWHERE = pl.BlockSpec(memory_space=pl.ANY)
GROUP = 2
CHUNK = 64
WIDE = 512


def in_vmem(arrays):
    return [pltpu.with_memory_space_constraint(a, pltpu.VMEM) for a in arrays]


def place_of(order_ref, i, j):
    return order_ref[i * 4 + j]


def assemble(arrays, outputs):
    n_arrays = len(arrays)

    def body(*refs):
        for o_ref, (_, pieces) in zip(refs[n_arrays:], outputs, strict=True):
            for row, column, rows, columns, terms in pieces:
                parts = [refs[a][r : r + rows, c : c + columns] for a, r, c in terms]
                if len(parts) > 1:
                    total = parts[0].astype(F32)
                    for part in parts[1:]:
                        total = total + part.astype(F32)
                    parts = [total.astype(BF16)]
                o_ref[row : row + rows, column : column + columns] = parts[0]

    return pl.pallas_call(
        body,
        out_shape=[pltpu.VMEM(shape, BF16) for shape, _ in outputs],
        in_specs=[VMEM] * n_arrays,
        out_specs=[VMEM] * len(outputs),
        compiler_params=params(8),
        cost_estimate=estimate(0, 0),
        name="assemble",
    )(*in_vmem(arrays))


def rows_piece(row, rows, *terms):
    return (row, 0, rows, WIDE, [(a, r, 0) for a, r in terms])


def packed(row, rows, *terms):
    quarter = rows // 4
    pieces = []
    for k in range(4):
        places = [(a, start + k * quarter, column) for a, start, column in terms]
        pieces.append((row, k * HD, quarter, HD, places))
    return pieces


def kv_partial(tokens, gain, w_keyvalue, order, steps):
    spots = [(i, j) for i in steps for j in range(4)]
    count = len(spots)

    def body(order_ref, t_ref, g_ref, w_ref, o_ref, weights, sems):
        copies = []
        for n, (i, j) in enumerate(spots):
            target = place_of(order_ref, i, j)
            column = pl.multiple_of(lax.div(target, 2) * HD, HD)
            copies.append(
                pltpu.make_async_copy(
                    w_ref.at[lax.rem(target, 2), :, pl.ds(column, HD)],
                    weights.at[:, pl.ds(n * HD, HD)],
                    sems.at[n],
                )
            )
        for copy in copies:
            copy.start()
        own = g_ref[pl.ds(place_of(order_ref, 0, 0), 1), :]
        scaled = (t_ref[...].astype(F32) * own).astype(BF16)
        for copy in copies:
            copy.wait()
        for n in range(0, count * HD, WIDE):
            o_ref[:, n : n + WIDE] = jnp.dot(
                scaled, weights[:, n : n + WIDE], preferred_element_type=F32
            ).astype(BF16)

    return pl.pallas_call(
        body,
        out_shape=jax.ShapeDtypeStruct((WIDE, count * HD), BF16),
        in_specs=[SMEM, VMEM, VMEM, FIXED],
        out_specs=VMEM,
        scratch_shapes=[
            pltpu.VMEM((WIDE, count * HD), BF16),
            pltpu.SemaphoreType.DMA((count,)),
        ],
        compiler_params=params(7),
        cost_estimate=estimate(0, 0),
        name="kv_partial",
    )(order, tokens, gain, w_keyvalue)


def query_part(blocks, arrays, order, gain, w_query, carry):
    count = len(blocks)
    n_arrays = len(arrays)
    first = carry is None

    def body(order_ref, *refs):
        a_refs = refs[:n_arrays]
        g_ref, w_ref = refs[n_arrays : n_arrays + 2]
        q_ref, s_ref, scaled, weights, sems = refs[-5:]
        places = [place_of(order_ref, *spot) for spot, _ in blocks]

        def fetch(n):
            return pltpu.make_async_copy(
                w_ref.at[pl.ds(pl.multiple_of(places[n] * WIDE, WIDE), WIDE), :],
                weights.at[n // GROUP % 2, pl.ds(n % GROUP * WIDE, WIDE), :],
                sems.at[n],
            )

        for n in range(min(count, 2 * GROUP)):
            fetch(n).start()
        s_ref[...] = jnp.zeros_like(s_ref) if first else refs[n_arrays + 3][...]
        for low in range(0, count, GROUP):
            members = range(low, min(low + GROUP, count))
            for n in members:
                own = g_ref[pl.ds(places[n], 1), :]
                lanes_at = pl.ds((n - low) * WIDE, WIDE)
                for which, start, target, size in blocks[n][1]:

                    @pl.loop(0, size // CHUNK)
                    def _(step, which=which, start=start, target=target, own=own, lanes_at=lanes_at):
                        row = pl.multiple_of(step * CHUNK, CHUNK)
                        values = a_refs[which][pl.ds(start + row, CHUNK), :].astype(F32)
                        squares = values * values
                        lanes = squares[:, :HD]
                        for k in range(1, WIDE // HD):
                            lanes = lanes + squares[:, k * HD : (k + 1) * HD]
                        s_ref[pl.ds(target + row, CHUNK), :] += lanes
                        scaled[pl.ds(target + row, CHUNK), lanes_at] = (values * own).astype(BF16)

            for n in members:
                fetch(n).wait()
            depth = len(members) * WIDE
            for half in range(2):
                rows = slice(half * HALF, (half + 1) * HALF)
                product = jnp.dot(
                    scaled[rows, :depth], weights[low // GROUP % 2, :depth, :], preferred_element_type=F32
                )
                if low:
                    q_ref[rows, :] += product
                else:
                    q_ref[rows, :] = product if first else refs[n_arrays + 2][rows, :] + product
            for n in range(low + 2 * GROUP, min(low + 3 * GROUP, count)):
                fetch(n).start()

    carried = [] if first else list(carry)
    return pl.pallas_call(
        body,
        out_shape=(
            jax.ShapeDtypeStruct((WIDE, WIDE), F32),
            jax.ShapeDtypeStruct((WIDE, HD), F32),
        ),
        in_specs=[SMEM] + [VMEM] * n_arrays + [VMEM, FIXED] + [VMEM] * len(carried),
        out_specs=(VMEM, VMEM),
        scratch_shapes=[
            pltpu.VMEM((WIDE, GROUP * WIDE), BF16),
            pltpu.VMEM((2, GROUP * WIDE, WIDE), BF16),
            pltpu.SemaphoreType.DMA((count,)),
        ],
        input_output_aliases={} if first else {n_arrays + 3: 0, n_arrays + 4: 1},
        compiler_params=params(14),
        cost_estimate=estimate(0, 0),
        name="query_part",
    )(order, *in_vmem(arrays), gain, w_query, *in_vmem(carried))


def gather_blocks(pools, codes):
    branches = codes.shape[0]
    span = PDEPTH * PB + PB

    def body(code_ref, *refs):
        pool_refs, (o_ref, sems) = refs[:4], refs[4:]
        for b in range(branches):
            for d in range(PDEPTH):
                code = code_ref[b, d]
                slot, block = lax.rem(lax.div(code, 16), 2), lax.rem(code, 16)
                for which, source in enumerate(pool_refs):

                    @pl.when(lax.div(code, 32) == which)
                    def _(source=source):
                        pltpu.make_async_copy(
                            source.at[slot, :, block], o_ref.at[b, :, pl.ds(d * PB, PB), :], sems.at[b, d]
                        ).start()

        for b in range(branches):
            for d in range(PDEPTH):
                pltpu.make_async_copy(
                    pool_refs[0].at[0, :, 0], o_ref.at[b, :, pl.ds(d * PB, PB), :], sems.at[b, d]
                ).wait()

    return pl.pallas_call(
        body,
        out_shape=jax.ShapeDtypeStruct((branches, 2, span, HD), BF16),
        in_specs=[SMEM] + [ANYWHERE] * 4,
        out_specs=VMEM,
        scratch_shapes=[pltpu.SemaphoreType.DMA((branches, PDEPTH))],
        compiler_params=params(8),
        cost_estimate=estimate(0, 0),
        name="gather_blocks",
    )(codes, *pools)


def middle(query, squares, order, keyvalue, tables, prefix, lengths, w_output):
    branches = WIDE // PB
    heads = WIDE // HD
    span = PDEPTH * PB + PB
    scale = 1.0 / math.sqrt(HD)
    spots = [(2, 2), (1, 2), (3, 2), (0, 2)]

    def body(
        order_ref, len_ref, q_ref, s_ref, mine_ref, other_ref, cos_ref, sin_ref, prefix_ref, wo_ref,
        heads_ref, far_ref, kv_ref,
        wo, qb, wsems,
    ):
        copies = []
        for n, (i, j) in enumerate(spots):
            column = pl.multiple_of(place_of(order_ref, i, j) * WIDE, WIDE)
            copies.append(
                pltpu.make_async_copy(wo_ref.at[:, pl.ds(column, WIDE)], wo.at[n], wsems.at[n])
            )
        for copy in copies:
            copy.start()
        total = jnp.sum(s_ref[...], axis=1, keepdims=True)
        factor = lax.rsqrt(total * (1.0 / 8192.0) + 1e-06)
        cos_part = cos_ref[...] * factor
        sin_part = sin_ref[...] * factor

        def rope(v, cos_part, sin_part):
            return (v * cos_part + pltpu.roll(v, HD // 2, 1) * sin_part).astype(BF16)

        even = lax.rem(place_of(order_ref, 0, 0), 2) == 0
        mine, other = mine_ref[...].astype(F32), other_ref[...].astype(F32)
        new_keys = rope(jnp.where(even, mine, other), cos_part, sin_part)
        new_values = (jnp.where(even, other, mine) * factor).astype(BF16)
        for b in range(branches):
            kv_ref[b, 0, PDEPTH * PB :, :] = new_keys[b * PB : (b + 1) * PB]
            kv_ref[b, 1, PDEPTH * PB :, :] = new_values[b * PB : (b + 1) * PB]
        cos_part, sin_part = cos_part * scale, sin_part * scale
        for h in range(heads):
            qb[h] = rope(q_ref[:, h * HD : (h + 1) * HD], cos_part, sin_part)
        column = lax.broadcasted_iota(jnp.int32, (heads * PB, span), 1)
        within = lax.rem(lax.broadcasted_iota(jnp.int32, (heads * PB, span), 0), PB)
        own_seen = (column >= PDEPTH * PB) & (column - PDEPTH * PB <= within)
        for b in range(branches):
            queries = qb[:, b * PB : (b + 1) * PB, :].reshape(heads * PB, HD)
            scores = lax.dot_general(
                queries, kv_ref[b, 0], (((1,), (1,)), ((), ())), preferred_element_type=F32
            )
            seen = (column < len_ref[b] * PB) | own_seen
            scores = jnp.where(seen, scores, -1e30)
            highest = jnp.max(scores, axis=1, keepdims=True)
            expo = jnp.exp(scores - highest)
            inverse = 1.0 / jnp.sum(expo, axis=1, keepdims=True)
            mixed = jnp.dot(expo.astype(BF16), kv_ref[b, 1], preferred_element_type=F32)
            mixed = (mixed * inverse).astype(BF16)
            for h in range(heads):
                heads_ref[b * PB : (b + 1) * PB, h * HD : (h + 1) * HD] = mixed[
                    h * PB : (h + 1) * PB
                ]
        for n, copy in enumerate(copies):
            copy.wait()
            far_ref[n] = jnp.dot(heads_ref[...], wo[n], preferred_element_type=F32).astype(BF16)

    return pl.pallas_call(
        body,
        out_shape=(
            jax.ShapeDtypeStruct((WIDE, WIDE), BF16),
            jax.ShapeDtypeStruct((len(spots), WIDE, WIDE), BF16),
            jax.ShapeDtypeStruct(prefix.shape, BF16),
        ),
        in_specs=[SMEM] * 2 + [VMEM] * 7 + [FIXED],
        out_specs=(VMEM, VMEM, VMEM),
        scratch_shapes=[
            pltpu.VMEM((len(spots), WIDE, WIDE), BF16),
            pltpu.VMEM((heads, WIDE, HD), BF16),
            pltpu.SemaphoreType.DMA((len(spots),)),
        ],
        input_output_aliases={8: 2},
        compiler_params=params(9),
        cost_estimate=estimate(0, 0),
        name="middle",
    )(
        order, lengths, *in_vmem([query, squares, *keyvalue, *tables, prefix]), w_output
    )[:2]


def output_part(heads_out, w_output, order, spots):
    count = len(spots)

    def body(order_ref, h_ref, w_ref, o_ref, weights, sems):
        copies = []
        for n, (i, j) in enumerate(spots):
            column = pl.multiple_of(place_of(order_ref, i, j) * WIDE, WIDE)
            copies.append(
                pltpu.make_async_copy(w_ref.at[:, pl.ds(column, WIDE)], weights.at[n], sems.at[n])
            )
        for copy in copies:
            copy.start()
        for n, copy in enumerate(copies):
            copy.wait()
            o_ref[n] = jnp.dot(h_ref[...], weights[n], preferred_element_type=F32).astype(BF16)

    return pl.pallas_call(
        body,
        out_shape=jax.ShapeDtypeStruct((count, WIDE, WIDE), BF16),
        in_specs=[SMEM, VMEM, FIXED],
        out_specs=VMEM,
        scratch_shapes=[
            pltpu.VMEM((count, WIDE, WIDE), BF16),
            pltpu.SemaphoreType.DMA((count,)),
        ],
        compiler_params=params(7),
        cost_estimate=estimate(0, 0),
        name="output_part",
    )(order, heads_out, w_output)


def local(tokens, gain, w_query, w_keyvalue, w_output, cache, parents, lengths):
    bar = lax.optimization_barrier
    group = lax.axis_index("branch")
    place = lax.axis_index("tensor")
    x, y = place // 4, place % 4
    z, core = group // 2, group % 2
    row_count = tokens.shape[0]
    branch_count = row_count // PB

    count = jnp.arange(16, dtype=jnp.int32)
    i_step, j_step = count // 4, count % 4
    dx = jnp.where(core == 0, j_step, i_step)
    dy = jnp.where(core == 0, i_step, j_step)
    order = ((x + dx) % 4) * 4 + (y + dy) % 4
    gains = gain.astype(F32).reshape(16, WIDE)
    w_query, w_keyvalue, w_output = [
        pltpu.with_memory_space_constraint(w, pltpu.HBM) for w in (w_query, w_keyvalue, w_output)
    ]

    s1 = both(tokens, tokens, "first")
    kv = kv_partial(tokens, gains, w_keyvalue, order, (0, 1, 3, 2))
    k_far = both(kv[:HALF, 3 * WIDE :], kv[HALF:, 3 * WIDE :], "first")
    b1m, b1p, k_m, k_p, kv_near, cache = bar((*s1, *k_far, kv, cache))
    (near,) = assemble(
        [tokens, b1p, b1m],
        [((3 * WIDE, WIDE), [rows_piece(n * WIDE, WIDE, (n, 0)) for n in range(3)])],
    )
    s2 = both(near, near, "second")
    s3 = both(
        *assemble(
            [b1m, b1p, kv_near, k_m, k_p],
            [
                (
                    (3 * HALF, WIDE),
                    [
                        rows_piece(0, HALF, (0, 0)),
                        (HALF, 0, HALF, WIDE, [(2, 0, WIDE), (3, 0, 0)]),
                        (2 * HALF, 0, HALF, WIDE, [(2, HALF, WIDE)]),
                    ],
                ),
                (
                    (3 * HALF, WIDE),
                    [
                        rows_piece(0, HALF, (1, HALF)),
                        (HALF, 0, HALF, WIDE, [(2, 0, 2 * WIDE)]),
                        (2 * HALF, 0, HALF, WIDE, [(2, HALF, 2 * WIDE), (4, 0, 0)]),
                    ],
                ),
            ],
        ),
        "first",
    )
    kv_head = place * (w_query.shape[1] // HD) // (HEADS // KVH)
    cache_head = lax.dynamic_slice_in_dim(cache, kv_head * HD, HD, 3)
    z_one = hop(cache_head, "z_one", 1)
    part = query_part(
        [((0, 0), [(0, 0, 0, WIDE)]), ((1, 0), [(1, 0, 0, WIDE)]), ((3, 0), [(2, 0, 0, WIDE)])],
        [tokens, b1p, b1m],
        order,
        gains,
        w_query,
        None,
    )
    b3m, b3p, b2m, b2p, z_one, *part = bar((*s3, *s2, z_one, *part))
    ksum, to_next, to_last = assemble(
        [b3m, b3p, kv_near, b2m, b2p],
        [
            ((WIDE, WIDE), [(0, 0, WIDE, WIDE, [(2, 0, 0), (0, HALF, 0), (1, HALF, 0)])]),
            (
                (5 * HALF + HALF // 4, WIDE),
                [rows_piece(0, HALF, (0, 0)), rows_piece(HALF, HALF, (1, 0))]
                + [rows_piece(WIDE + n * HALF, HALF, (3, n * WIDE)) for n in range(3)]
                + packed(5 * HALF, HALF, (2, 0, 2 * HD), (0, HALF, 2 * HD), (1, HALF, 2 * HD)),
            ),
            (
                (5 * HALF + HALF // 4, WIDE),
                [rows_piece(0, HALF, (0, 0)), rows_piece(HALF, HALF, (1, 0))]
                + [rows_piece(WIDE + n * HALF, HALF, (4, n * WIDE + HALF)) for n in range(3)]
                + packed(5 * HALF, HALF, (2, HALF, 2 * HD), (0, WIDE, 2 * HD), (1, WIDE, 2 * HD)),
            ),
        ],
    )
    s5 = both(to_next, to_last, "second")
    pool = jnp.stack([cache_head, z_one])
    z_two = hop(pool, "z_two", 1)
    near_twin = hop(pool, "core", 1)
    my_lengths = lax.dynamic_slice_in_dim(lengths, group * branch_count, branch_count, 0)
    my_parents = lax.dynamic_slice_in_dim(parents, group * branch_count, branch_count, 0)
    owner = my_parents // 16
    owner_z, owner_core = owner // 2, owner % 2
    across = z + 1 - 2 * (z % 2)
    partner = jnp.where(owner_core == 0, across, 3 - z)
    slot = jnp.where(
        owner_z == z, 0, jnp.where(owner_z == partner, 1, jnp.where(owner_z == (z + 2) % 4, 3, 2))
    )
    codes = jnp.where(owner_core == core, 0, 64) + slot * 16 + my_parents % 16

    positions = jnp.repeat(my_lengths, PB) * PB + jnp.tile(
        jnp.arange(PB, dtype=jnp.int32), branch_count
    )
    halfway = HD // 2
    frequency = jnp.exp(jnp.arange(halfway, dtype=F32) * (-2.0 * math.log(1000000.0) / HD))
    angles = positions.astype(F32)[:, None] * frequency[None, :]
    cosine, sine = jnp.cos(angles), jnp.sin(angles)
    cosine = jnp.concatenate([cosine, cosine], axis=1)
    sine = jnp.concatenate([-sine, sine], axis=1)

    part = query_part(
        [
            ((2, 0), [(0, 0, 0, HALF), (1, 0, HALF, HALF)]),
            ((0, 1), [(2, 0, 0, WIDE)]),
            ((1, 1), [(2, WIDE, 0, WIDE)]),
            ((3, 1), [(2, 2 * WIDE, 0, WIDE)]),
            ((0, 3), [(3, 0, 0, WIDE)]),
            ((1, 3), [(3, WIDE, 0, WIDE)]),
            ((3, 3), [(3, 2 * WIDE, 0, WIDE)]),
        ],
        [b3m, b3p, b2p, b2m],
        order,
        gains,
        w_query,
        part,
    )
    b5m, b5p, z_two, near_twin, cosine, sine, codes, *part = bar(
        (*s5, z_two, near_twin, cosine, sine, codes, *part)
    )
    quarter = HALF // 4
    s7 = both(
        *assemble(
            [b5m, b5p, ksum],
            [
                (
                    (HALF + WIDE // 4, WIDE),
                    [rows_piece(0, HALF, (0, 0))]
                    + [
                        piece
                        for k in range(4)
                        for piece in [
                            (
                                HALF,
                                k * HD,
                                2 * quarter,
                                HD,
                                [(2, k * 2 * quarter, HD)],
                            )
                        ]
                        if k >= 2
                    ]
                    + [
                        (
                            HALF + t * quarter,
                            k * HD,
                            quarter,
                            HD,
                            [(2, (2 * k + t) * quarter, HD), (0, 5 * HALF, (2 * k + t) * HD)],
                        )
                        for k in range(2)
                        for t in range(2)
                    ],
                ),
                (
                    (HALF + WIDE // 4, WIDE),
                    [rows_piece(0, HALF, (1, HALF))]
                    + [
                        (HALF, k * HD, 2 * quarter, HD, [(2, k * 2 * quarter, 3 * HD)])
                        for k in range(2)
                    ]
                    + [
                        (
                            HALF + t * quarter,
                            k * HD,
                            quarter,
                            HD,
                            [(2, (2 * k + t) * quarter, 3 * HD), (1, 5 * HALF, (2 * k + t - 4) * HD)],
                        )
                        for k in range(2, 4)
                        for t in range(2)
                    ],
                ),
            ],
        ),
        "second",
    )
    far_twin = hop(z_two, "core", 1)
    pools = [
        pltpu.with_memory_space_constraint(a, pltpu.HBM) for a in (pool, z_two, near_twin, far_twin)
    ]
    prefix = gather_blocks(pools, codes)
    part = query_part(
        [
            ((2, 1), [(0, 0, 0, WIDE)]),
            ((2, 3), [(1, 0, 0, WIDE)]),
            ((0, 2), [(1, WIDE, 0, HALF), (0, WIDE, HALF, HALF)]),
            ((1, 2), [(1, WIDE + HALF, 0, HALF), (0, WIDE + HALF, HALF, HALF)]),
            ((3, 2), [(1, 2 * WIDE, 0, HALF), (0, 2 * WIDE, HALF, HALF)]),
        ],
        [b5p, b5m],
        order,
        gains,
        w_query,
        part,
    )
    b7m, b7p, prefix, *part = bar((*s7, prefix, *part))
    (mine,) = assemble(
        [ksum, b7m, b7p],
        [
            (
                (WIDE, HD),
                [
                    (k * 128, 0, 128, HD, [(0, k * 128, 0), (1, HALF, k * HD), (2, HALF, k * HD)])
                    for k in range(4)
                ],
            )
        ],
    )
    other = hop(mine, "twin", 1)
    part = query_part(
        [
            ((2, 2), [(0, 0, 0, HALF), (1, 0, HALF, HALF)]),
        ],
        [b7m, b7p],
        order,
        gains,
        w_query,
        part,
    )
    heads_out, far = middle(
        *part, order, (mine, other), (cosine, sine), prefix, my_lengths, w_output
    )

    ra = both(far[0, :HALF], far[0, HALF:], "second")
    rb = both(
        stack_rows(far[1, :HALF], far[2, :HALF], far[3, :HALF]),
        stack_rows(far[1, HALF:], far[2, HALF:], far[3, HALF:]),
        "second",
    )
    spots = [(2, 1), (2, 3), (1, 1), (3, 1), (1, 3), (3, 3)]
    rest = output_part(heads_out, w_output, order, spots)
    ra_m, ra_p, rest = bar((*ra, rest))
    q21, q23, q11, q31, q13, q33 = [rest[n] for n in range(6)]
    rc = both(
        stack_rows(plus(q21[:HALF], ra_m), q21[HALF:]),
        stack_rows(q23[:HALF], plus(q23[HALF:], ra_p)),
        "second",
    )
    rb_m, rb_p = bar(rb)
    rd = both(
        stack_rows(
            plus(q11[:HALF], rb_m[:HALF]), q11[HALF:], plus(q31[:HALF], rb_m[HALF:WIDE]), q31[HALF:]
        ),
        stack_rows(
            q13[:HALF], plus(q13[HALF:], rb_p[:HALF]), q33[:HALF], plus(q33[HALF:], rb_p[HALF:WIDE])
        ),
        "second",
    )
    spots = [(2, 0), (0, 1), (0, 3), (1, 0), (3, 0), (0, 0)]
    heads_late, rb_m = bar((heads_out, rb_m))
    rest = output_part(heads_late, w_output, order, spots)
    rc_m, rc_p, rest = bar((*rc, rest))
    q20, q01, q03, q10, q30, q00 = [rest[n] for n in range(6)]
    sum2 = plus(q20, rc_m, rc_p)
    re = both(sum2[:HALF], sum2[HALF:], "first")
    rf = both(
        stack_rows(plus(q01[:HALF], rb_m[WIDE:]), q01[HALF:]),
        stack_rows(q03[:HALF], plus(q03[HALF:], rb_p[WIDE:])),
        "second",
    )
    rd_m, rd_p, re_m, re_p = bar((*rd, *re))
    sum1 = stack_rows(
        plus(q10[:HALF], rd_m[:HALF], rd_p[:HALF], re_m), plus(q10[HALF:], rd_m[HALF:WIDE], rd_p[HALF:WIDE])
    )
    sum3 = stack_rows(
        plus(q30[:HALF], rd_m[WIDE : WIDE + HALF], rd_p[WIDE : WIDE + HALF]),
        plus(q30[HALF:], rd_m[WIDE + HALF :], rd_p[WIDE + HALF :], re_p),
    )
    rg = both(sum1, sum3, "first")
    return plus(q00, *rf, *rg)


def solution(mesh):
    return jax.shard_map(
        local,
        mesh=mesh,
        in_specs=(
            P("branch", "tensor"),
            P(),
            P(None, "tensor"),
            P(None, "tensor", None),
            P("tensor", None),
            P(None, "branch", None, None),
            P(),
            P(),
        ),
        out_specs=P("branch", "tensor"),
        check_vma=False,
    )
```

```python
import math

import jax
import jax.numpy as jnp
from jax import lax
from jax.experimental import pallas as pl
from jax.experimental.pallas import tpu as pltpu
from jax.sharding import PartitionSpec as P

HEADS = 64
KVH = 8
HD = 128
PB = 64
PDEPTH = 4
HALF = 256
AXES = ("branch", "tensor")
F32 = jnp.float32
BF16 = jnp.bfloat16
MIB = 1024 * 1024


def pairs(move):
    table = []
    for z in range(4):
        for c in range(2):
            for x in range(4):
                for y in range(4):
                    z2, c2, x2, y2 = move(z, c, x, y)
                    target = ((z2 % 4) * 2 + c2 % 2) * 16 + (x2 % 4) * 4 + y2 % 4
                    table.append(((z * 2 + c) * 16 + x * 4 + y, target))
    return table


HOPS = {}
for step in (1, -1):
    HOPS["first", step] = pairs(
        lambda z, c, x, y, s=step: (z, c, x, y + s) if c == 0 else (z, c, x + s, y)
    )
    HOPS["second", step] = pairs(
        lambda z, c, x, y, s=step: (z, c, x + s, y) if c == 0 else (z, c, x, y + s)
    )
HOPS["twin", 1] = pairs(lambda z, c, x, y: (z, c, x, y ^ 1))
HOPS["z_one", 1] = pairs(lambda z, c, x, y: (z ^ 1 if c == 0 else 3 - z, c, x, y))
HOPS["z_two", 1] = pairs(lambda z, c, x, y: (3 - z if c == 0 else z ^ 1, c, x, y))
HOPS["core", 1] = pairs(lambda z, c, x, y: (z, c + 1, x, y))


def hop(value, axis, step):
    return lax.ppermute(value, AXES, HOPS[axis, step])


def both(forward, backward, axis):
    return hop(forward, axis, 1), hop(backward, axis, -1)


def stack_rows(*parts):
    return jnp.concatenate(parts, axis=0)


def plus(base, *terms):
    total = base.astype(F32)
    for term in terms:
        total = total + term.astype(F32)
    return total.astype(BF16)


def pack(block):
    quarter = block.shape[0] // 4
    return jnp.concatenate([block[k * quarter : (k + 1) * quarter] for k in range(4)], axis=1)


def unpack(block):
    return jnp.concatenate([block[:, k * HD : (k + 1) * HD] for k in range(4)], axis=0)


def params(mebibytes):
    return pltpu.CompilerParams(vmem_limit_bytes=mebibytes * MIB)


def estimate(flops, moved):
    return pl.CostEstimate(flops=flops, bytes_accessed=moved, transcendentals=0)


VMEM = pl.BlockSpec(memory_space=pltpu.VMEM)
SMEM = pl.BlockSpec(memory_space=pltpu.SMEM)
FIXED = pl.BlockSpec(memory_space=pltpu.HBM)
ANYWHERE = pl.BlockSpec(memory_space=pl.ANY)
GROUP = 2
CHUNK = 64
WIDE = 512


def in_vmem(arrays):
    return [pltpu.with_memory_space_constraint(a, pltpu.VMEM) for a in arrays]


def place_of(order_ref, i, j):
    return order_ref[i * 4 + j]


def assemble(arrays, outputs):
    n_arrays = len(arrays)

    def body(*refs):
        for o_ref, (_, pieces) in zip(refs[n_arrays:], outputs, strict=True):
            for row, column, rows, columns, terms in pieces:
                parts = [refs[a][r : r + rows, c : c + columns] for a, r, c in terms]
                if len(parts) > 1:
                    total = parts[0].astype(F32)
                    for part in parts[1:]:
                        total = total + part.astype(F32)
                    parts = [total.astype(BF16)]
                o_ref[row : row + rows, column : column + columns] = parts[0]

    return pl.pallas_call(
        body,
        out_shape=[pltpu.VMEM(shape, BF16) for shape, _ in outputs],
        in_specs=[VMEM] * n_arrays,
        out_specs=[VMEM] * len(outputs),
        compiler_params=params(6),
        cost_estimate=estimate(0, 0),
        name="assemble",
    )(*in_vmem(arrays))


def rows_piece(row, rows, *terms):
    return (row, 0, rows, WIDE, [(a, r, 0) for a, r in terms])


def packed(row, rows, *terms):
    quarter = rows // 4
    pieces = []
    for k in range(4):
        places = [(a, start + k * quarter, column) for a, start, column in terms]
        pieces.append((row, k * HD, quarter, HD, places))
    return pieces


def kv_partial(tokens, gain, w_keyvalue, order, steps):
    spots = [(i, j) for i in steps for j in range(4)]
    count = len(spots)

    def body(order_ref, t_ref, g_ref, w_ref, o_ref, weights, sems):
        copies = []
        for n, (i, j) in enumerate(spots):
            target = place_of(order_ref, i, j)
            column = pl.multiple_of(lax.div(target, 2) * HD, HD)
            copies.append(
                pltpu.make_async_copy(
                    w_ref.at[lax.rem(target, 2), :, pl.ds(column, HD)],
                    weights.at[:, pl.ds(n * HD, HD)],
                    sems.at[n],
                )
            )
        for copy in copies:
            copy.start()
        own = g_ref[pl.ds(place_of(order_ref, 0, 0), 1), :]
        scaled = (t_ref[...].astype(F32) * own).astype(BF16)
        for copy in copies:
            copy.wait()
        for n in range(0, count * HD, WIDE):
            o_ref[:, n : n + WIDE] = jnp.dot(
                scaled, weights[:, n : n + WIDE], preferred_element_type=F32
            ).astype(BF16)

    return pl.pallas_call(
        body,
        out_shape=jax.ShapeDtypeStruct((WIDE, count * HD), BF16),
        in_specs=[SMEM, VMEM, VMEM, FIXED],
        out_specs=VMEM,
        scratch_shapes=[
            pltpu.VMEM((WIDE, count * HD), BF16),
            pltpu.SemaphoreType.DMA((count,)),
        ],
        compiler_params=params(6),
        cost_estimate=estimate(0, 0),
        name="kv_partial",
    )(order, tokens, gain, w_keyvalue)


def query_part(blocks, arrays, order, gain, w_query, carry):
    count = len(blocks)
    n_arrays = len(arrays)
    first = carry is None

    def body(order_ref, *refs):
        a_refs = refs[:n_arrays]
        g_ref, w_ref = refs[n_arrays : n_arrays + 2]
        q_ref, s_ref, scaled, weights, sems = refs[-5:]
        places = [place_of(order_ref, *spot) for spot, _ in blocks]

        def fetch(n):
            return pltpu.make_async_copy(
                w_ref.at[pl.ds(pl.multiple_of(places[n] * WIDE, WIDE), WIDE), :],
                weights.at[n // GROUP % 2, pl.ds(n % GROUP * WIDE, WIDE), :],
                sems.at[n],
            )

        for n in range(min(count, 2 * GROUP)):
            fetch(n).start()
        s_ref[...] = jnp.zeros_like(s_ref) if first else refs[n_arrays + 3][...]
        for low in range(0, count, GROUP):
            members = range(low, min(low + GROUP, count))
            for n in members:
                own = g_ref[pl.ds(places[n], 1), :]
                lanes_at = pl.ds((n - low) * WIDE, WIDE)
                for which, start, target, size in blocks[n][1]:

                    @pl.loop(0, size // CHUNK)
                    def _(step, which=which, start=start, target=target, own=own, lanes_at=lanes_at):
                        row = pl.multiple_of(step * CHUNK, CHUNK)
                        values = a_refs[which][pl.ds(start + row, CHUNK), :].astype(F32)
                        squares = values * values
                        lanes = squares[:, :HD]
                        for k in range(1, WIDE // HD):
                            lanes = lanes + squares[:, k * HD : (k + 1) * HD]
                        s_ref[pl.ds(target + row, CHUNK), :] += lanes
                        scaled[pl.ds(target + row, CHUNK), lanes_at] = (values * own).astype(BF16)

            for n in members:
                fetch(n).wait()
            depth = len(members) * WIDE
            for half in range(2):
                rows = slice(half * HALF, (half + 1) * HALF)
                product = jnp.dot(
                    scaled[rows, :depth], weights[low // GROUP % 2, :depth, :], preferred_element_type=F32
                )
                if low:
                    q_ref[rows, :] += product
                else:
                    q_ref[rows, :] = product if first else refs[n_arrays + 2][rows, :] + product
            for n in range(low + 2 * GROUP, min(low + 3 * GROUP, count)):
                fetch(n).start()

    carried = [] if first else list(carry)
    return pl.pallas_call(
        body,
        out_shape=(
            jax.ShapeDtypeStruct((WIDE, WIDE), F32),
            jax.ShapeDtypeStruct((WIDE, HD), F32),
        ),
        in_specs=[SMEM] + [VMEM] * n_arrays + [VMEM, FIXED] + [VMEM] * len(carried),
        out_specs=(VMEM, VMEM),
        scratch_shapes=[
            pltpu.VMEM((WIDE, GROUP * WIDE), BF16),
            pltpu.VMEM((2, GROUP * WIDE, WIDE), BF16),
            pltpu.SemaphoreType.DMA((count,)),
        ],
        input_output_aliases={} if first else {n_arrays + 3: 0, n_arrays + 4: 1},
        compiler_params=params(8),
        cost_estimate=estimate(0, 0),
        name="query_part",
    )(order, *in_vmem(arrays), gain, w_query, *in_vmem(carried))


def gather_blocks(pools, codes):
    branches = codes.shape[0]
    span = PDEPTH * PB + PB

    def body(code_ref, *refs):
        pool_refs, (o_ref, sems) = refs[:4], refs[4:]
        for b in range(branches):
            for d in range(PDEPTH):
                code = code_ref[b, d]
                slot, block = lax.rem(lax.div(code, 16), 2), lax.rem(code, 16)
                for which, source in enumerate(pool_refs):

                    @pl.when(lax.div(code, 32) == which)
                    def _(source=source):
                        pltpu.make_async_copy(
                            source.at[slot, :, block], o_ref.at[b, :, pl.ds(d * PB, PB), :], sems.at[b, d]
                        ).start()

        for b in range(branches):
            for d in range(PDEPTH):
                pltpu.make_async_copy(
                    pool_refs[0].at[0, :, 0], o_ref.at[b, :, pl.ds(d * PB, PB), :], sems.at[b, d]
                ).wait()

    return pl.pallas_call(
        body,
        out_shape=jax.ShapeDtypeStruct((branches, 2, span, HD), BF16),
        in_specs=[SMEM] + [ANYWHERE] * 4,
        out_specs=VMEM,
        scratch_shapes=[pltpu.SemaphoreType.DMA((branches, PDEPTH))],
        compiler_params=params(6),
        cost_estimate=estimate(0, 0),
        name="gather_blocks",
    )(codes, *pools)


def middle(query, squares, order, keyvalue, tables, prefix, lengths, w_output):
    branches = WIDE // PB
    heads = WIDE // HD
    span = PDEPTH * PB + PB
    scale = 1.0 / math.sqrt(HD)
    spots = [(2, 2), (1, 2), (3, 2), (0, 2)]

    def body(
        order_ref, len_ref, q_ref, s_ref, mine_ref, other_ref, cos_ref, sin_ref, prefix_ref, wo_ref,
        heads_ref, far_ref, kv_ref,
        wo, qb, wsems,
    ):
        copies = []
        for n, (i, j) in enumerate(spots):
            column = pl.multiple_of(place_of(order_ref, i, j) * WIDE, WIDE)
            copies.append(
                pltpu.make_async_copy(wo_ref.at[:, pl.ds(column, WIDE)], wo.at[n], wsems.at[n])
            )
        for copy in copies:
            copy.start()
        total = jnp.sum(s_ref[...], axis=1, keepdims=True)
        factor = lax.rsqrt(total * (1.0 / 8192.0) + 1e-06)
        cos_part = cos_ref[...] * factor
        sin_part = sin_ref[...] * factor

        def rope(v, cos_part, sin_part):
            return (v * cos_part + pltpu.roll(v, HD // 2, 1) * sin_part).astype(BF16)

        even = lax.rem(place_of(order_ref, 0, 0), 2) == 0
        mine, other = mine_ref[...].astype(F32), other_ref[...].astype(F32)
        new_keys = rope(jnp.where(even, mine, other), cos_part, sin_part)
        new_values = (jnp.where(even, other, mine) * factor).astype(BF16)
        for b in range(branches):
            kv_ref[b, 0, PDEPTH * PB :, :] = new_keys[b * PB : (b + 1) * PB]
            kv_ref[b, 1, PDEPTH * PB :, :] = new_values[b * PB : (b + 1) * PB]
        cos_part, sin_part = cos_part * scale, sin_part * scale
        for h in range(heads):
            qb[h] = rope(q_ref[:, h * HD : (h + 1) * HD], cos_part, sin_part)
        column = lax.broadcasted_iota(jnp.int32, (heads * PB, span), 1)
        within = lax.rem(lax.broadcasted_iota(jnp.int32, (heads * PB, span), 0), PB)
        own_seen = (column >= PDEPTH * PB) & (column - PDEPTH * PB <= within)
        for b in range(branches):
            queries = qb[:, b * PB : (b + 1) * PB, :].reshape(heads * PB, HD)
            scores = lax.dot_general(
                queries, kv_ref[b, 0], (((1,), (1,)), ((), ())), preferred_element_type=F32
            )
            seen = (column < len_ref[b] * PB) | own_seen
            scores = jnp.where(seen, scores, -1e30)
            highest = jnp.max(scores, axis=1, keepdims=True)
            expo = jnp.exp(scores - highest)
            inverse = 1.0 / jnp.sum(expo, axis=1, keepdims=True)
            mixed = jnp.dot(expo.astype(BF16), kv_ref[b, 1], preferred_element_type=F32)
            mixed = (mixed * inverse).astype(BF16)
            for h in range(heads):
                heads_ref[b * PB : (b + 1) * PB, h * HD : (h + 1) * HD] = mixed[
                    h * PB : (h + 1) * PB
                ]
        for n, copy in enumerate(copies):
            copy.wait()
            far_ref[n] = jnp.dot(heads_ref[...], wo[n], preferred_element_type=F32).astype(BF16)

    return pl.pallas_call(
        body,
        out_shape=(
            jax.ShapeDtypeStruct((WIDE, WIDE), BF16),
            jax.ShapeDtypeStruct((len(spots), WIDE, WIDE), BF16),
            jax.ShapeDtypeStruct(prefix.shape, BF16),
        ),
        in_specs=[SMEM] * 2 + [VMEM] * 7 + [FIXED],
        out_specs=(VMEM, VMEM, VMEM),
        scratch_shapes=[
            pltpu.VMEM((len(spots), WIDE, WIDE), BF16),
            pltpu.VMEM((heads, WIDE, HD), BF16),
            pltpu.SemaphoreType.DMA((len(spots),)),
        ],
        input_output_aliases={8: 2},
        compiler_params=params(8),
        cost_estimate=estimate(0, 0),
        name="middle",
    )(
        order, lengths, *in_vmem([query, squares, *keyvalue, *tables, prefix]), w_output
    )[:2]


def output_part(heads_out, w_output, order, spots):
    count = len(spots)

    def body(order_ref, h_ref, w_ref, o_ref, weights, sems):
        copies = []
        for n, (i, j) in enumerate(spots):
            column = pl.multiple_of(place_of(order_ref, i, j) * WIDE, WIDE)
            copies.append(
                pltpu.make_async_copy(w_ref.at[:, pl.ds(column, WIDE)], weights.at[n], sems.at[n])
            )
        for copy in copies:
            copy.start()
        for n, copy in enumerate(copies):
            copy.wait()
            o_ref[n] = jnp.dot(h_ref[...], weights[n], preferred_element_type=F32).astype(BF16)

    return pl.pallas_call(
        body,
        out_shape=jax.ShapeDtypeStruct((count, WIDE, WIDE), BF16),
        in_specs=[SMEM, VMEM, FIXED],
        out_specs=VMEM,
        scratch_shapes=[
            pltpu.VMEM((count, WIDE, WIDE), BF16),
            pltpu.SemaphoreType.DMA((count,)),
        ],
        compiler_params=params(6),
        cost_estimate=estimate(0, 0),
        name="output_part",
    )(order, heads_out, w_output)


def local(tokens, gain, w_query, w_keyvalue, w_output, cache, parents, lengths):
    bar = lax.optimization_barrier
    group = lax.axis_index("branch")
    place = lax.axis_index("tensor")
    x, y = place // 4, place % 4
    z, core = group // 2, group % 2
    row_count = tokens.shape[0]
    branch_count = row_count // PB

    count = jnp.arange(16, dtype=jnp.int32)
    i_step, j_step = count // 4, count % 4
    dx = jnp.where(core == 0, j_step, i_step)
    dy = jnp.where(core == 0, i_step, j_step)
    order = ((x + dx) % 4) * 4 + (y + dy) % 4
    gains = gain.astype(F32).reshape(16, WIDE)
    w_query, w_keyvalue, w_output = [
        pltpu.with_memory_space_constraint(w, pltpu.HBM) for w in (w_query, w_keyvalue, w_output)
    ]

    s1 = both(tokens, tokens, "first")
    kv = kv_partial(tokens, gains, w_keyvalue, order, (0, 1, 3, 2))
    k_far = both(kv[:HALF, 3 * WIDE :], kv[HALF:, 3 * WIDE :], "first")
    kv_head = place * (w_query.shape[1] // HD) // (HEADS // KVH)
    cache_head = lax.dynamic_slice_in_dim(cache, kv_head * HD, HD, 3)
    z_one = hop(cache_head, "z_one", 1)
    b1m, b1p, k_m, k_p, kv_near, z_one = bar((*s1, *k_far, kv, z_one))
    (near,) = assemble(
        [tokens, b1p, b1m],
        [((3 * WIDE, WIDE), [rows_piece(n * WIDE, WIDE, (n, 0)) for n in range(3)])],
    )
    s2 = both(near, near, "second")
    s3 = both(
        *assemble(
            [b1m, b1p, kv_near, k_m, k_p],
            [
                (
                    (3 * HALF, WIDE),
                    [
                        rows_piece(0, HALF, (0, 0)),
                        (HALF, 0, HALF, WIDE, [(2, 0, WIDE), (3, 0, 0)]),
                        (2 * HALF, 0, HALF, WIDE, [(2, HALF, WIDE)]),
                    ],
                ),
                (
                    (3 * HALF, WIDE),
                    [
                        rows_piece(0, HALF, (1, HALF)),
                        (HALF, 0, HALF, WIDE, [(2, 0, 2 * WIDE)]),
                        (2 * HALF, 0, HALF, WIDE, [(2, HALF, 2 * WIDE), (4, 0, 0)]),
                    ],
                ),
            ],
        ),
        "first",
    )
    part = query_part(
        [((0, 0), [(0, 0, 0, WIDE)]), ((1, 0), [(1, 0, 0, WIDE)]), ((3, 0), [(2, 0, 0, WIDE)])],
        [tokens, b1p, b1m],
        order,
        gains,
        w_query,
        None,
    )
    pool = jnp.stack([cache_head, z_one])
    z_two = hop(pool, "z_two", 1)
    b3m, b3p, b2m, b2p, pool, z_two, *part = bar((*s3, *s2, pool, z_two, *part))
    (to_next,) = assemble(
        [b3m, b3p, kv_near, b2m],
        [
            (
                (5 * HALF + HALF // 4, WIDE),
                [rows_piece(0, HALF, (0, 0)), rows_piece(HALF, HALF, (1, 0))]
                + [rows_piece(WIDE + n * HALF, HALF, (3, n * WIDE)) for n in range(3)]
                + packed(5 * HALF, HALF, (2, 0, 2 * HD), (0, HALF, 2 * HD), (1, HALF, 2 * HD)),
            )
        ],
    )
    (to_last,) = assemble(
        [b3m, b3p, kv_near, b2p],
        [
            (
                (5 * HALF + HALF // 4, WIDE),
                [rows_piece(0, HALF, (0, 0)), rows_piece(HALF, HALF, (1, 0))]
                + [rows_piece(WIDE + n * HALF, HALF, (3, n * WIDE + HALF)) for n in range(3)]
                + packed(5 * HALF, HALF, (2, HALF, 2 * HD), (0, WIDE, 2 * HD), (1, WIDE, 2 * HD)),
            )
        ],
    )
    s5 = both(to_next, to_last, "second")
    (ksum,) = assemble(
        [kv_near, b3m, b3p],
        [((WIDE, WIDE), [(0, 0, WIDE, WIDE, [(0, 0, 0), (1, HALF, 0), (2, HALF, 0)])])],
    )
    near_twin, far_twin = hop(pool, "core", 1), hop(z_two, "core", 1)
    my_lengths = lax.dynamic_slice_in_dim(lengths, group * branch_count, branch_count, 0)
    my_parents = lax.dynamic_slice_in_dim(parents, group * branch_count, branch_count, 0)
    owner = my_parents // 16
    owner_z, owner_core = owner // 2, owner % 2
    across = z + 1 - 2 * (z % 2)
    partner = jnp.where(owner_core == 0, across, 3 - z)
    slot = jnp.where(
        owner_z == z, 0, jnp.where(owner_z == partner, 1, jnp.where(owner_z == (z + 2) % 4, 3, 2))
    )
    codes = jnp.where(owner_core == core, 0, 64) + slot * 16 + my_parents % 16

    positions = jnp.repeat(my_lengths, PB) * PB + jnp.tile(
        jnp.arange(PB, dtype=jnp.int32), branch_count
    )
    halfway = HD // 2
    frequency = jnp.exp(jnp.arange(halfway, dtype=F32) * (-2.0 * math.log(1000000.0) / HD))
    angles = positions.astype(F32)[:, None] * frequency[None, :]
    cosine, sine = jnp.cos(angles), jnp.sin(angles)
    cosine = jnp.concatenate([cosine, cosine], axis=1)
    sine = jnp.concatenate([-sine, sine], axis=1)

    part = query_part(
        [
            ((2, 0), [(0, 0, 0, HALF), (1, 0, HALF, HALF)]),
            ((0, 1), [(2, 0, 0, WIDE)]),
            ((1, 1), [(2, WIDE, 0, WIDE)]),
            ((3, 1), [(2, 2 * WIDE, 0, WIDE)]),
            ((0, 3), [(3, 0, 0, WIDE)]),
            ((1, 3), [(3, WIDE, 0, WIDE)]),
            ((3, 3), [(3, 2 * WIDE, 0, WIDE)]),
        ],
        [b3m, b3p, b2p, b2m],
        order,
        gains,
        w_query,
        part,
    )
    pools = [
        pltpu.with_memory_space_constraint(a, pltpu.HBM) for a in (pool, z_two, near_twin, far_twin)
    ]
    prefix = gather_blocks(pools, codes)
    b5m, b5p, prefix, cosine, sine, ksum, *part = bar((*s5, prefix, cosine, sine, ksum, *part))
    quarter = HALF // 4
    s7 = both(
        *assemble(
            [b5m, b5p, ksum],
            [
                (
                    (HALF + WIDE // 4, WIDE),
                    [rows_piece(0, HALF, (0, 0))]
                    + [
                        piece
                        for k in range(4)
                        for piece in [
                            (
                                HALF,
                                k * HD,
                                2 * quarter,
                                HD,
                                [(2, k * 2 * quarter, HD)],
                            )
                        ]
                        if k >= 2
                    ]
                    + [
                        (
                            HALF + t * quarter,
                            k * HD,
                            quarter,
                            HD,
                            [(2, (2 * k + t) * quarter, HD), (0, 5 * HALF, (2 * k + t) * HD)],
                        )
                        for k in range(2)
                        for t in range(2)
                    ],
                ),
                (
                    (HALF + WIDE // 4, WIDE),
                    [rows_piece(0, HALF, (1, HALF))]
                    + [
                        (HALF, k * HD, 2 * quarter, HD, [(2, k * 2 * quarter, 3 * HD)])
                        for k in range(2)
                    ]
                    + [
                        (
                            HALF + t * quarter,
                            k * HD,
                            quarter,
                            HD,
                            [(2, (2 * k + t) * quarter, 3 * HD), (1, 5 * HALF, (2 * k + t - 4) * HD)],
                        )
                        for k in range(2, 4)
                        for t in range(2)
                    ],
                ),
            ],
        ),
        "second",
    )
    part = query_part(
        [
            ((2, 1), [(0, 0, 0, WIDE)]),
            ((2, 3), [(1, 0, 0, WIDE)]),
            ((0, 2), [(1, WIDE, 0, HALF), (0, WIDE, HALF, HALF)]),
            ((1, 2), [(1, WIDE + HALF, 0, HALF), (0, WIDE + HALF, HALF, HALF)]),
            ((3, 2), [(1, 2 * WIDE, 0, HALF), (0, 2 * WIDE, HALF, HALF)]),
        ],
        [b5p, b5m],
        order,
        gains,
        w_query,
        part,
    )
    b7m, b7p, *part = bar((*s7, *part))
    (mine,) = assemble(
        [ksum, b7m, b7p],
        [
            (
                (WIDE, HD),
                [
                    (k * 128, 0, 128, HD, [(0, k * 128, 0), (1, HALF, k * HD), (2, HALF, k * HD)])
                    for k in range(4)
                ],
            )
        ],
    )
    other = hop(mine, "twin", 1)
    part = query_part(
        [
            ((2, 2), [(0, 0, 0, HALF), (1, 0, HALF, HALF)]),
        ],
        [b7m, b7p],
        order,
        gains,
        w_query,
        part,
    )
    heads_out, far = middle(
        *part, order, (mine, other), (cosine, sine), prefix, my_lengths, w_output
    )

    ra = both(far[0, :HALF], far[0, HALF:], "second")
    rb = both(
        stack_rows(far[1, :HALF], far[2, :HALF], far[3, :HALF]),
        stack_rows(far[1, HALF:], far[2, HALF:], far[3, HALF:]),
        "second",
    )
    spots = [(2, 1), (2, 3), (1, 1), (3, 1), (1, 3), (3, 3)]
    rest = output_part(heads_out, w_output, order, spots)
    ra_m, ra_p, rest = bar((*ra, rest))
    q21, q23, q11, q31, q13, q33 = [rest[n] for n in range(6)]
    rc = both(
        stack_rows(plus(q21[:HALF], ra_m), q21[HALF:]),
        stack_rows(q23[:HALF], plus(q23[HALF:], ra_p)),
        "second",
    )
    rb_m, rb_p = bar(rb)
    rd = both(
        stack_rows(
            plus(q11[:HALF], rb_m[:HALF]), q11[HALF:], plus(q31[:HALF], rb_m[HALF:WIDE]), q31[HALF:]
        ),
        stack_rows(
            q13[:HALF], plus(q13[HALF:], rb_p[:HALF]), q33[:HALF], plus(q33[HALF:], rb_p[HALF:WIDE])
        ),
        "second",
    )
    spots = [(2, 0), (0, 1), (0, 3), (1, 0), (3, 0), (0, 0)]
    heads_late, rb_m = bar((heads_out, rb_m))
    rest = output_part(heads_late, w_output, order, spots)
    rc_m, rc_p, rest = bar((*rc, rest))
    q20, q01, q03, q10, q30, q00 = [rest[n] for n in range(6)]
    sum2 = plus(q20, rc_m, rc_p)
    re = both(sum2[:HALF], sum2[HALF:], "first")
    re_m, re_p, rb_m, rb_p = bar((*re, rb_m, rb_p))
    rf = both(
        stack_rows(plus(q01[:HALF], rb_m[WIDE:]), q01[HALF:]),
        stack_rows(q03[:HALF], plus(q03[HALF:], rb_p[WIDE:])),
        "second",
    )
    rd_m, rd_p = bar(rd)
    sum1 = stack_rows(
        plus(q10[:HALF], rd_m[:HALF], rd_p[:HALF], re_m), plus(q10[HALF:], rd_m[HALF:WIDE], rd_p[HALF:WIDE])
    )
    sum3 = stack_rows(
        plus(q30[:HALF], rd_m[WIDE : WIDE + HALF], rd_p[WIDE : WIDE + HALF]),
        plus(q30[HALF:], rd_m[WIDE + HALF :], rd_p[WIDE + HALF :], re_p),
    )
    rg = both(sum1, sum3, "first")
    return plus(q00, *rf, *rg)


def solution(mesh):
    return jax.shard_map(
        local,
        mesh=mesh,
        in_specs=(
            P("branch", "tensor"),
            P(),
            P(None, "tensor"),
            P(None, "tensor", None),
            P("tensor", None),
            P(None, "branch", None, None),
            P(),
            P(),
        ),
        out_specs=P("branch", "tensor"),
        check_vma=False,
    )
```

```python
import math

import jax
import jax.numpy as jnp
from jax import lax
from jax.experimental import pallas as pl
from jax.experimental.pallas import tpu as pltpu
from jax.sharding import PartitionSpec as P

HEADS = 64
KVH = 8
HD = 128
PB = 64
PDEPTH = 4
HALF = 256
AXES = ("branch", "tensor")
F32 = jnp.float32
BF16 = jnp.bfloat16
MIB = 1024 * 1024


def pairs(move):
    table = []
    for z in range(4):
        for c in range(2):
            for x in range(4):
                for y in range(4):
                    z2, c2, x2, y2 = move(z, c, x, y)
                    target = ((z2 % 4) * 2 + c2 % 2) * 16 + (x2 % 4) * 4 + y2 % 4
                    table.append(((z * 2 + c) * 16 + x * 4 + y, target))
    return table


HOPS = {}
for step in (1, -1):
    HOPS["first", step] = pairs(
        lambda z, c, x, y, s=step: (z, c, x, y + s) if c == 0 else (z, c, x + s, y)
    )
    HOPS["second", step] = pairs(
        lambda z, c, x, y, s=step: (z, c, x + s, y) if c == 0 else (z, c, x, y + s)
    )
HOPS["twin", 1] = pairs(lambda z, c, x, y: (z, c, x, y ^ 1))
HOPS["z_one", 1] = pairs(lambda z, c, x, y: (z ^ 1 if c == 0 else 3 - z, c, x, y))
HOPS["z_two", 1] = pairs(lambda z, c, x, y: (3 - z if c == 0 else z ^ 1, c, x, y))
HOPS["core", 1] = pairs(lambda z, c, x, y: (z, c + 1, x, y))


def hop(value, axis, step):
    return lax.ppermute(value, AXES, HOPS[axis, step])


def both(forward, backward, axis):
    return hop(forward, axis, 1), hop(backward, axis, -1)


def stack_rows(*parts):
    return jnp.concatenate(parts, axis=0)


def plus(base, *terms):
    total = base.astype(F32)
    for term in terms:
        total = total + term.astype(F32)
    return total.astype(BF16)


def pack(block):
    quarter = block.shape[0] // 4
    return jnp.concatenate([block[k * quarter : (k + 1) * quarter] for k in range(4)], axis=1)


def unpack(block):
    return jnp.concatenate([block[:, k * HD : (k + 1) * HD] for k in range(4)], axis=0)


def params(mebibytes):
    return pltpu.CompilerParams(vmem_limit_bytes=mebibytes * MIB)


def estimate(flops, moved):
    return pl.CostEstimate(flops=flops, bytes_accessed=moved, transcendentals=0)


VMEM = pl.BlockSpec(memory_space=pltpu.VMEM)
SMEM = pl.BlockSpec(memory_space=pltpu.SMEM)
FIXED = pl.BlockSpec(memory_space=pltpu.HBM)
ANYWHERE = pl.BlockSpec(memory_space=pl.ANY)
GROUP = 2
CHUNK = 64
WIDE = 512


def in_vmem(arrays):
    return [pltpu.with_memory_space_constraint(a, pltpu.VMEM) for a in arrays]


def place_of(order_ref, i, j):
    return order_ref[i * 4 + j]


def assemble(arrays, outputs):
    n_arrays = len(arrays)

    def body(*refs):
        for o_ref, (_, pieces) in zip(refs[n_arrays:], outputs, strict=True):
            for row, column, rows, columns, terms in pieces:
                parts = [refs[a][r : r + rows, c : c + columns] for a, r, c in terms]
                if len(parts) > 1:
                    total = parts[0].astype(F32)
                    for part in parts[1:]:
                        total = total + part.astype(F32)
                    parts = [total.astype(BF16)]
                o_ref[row : row + rows, column : column + columns] = parts[0]

    return pl.pallas_call(
        body,
        out_shape=[pltpu.VMEM(shape, BF16) for shape, _ in outputs],
        in_specs=[VMEM] * n_arrays,
        out_specs=[VMEM] * len(outputs),
        compiler_params=params(6),
        cost_estimate=estimate(0, 0),
        name="assemble",
    )(*in_vmem(arrays))


def rows_piece(row, rows, *terms):
    return (row, 0, rows, WIDE, [(a, r, 0) for a, r in terms])


def packed(row, rows, *terms):
    quarter = rows // 4
    pieces = []
    for k in range(4):
        places = [(a, start + k * quarter, column) for a, start, column in terms]
        pieces.append((row, k * HD, quarter, HD, places))
    return pieces


def kv_partial(tokens, gain, w_keyvalue, order, steps):
    spots = [(i, j) for i in steps for j in range(4)]
    count = len(spots)

    def body(order_ref, t_ref, g_ref, w_ref, o_ref, weights, sems):
        copies = []
        for n, (i, j) in enumerate(spots):
            target = place_of(order_ref, i, j)
            column = pl.multiple_of(lax.div(target, 2) * HD, HD)
            copies.append(
                pltpu.make_async_copy(
                    w_ref.at[lax.rem(target, 2), :, pl.ds(column, HD)],
                    weights.at[:, pl.ds(n * HD, HD)],
                    sems.at[n],
                )
            )
        for copy in copies:
            copy.start()
        own = g_ref[pl.ds(place_of(order_ref, 0, 0), 1), :]
        scaled = (t_ref[...].astype(F32) * own).astype(BF16)
        for copy in copies:
            copy.wait()
        for n in range(0, count * HD, WIDE):
            o_ref[:, n : n + WIDE] = jnp.dot(
                scaled, weights[:, n : n + WIDE], preferred_element_type=F32
            ).astype(BF16)

    return pl.pallas_call(
        body,
        out_shape=jax.ShapeDtypeStruct((WIDE, count * HD), BF16),
        in_specs=[SMEM, VMEM, VMEM, FIXED],
        out_specs=VMEM,
        scratch_shapes=[
            pltpu.VMEM((WIDE, count * HD), BF16),
            pltpu.SemaphoreType.DMA((count,)),
        ],
        compiler_params=params(6),
        cost_estimate=estimate(0, 0),
        name="kv_partial",
    )(order, tokens, gain, w_keyvalue)


def query_part(blocks, arrays, order, gain, w_query, carry):
    count = len(blocks)
    n_arrays = len(arrays)
    first = carry is None

    def body(order_ref, *refs):
        a_refs = refs[:n_arrays]
        g_ref, w_ref = refs[n_arrays : n_arrays + 2]
        q_ref, s_ref, scaled, weights, sems = refs[-5:]
        places = [place_of(order_ref, *spot) for spot, _ in blocks]

        def fetch(n):
            return pltpu.make_async_copy(
                w_ref.at[pl.ds(pl.multiple_of(places[n] * WIDE, WIDE), WIDE), :],
                weights.at[n // GROUP % 2, pl.ds(n % GROUP * WIDE, WIDE), :],
                sems.at[n],
            )

        for n in range(min(count, 2 * GROUP)):
            fetch(n).start()
        s_ref[...] = jnp.zeros_like(s_ref) if first else refs[n_arrays + 3][...]
        for low in range(0, count, GROUP):
            members = range(low, min(low + GROUP, count))
            for n in members:
                own = g_ref[pl.ds(places[n], 1), :]
                lanes_at = pl.ds((n - low) * WIDE, WIDE)
                for which, start, target, size in blocks[n][1]:

                    @pl.loop(0, size // CHUNK)
                    def _(step, which=which, start=start, target=target, own=own, lanes_at=lanes_at):
                        row = pl.multiple_of(step * CHUNK, CHUNK)
                        values = a_refs[which][pl.ds(start + row, CHUNK), :].astype(F32)
                        squares = values * values
                        lanes = squares[:, :HD]
                        for k in range(1, WIDE // HD):
                            lanes = lanes + squares[:, k * HD : (k + 1) * HD]
                        s_ref[pl.ds(target + row, CHUNK), :] += lanes
                        scaled[pl.ds(target + row, CHUNK), lanes_at] = (values * own).astype(BF16)

            for n in members:
                fetch(n).wait()
            depth = len(members) * WIDE
            for half in range(2):
                rows = slice(half * HALF, (half + 1) * HALF)
                product = jnp.dot(
                    scaled[rows, :depth], weights[low // GROUP % 2, :depth, :], preferred_element_type=F32
                )
                if low:
                    q_ref[rows, :] += product
                else:
                    q_ref[rows, :] = product if first else refs[n_arrays + 2][rows, :] + product
            for n in range(low + 2 * GROUP, min(low + 3 * GROUP, count)):
                fetch(n).start()

    carried = [] if first else list(carry)
    return pl.pallas_call(
        body,
        out_shape=(
            jax.ShapeDtypeStruct((WIDE, WIDE), F32),
            jax.ShapeDtypeStruct((WIDE, HD), F32),
        ),
        in_specs=[SMEM] + [VMEM] * n_arrays + [VMEM, FIXED] + [VMEM] * len(carried),
        out_specs=(VMEM, VMEM),
        scratch_shapes=[
            pltpu.VMEM((WIDE, GROUP * WIDE), BF16),
            pltpu.VMEM((2, GROUP * WIDE, WIDE), BF16),
            pltpu.SemaphoreType.DMA((count,)),
        ],
        input_output_aliases={} if first else {n_arrays + 3: 0, n_arrays + 4: 1},
        compiler_params=params(8),
        cost_estimate=estimate(0, 0),
        name="query_part",
    )(order, *in_vmem(arrays), gain, w_query, *in_vmem(carried))


def gather_blocks(pools, codes):
    branches = codes.shape[0]
    span = PDEPTH * PB + PB

    def body(code_ref, *refs):
        pool_refs, (o_ref, sems) = refs[:4], refs[4:]
        for b in range(branches):
            for d in range(PDEPTH):
                code = code_ref[b, d]
                slot, block = lax.rem(lax.div(code, 16), 2), lax.rem(code, 16)
                for which, source in enumerate(pool_refs):

                    @pl.when(lax.div(code, 32) == which)
                    def _(source=source):
                        pltpu.make_async_copy(
                            source.at[slot, :, block], o_ref.at[b, :, pl.ds(d * PB, PB), :], sems.at[b, d]
                        ).start()

        for b in range(branches):
            for d in range(PDEPTH):
                pltpu.make_async_copy(
                    pool_refs[0].at[0, :, 0], o_ref.at[b, :, pl.ds(d * PB, PB), :], sems.at[b, d]
                ).wait()

    return pl.pallas_call(
        body,
        out_shape=jax.ShapeDtypeStruct((branches, 2, span, HD), BF16),
        in_specs=[SMEM] + [ANYWHERE] * 4,
        out_specs=VMEM,
        scratch_shapes=[pltpu.SemaphoreType.DMA((branches, PDEPTH))],
        compiler_params=params(6),
        cost_estimate=estimate(0, 0),
        name="gather_blocks",
    )(codes, *pools)


def middle(query, squares, order, keyvalue, tables, prefix, lengths, w_output):
    branches = WIDE // PB
    heads = WIDE // HD
    span = PDEPTH * PB + PB
    scale = 1.0 / math.sqrt(HD)
    spots = [(2, 2), (1, 2), (3, 2), (0, 2)]

    def body(
        order_ref, len_ref, q_ref, s_ref, mine_ref, other_ref, cos_ref, sin_ref, prefix_ref, wo_ref,
        heads_ref, far_ref, kv_ref,
        wo, qb, wsems,
    ):
        copies = []
        for n, (i, j) in enumerate(spots):
            column = pl.multiple_of(place_of(order_ref, i, j) * WIDE, WIDE)
            copies.append(
                pltpu.make_async_copy(wo_ref.at[:, pl.ds(column, WIDE)], wo.at[n], wsems.at[n])
            )
        for copy in copies:
            copy.start()
        total = jnp.sum(s_ref[...], axis=1, keepdims=True)
        factor = lax.rsqrt(total * (1.0 / 8192.0) + 1e-06)
        cos_part = cos_ref[...] * factor
        sin_part = sin_ref[...] * factor

        def rope(v, cos_part, sin_part):
            return (v * cos_part + pltpu.roll(v, HD // 2, 1) * sin_part).astype(BF16)

        even = lax.rem(place_of(order_ref, 0, 0), 2) == 0
        mine, other = mine_ref[...].astype(F32), other_ref[...].astype(F32)
        new_keys = rope(jnp.where(even, mine, other), cos_part, sin_part)
        new_values = (jnp.where(even, other, mine) * factor).astype(BF16)
        for b in range(branches):
            kv_ref[b, 0, PDEPTH * PB :, :] = new_keys[b * PB : (b + 1) * PB]
            kv_ref[b, 1, PDEPTH * PB :, :] = new_values[b * PB : (b + 1) * PB]
        cos_part, sin_part = cos_part * scale, sin_part * scale
        for h in range(heads):
            qb[h] = rope(q_ref[:, h * HD : (h + 1) * HD], cos_part, sin_part)
        column = lax.broadcasted_iota(jnp.int32, (heads * PB, span), 1)
        within = lax.rem(lax.broadcasted_iota(jnp.int32, (heads * PB, span), 0), PB)
        own_seen = (column >= PDEPTH * PB) & (column - PDEPTH * PB <= within)
        for b in range(branches):
            queries = qb[:, b * PB : (b + 1) * PB, :].reshape(heads * PB, HD)
            scores = lax.dot_general(
                queries, kv_ref[b, 0], (((1,), (1,)), ((), ())), preferred_element_type=F32
            )
            seen = (column < len_ref[b] * PB) | own_seen
            scores = jnp.where(seen, scores, -1e30)
            highest = jnp.max(scores, axis=1, keepdims=True)
            expo = jnp.exp(scores - highest)
            inverse = 1.0 / jnp.sum(expo, axis=1, keepdims=True)
            mixed = jnp.dot(expo.astype(BF16), kv_ref[b, 1], preferred_element_type=F32)
            mixed = (mixed * inverse).astype(BF16)
            for h in range(heads):
                heads_ref[b * PB : (b + 1) * PB, h * HD : (h + 1) * HD] = mixed[
                    h * PB : (h + 1) * PB
                ]
        for n, copy in enumerate(copies):
            copy.wait()
            far_ref[n] = jnp.dot(heads_ref[...], wo[n], preferred_element_type=F32).astype(BF16)

    return pl.pallas_call(
        body,
        out_shape=(
            jax.ShapeDtypeStruct((WIDE, WIDE), BF16),
            jax.ShapeDtypeStruct((len(spots), WIDE, WIDE), BF16),
            jax.ShapeDtypeStruct(prefix.shape, BF16),
        ),
        in_specs=[SMEM] * 2 + [VMEM] * 7 + [FIXED],
        out_specs=(VMEM, VMEM, VMEM),
        scratch_shapes=[
            pltpu.VMEM((len(spots), WIDE, WIDE), BF16),
            pltpu.VMEM((heads, WIDE, HD), BF16),
            pltpu.SemaphoreType.DMA((len(spots),)),
        ],
        input_output_aliases={8: 2},
        compiler_params=params(8),
        cost_estimate=estimate(0, 0),
        name="middle",
    )(
        order, lengths, *in_vmem([query, squares, *keyvalue, *tables, prefix]), w_output
    )[:2]


def output_part(heads_out, w_output, order, spots):
    count = len(spots)

    def body(order_ref, h_ref, w_ref, o_ref, weights, sems):
        copies = []
        for n, (i, j) in enumerate(spots):
            column = pl.multiple_of(place_of(order_ref, i, j) * WIDE, WIDE)
            copies.append(
                pltpu.make_async_copy(w_ref.at[:, pl.ds(column, WIDE)], weights.at[n], sems.at[n])
            )
        for copy in copies:
            copy.start()
        for n, copy in enumerate(copies):
            copy.wait()
            o_ref[n] = jnp.dot(h_ref[...], weights[n], preferred_element_type=F32).astype(BF16)

    return pl.pallas_call(
        body,
        out_shape=jax.ShapeDtypeStruct((count, WIDE, WIDE), BF16),
        in_specs=[SMEM, VMEM, FIXED],
        out_specs=VMEM,
        scratch_shapes=[
            pltpu.VMEM((count, WIDE, WIDE), BF16),
            pltpu.SemaphoreType.DMA((count,)),
        ],
        compiler_params=params(6),
        cost_estimate=estimate(0, 0),
        name="output_part",
    )(order, heads_out, w_output)


def local(tokens, gain, w_query, w_keyvalue, w_output, cache, parents, lengths):
    bar = lax.optimization_barrier
    group = lax.axis_index("branch")
    place = lax.axis_index("tensor")
    x, y = place // 4, place % 4
    z, core = group // 2, group % 2
    row_count = tokens.shape[0]
    branch_count = row_count // PB

    count = jnp.arange(16, dtype=jnp.int32)
    i_step, j_step = count // 4, count % 4
    dx = jnp.where(core == 0, j_step, i_step)
    dy = jnp.where(core == 0, i_step, j_step)
    order = ((x + dx) % 4) * 4 + (y + dy) % 4
    gains = gain.astype(F32).reshape(16, WIDE)
    w_query, w_keyvalue, w_output = [
        pltpu.with_memory_space_constraint(w, pltpu.HBM) for w in (w_query, w_keyvalue, w_output)
    ]

    s1 = both(tokens, tokens, "first")
    kv = kv_partial(tokens, gains, w_keyvalue, order, (0, 1, 3, 2))
    k_far = both(kv[:HALF, 3 * WIDE :], kv[HALF:, 3 * WIDE :], "first")
    b1m, b1p, k_m, k_p, kv_near, cache = bar((*s1, *k_far, kv, cache))
    (near,) = assemble(
        [tokens, b1p, b1m],
        [((3 * WIDE, WIDE), [rows_piece(n * WIDE, WIDE, (n, 0)) for n in range(3)])],
    )
    s2 = both(near, near, "second")
    s3 = both(
        *assemble(
            [b1m, b1p, kv_near, k_m, k_p],
            [
                (
                    (3 * HALF, WIDE),
                    [
                        rows_piece(0, HALF, (0, 0)),
                        (HALF, 0, HALF, WIDE, [(2, 0, WIDE), (3, 0, 0)]),
                        (2 * HALF, 0, HALF, WIDE, [(2, HALF, WIDE)]),
                    ],
                ),
                (
                    (3 * HALF, WIDE),
                    [
                        rows_piece(0, HALF, (1, HALF)),
                        (HALF, 0, HALF, WIDE, [(2, 0, 2 * WIDE)]),
                        (2 * HALF, 0, HALF, WIDE, [(2, HALF, 2 * WIDE), (4, 0, 0)]),
                    ],
                ),
            ],
        ),
        "first",
    )
    kv_head = place * (w_query.shape[1] // HD) // (HEADS // KVH)
    cache_head = lax.dynamic_slice_in_dim(cache, kv_head * HD, HD, 3)
    z_one = hop(cache_head, "z_one", 1)
    part = query_part(
        [((0, 0), [(0, 0, 0, WIDE)]), ((1, 0), [(1, 0, 0, WIDE)]), ((3, 0), [(2, 0, 0, WIDE)])],
        [tokens, b1p, b1m],
        order,
        gains,
        w_query,
        None,
    )
    pool = jnp.stack([cache_head, z_one])
    b3m, b3p, b2m, b2p, pool, *part = bar((*s3, *s2, pool, *part))
    (to_next,) = assemble(
        [b3m, b3p, kv_near, b2m],
        [
            (
                (5 * HALF + HALF // 4, WIDE),
                [rows_piece(0, HALF, (0, 0)), rows_piece(HALF, HALF, (1, 0))]
                + [rows_piece(WIDE + n * HALF, HALF, (3, n * WIDE)) for n in range(3)]
                + packed(5 * HALF, HALF, (2, 0, 2 * HD), (0, HALF, 2 * HD), (1, HALF, 2 * HD)),
            )
        ],
    )
    (to_last,) = assemble(
        [b3m, b3p, kv_near, b2p],
        [
            (
                (5 * HALF + HALF // 4, WIDE),
                [rows_piece(0, HALF, (0, 0)), rows_piece(HALF, HALF, (1, 0))]
                + [rows_piece(WIDE + n * HALF, HALF, (3, n * WIDE + HALF)) for n in range(3)]
                + packed(5 * HALF, HALF, (2, HALF, 2 * HD), (0, WIDE, 2 * HD), (1, WIDE, 2 * HD)),
            )
        ],
    )
    s5 = both(to_next, to_last, "second")
    (ksum,) = assemble(
        [kv_near, b3m, b3p],
        [((WIDE, WIDE), [(0, 0, WIDE, WIDE, [(0, 0, 0), (1, HALF, 0), (2, HALF, 0)])])],
    )
    z_two, near_twin = hop(pool, "z_two", 1), hop(pool, "core", 1)
    my_lengths = lax.dynamic_slice_in_dim(lengths, group * branch_count, branch_count, 0)
    my_parents = lax.dynamic_slice_in_dim(parents, group * branch_count, branch_count, 0)
    owner = my_parents // 16
    owner_z, owner_core = owner // 2, owner % 2
    across = z + 1 - 2 * (z % 2)
    partner = jnp.where(owner_core == 0, across, 3 - z)
    slot = jnp.where(
        owner_z == z, 0, jnp.where(owner_z == partner, 1, jnp.where(owner_z == (z + 2) % 4, 3, 2))
    )
    codes = jnp.where(owner_core == core, 0, 64) + slot * 16 + my_parents % 16

    positions = jnp.repeat(my_lengths, PB) * PB + jnp.tile(
        jnp.arange(PB, dtype=jnp.int32), branch_count
    )
    halfway = HD // 2
    frequency = jnp.exp(jnp.arange(halfway, dtype=F32) * (-2.0 * math.log(1000000.0) / HD))
    angles = positions.astype(F32)[:, None] * frequency[None, :]
    cosine, sine = jnp.cos(angles), jnp.sin(angles)
    cosine = jnp.concatenate([cosine, cosine], axis=1)
    sine = jnp.concatenate([-sine, sine], axis=1)

    part = query_part(
        [
            ((2, 0), [(0, 0, 0, HALF), (1, 0, HALF, HALF)]),
            ((0, 1), [(2, 0, 0, WIDE)]),
            ((1, 1), [(2, WIDE, 0, WIDE)]),
            ((3, 1), [(2, 2 * WIDE, 0, WIDE)]),
            ((0, 3), [(3, 0, 0, WIDE)]),
            ((1, 3), [(3, WIDE, 0, WIDE)]),
            ((3, 3), [(3, 2 * WIDE, 0, WIDE)]),
        ],
        [b3m, b3p, b2p, b2m],
        order,
        gains,
        w_query,
        part,
    )
    b5m, b5p, z_two, near_twin, cosine, sine, ksum, codes, *part = bar(
        (*s5, z_two, near_twin, cosine, sine, ksum, codes, *part)
    )
    quarter = HALF // 4
    s7 = both(
        *assemble(
            [b5m, b5p, ksum],
            [
                (
                    (HALF + WIDE // 4, WIDE),
                    [rows_piece(0, HALF, (0, 0))]
                    + [
                        piece
                        for k in range(4)
                        for piece in [
                            (
                                HALF,
                                k * HD,
                                2 * quarter,
                                HD,
                                [(2, k * 2 * quarter, HD)],
                            )
                        ]
                        if k >= 2
                    ]
                    + [
                        (
                            HALF + t * quarter,
                            k * HD,
                            quarter,
                            HD,
                            [(2, (2 * k + t) * quarter, HD), (0, 5 * HALF, (2 * k + t) * HD)],
                        )
                        for k in range(2)
                        for t in range(2)
                    ],
                ),
                (
                    (HALF + WIDE // 4, WIDE),
                    [rows_piece(0, HALF, (1, HALF))]
                    + [
                        (HALF, k * HD, 2 * quarter, HD, [(2, k * 2 * quarter, 3 * HD)])
                        for k in range(2)
                    ]
                    + [
                        (
                            HALF + t * quarter,
                            k * HD,
                            quarter,
                            HD,
                            [(2, (2 * k + t) * quarter, 3 * HD), (1, 5 * HALF, (2 * k + t - 4) * HD)],
                        )
                        for k in range(2, 4)
                        for t in range(2)
                    ],
                ),
            ],
        ),
        "second",
    )
    far_twin = hop(z_two, "core", 1)
    pools = [
        pltpu.with_memory_space_constraint(a, pltpu.HBM) for a in (pool, z_two, near_twin, far_twin)
    ]
    prefix = gather_blocks(pools, codes)
    part = query_part(
        [
            ((2, 1), [(0, 0, 0, WIDE)]),
            ((2, 3), [(1, 0, 0, WIDE)]),
            ((0, 2), [(1, WIDE, 0, HALF), (0, WIDE, HALF, HALF)]),
            ((1, 2), [(1, WIDE + HALF, 0, HALF), (0, WIDE + HALF, HALF, HALF)]),
            ((3, 2), [(1, 2 * WIDE, 0, HALF), (0, 2 * WIDE, HALF, HALF)]),
        ],
        [b5p, b5m],
        order,
        gains,
        w_query,
        part,
    )
    b7m, b7p, prefix, *part = bar((*s7, prefix, *part))
    (mine,) = assemble(
        [ksum, b7m, b7p],
        [
            (
                (WIDE, HD),
                [
                    (k * 128, 0, 128, HD, [(0, k * 128, 0), (1, HALF, k * HD), (2, HALF, k * HD)])
                    for k in range(4)
                ],
            )
        ],
    )
    other = hop(mine, "twin", 1)
    part = query_part(
        [
            ((2, 2), [(0, 0, 0, HALF), (1, 0, HALF, HALF)]),
        ],
        [b7m, b7p],
        order,
        gains,
        w_query,
        part,
    )
    heads_out, far = middle(
        *part, order, (mine, other), (cosine, sine), prefix, my_lengths, w_output
    )

    ra = both(far[0, :HALF], far[0, HALF:], "second")
    rb = both(
        stack_rows(far[1, :HALF], far[2, :HALF], far[3, :HALF]),
        stack_rows(far[1, HALF:], far[2, HALF:], far[3, HALF:]),
        "second",
    )
    spots = [(2, 1), (2, 3), (1, 1), (3, 1), (1, 3), (3, 3)]
    rest = output_part(heads_out, w_output, order, spots)
    ra_m, ra_p, rest = bar((*ra, rest))
    q21, q23, q11, q31, q13, q33 = [rest[n] for n in range(6)]
    rc = both(
        stack_rows(plus(q21[:HALF], ra_m), q21[HALF:]),
        stack_rows(q23[:HALF], plus(q23[HALF:], ra_p)),
        "second",
    )
    rb_m, rb_p = bar(rb)
    rd = both(
        stack_rows(
            plus(q11[:HALF], rb_m[:HALF]), q11[HALF:], plus(q31[:HALF], rb_m[HALF:WIDE]), q31[HALF:]
        ),
        stack_rows(
            q13[:HALF], plus(q13[HALF:], rb_p[:HALF]), q33[:HALF], plus(q33[HALF:], rb_p[HALF:WIDE])
        ),
        "second",
    )
    spots = [(2, 0), (0, 1), (0, 3), (1, 0), (3, 0), (0, 0)]
    heads_late, rb_m = bar((heads_out, rb_m))
    rest = output_part(heads_late, w_output, order, spots)
    rc_m, rc_p, rest = bar((*rc, rest))
    q20, q01, q03, q10, q30, q00 = [rest[n] for n in range(6)]
    sum2 = plus(q20, rc_m, rc_p)
    re = both(sum2[:HALF], sum2[HALF:], "first")
    re_m, re_p, rb_m, rb_p = bar((*re, rb_m, rb_p))
    rf = both(
        stack_rows(plus(q01[:HALF], rb_m[WIDE:]), q01[HALF:]),
        stack_rows(q03[:HALF], plus(q03[HALF:], rb_p[WIDE:])),
        "second",
    )
    rd_m, rd_p = bar(rd)
    sum1 = stack_rows(
        plus(q10[:HALF], rd_m[:HALF], rd_p[:HALF], re_m), plus(q10[HALF:], rd_m[HALF:WIDE], rd_p[HALF:WIDE])
    )
    sum3 = stack_rows(
        plus(q30[:HALF], rd_m[WIDE : WIDE + HALF], rd_p[WIDE : WIDE + HALF]),
        plus(q30[HALF:], rd_m[WIDE + HALF :], rd_p[WIDE + HALF :], re_p),
    )
    rg = both(sum1, sum3, "first")
    return plus(q00, *rf, *rg)


def solution(mesh):
    return jax.shard_map(
        local,
        mesh=mesh,
        in_specs=(
            P("branch", "tensor"),
            P(),
            P(None, "tensor"),
            P(None, "tensor", None),
            P("tensor", None),
            P(None, "branch", None, None),
            P(),
            P(),
        ),
        out_specs=P("branch", "tensor"),
        check_vma=False,
    )
```

```python
import math

import jax
import jax.numpy as jnp
from jax import lax
from jax.experimental import pallas as pl
from jax.experimental.pallas import tpu as pltpu
from jax.sharding import PartitionSpec as P

HEADS = 64
KVH = 8
HD = 128
PB = 64
PDEPTH = 4
HALF = 256
AXES = ("branch", "tensor")
F32 = jnp.float32
BF16 = jnp.bfloat16
MIB = 1024 * 1024


def pairs(move):
    table = []
    for z in range(4):
        for c in range(2):
            for x in range(4):
                for y in range(4):
                    z2, c2, x2, y2 = move(z, c, x, y)
                    target = ((z2 % 4) * 2 + c2 % 2) * 16 + (x2 % 4) * 4 + y2 % 4
                    table.append(((z * 2 + c) * 16 + x * 4 + y, target))
    return table


HOPS = {}
for step in (1, -1):
    HOPS["first", step] = pairs(
        lambda z, c, x, y, s=step: (z, c, x, y + s) if c == 0 else (z, c, x + s, y)
    )
    HOPS["second", step] = pairs(
        lambda z, c, x, y, s=step: (z, c, x + s, y) if c == 0 else (z, c, x, y + s)
    )
HOPS["twin", 1] = pairs(lambda z, c, x, y: (z, c, x, y ^ 1))
HOPS["z_one", 1] = pairs(lambda z, c, x, y: (z ^ 1 if c == 0 else 3 - z, c, x, y))
HOPS["z_two", 1] = pairs(lambda z, c, x, y: (3 - z if c == 0 else z ^ 1, c, x, y))
HOPS["core", 1] = pairs(lambda z, c, x, y: (z, c + 1, x, y))


def hop(value, axis, step):
    return lax.ppermute(value, AXES, HOPS[axis, step])


def both(forward, backward, axis):
    return hop(forward, axis, 1), hop(backward, axis, -1)


def stack_rows(*parts):
    return jnp.concatenate(parts, axis=0)


def plus(base, *terms):
    total = base.astype(F32)
    for term in terms:
        total = total + term.astype(F32)
    return total.astype(BF16)


def pack(block):
    quarter = block.shape[0] // 4
    return jnp.concatenate([block[k * quarter : (k + 1) * quarter] for k in range(4)], axis=1)


def unpack(block):
    return jnp.concatenate([block[:, k * HD : (k + 1) * HD] for k in range(4)], axis=0)


def params(mebibytes):
    return pltpu.CompilerParams(vmem_limit_bytes=mebibytes * MIB)


def estimate(flops, moved):
    return pl.CostEstimate(flops=flops, bytes_accessed=moved, transcendentals=0)


VMEM = pl.BlockSpec(memory_space=pltpu.VMEM)
SMEM = pl.BlockSpec(memory_space=pltpu.SMEM)
FIXED = pl.BlockSpec(memory_space=pltpu.HBM)
ANYWHERE = pl.BlockSpec(memory_space=pl.ANY)
GROUP = 2
CHUNK = 64
WIDE = 512


def in_vmem(arrays):
    return [pltpu.with_memory_space_constraint(a, pltpu.VMEM) for a in arrays]


def place_of(order_ref, i, j):
    return order_ref[i * 4 + j]


def assemble(arrays, outputs):
    n_arrays, n_outputs = len(arrays), len(outputs)
    needed, plans = {}, []
    for shape, pieces in outputs:
        direct, summed = [], []
        for piece in pieces:
            _, _, rows, columns, terms = piece
            whole = columns == shape[1] == arrays[terms[0][0]].shape[1]
            if len(terms) == 1 and whole:
                direct.append(piece)
                continue
            summed.append(piece)
            for a, r, _ in terms:
                low, high = needed.get(a, (r, r + rows))
                needed[a] = (min(low, r), max(high, r + rows))
        low = min([p[0] for p in summed], default=0)
        high = max([p[0] + p[2] for p in summed], default=0)
        plans.append((direct, summed, low, high))
    staged = sorted(needed)
    built = [n for n, plan in enumerate(plans) if plan[1]]
    n_copies = len(staged) + len(built) + sum(len(plan[0]) for plan in plans)

    def body(*refs):
        a_refs, o_refs = refs[:n_arrays], refs[n_arrays : n_arrays + n_outputs]
        stage = dict(zip(staged, refs[n_arrays + n_outputs :]))
        build = dict(zip(built, refs[n_arrays + n_outputs + len(staged) :]))
        sems = refs[-1]
        inward, outward = [], []
        for n, a in enumerate(staged):
            low, high = needed[a]
            inward.append(
                pltpu.make_async_copy(a_refs[a].at[pl.ds(low, high - low), :], stage[a], sems.at[n])
            )
        count = len(staged)
        for o_ref, (direct, _, _, _) in zip(o_refs, plans):
            for row, _, rows, _, terms in direct:
                source, start, _ = terms[0]
                outward.append(
                    pltpu.make_async_copy(
                        a_refs[source].at[pl.ds(start, rows), :], o_ref.at[pl.ds(row, rows), :], sems.at[count]
                    )
                )
                count += 1
        for copy in inward + outward:
            copy.start()
        for copy in inward:
            copy.wait()
        for n in built:
            _, summed, first, last = plans[n]
            for row, column, rows, columns, terms in summed:
                total = None
                for a, r, c in terms:
                    r -= needed[a][0]
                    part = stage[a][r : r + rows, c : c + columns]
                    if len(terms) > 1:
                        part = part.astype(F32)
                    total = part if total is None else total + part
                build[n][row - first : row - first + rows, column : column + columns] = total.astype(BF16)
            copy = pltpu.make_async_copy(build[n], o_refs[n].at[pl.ds(first, last - first), :], sems.at[count])
            copy.start()
            outward.append(copy)
            count += 1
        for copy in outward:
            copy.wait()

    scratch = [pltpu.VMEM((needed[a][1] - needed[a][0], arrays[a].shape[1]), BF16) for a in staged]
    scratch += [pltpu.VMEM((plans[n][3] - plans[n][2], outputs[n][0][1]), BF16) for n in built]
    return pl.pallas_call(
        body,
        out_shape=[jax.ShapeDtypeStruct(shape, BF16) for shape, _ in outputs],
        in_specs=[ANYWHERE] * n_arrays,
        out_specs=[ANYWHERE] * n_outputs,
        scratch_shapes=[*scratch, pltpu.SemaphoreType.DMA((n_copies,))],
        compiler_params=params(6),
        cost_estimate=estimate(0, 0),
        name="assemble",
    )(*arrays)


def rows_piece(row, rows, *terms):
    return (row, 0, rows, WIDE, [(a, r, 0) for a, r in terms])


def packed(row, rows, *terms):
    quarter = rows // 4
    pieces = []
    for k in range(4):
        places = [(a, start + k * quarter, column) for a, start, column in terms]
        pieces.append((row, k * HD, quarter, HD, places))
    return pieces


def kv_partial(tokens, gain, w_keyvalue, order, steps):
    spots = [(i, j) for i in steps for j in range(4)]
    count = len(spots)

    def body(order_ref, t_ref, g_ref, w_ref, *refs):
        o_refs, (weights, sems) = refs[:-2], refs[-2:]
        copies = []
        for n, (i, j) in enumerate(spots):
            target = place_of(order_ref, i, j)
            column = pl.multiple_of(lax.div(target, 2) * HD, HD)
            copies.append(
                pltpu.make_async_copy(
                    w_ref.at[lax.rem(target, 2), :, pl.ds(column, HD)],
                    weights.at[:, pl.ds(n * HD, HD)],
                    sems.at[n],
                )
            )
        for copy in copies:
            copy.start()
        own = g_ref[pl.ds(place_of(order_ref, 0, 0), 1), :]
        scaled = (t_ref[...].astype(F32) * own).astype(BF16)
        for copy in copies:
            copy.wait()
        for n, o_ref in enumerate(o_refs):
            o_ref[...] = jnp.dot(
                scaled, weights[:, n * WIDE : (n + 1) * WIDE], preferred_element_type=F32
            ).astype(BF16)

    return pl.pallas_call(
        body,
        out_shape=[jax.ShapeDtypeStruct((WIDE, WIDE), BF16)] * len(steps),
        in_specs=[SMEM, VMEM, VMEM, FIXED],
        out_specs=[VMEM] * len(steps),
        scratch_shapes=[
            pltpu.VMEM((WIDE, count * HD), BF16),
            pltpu.SemaphoreType.DMA((count,)),
        ],
        compiler_params=params(6),
        cost_estimate=estimate(0, 0),
        name="kv_partial",
    )(order, tokens, gain, w_keyvalue)


def query_part(blocks, arrays, order, gain, w_query, carry):
    count = len(blocks)
    n_arrays = len(arrays)
    first = carry is None

    def body(order_ref, *refs):
        a_refs = refs[:n_arrays]
        g_ref, w_ref = refs[n_arrays : n_arrays + 2]
        q_ref, s_ref, scaled, weights, sems = refs[-5:]
        places = [place_of(order_ref, *spot) for spot, _ in blocks]

        def fetch(n):
            return pltpu.make_async_copy(
                w_ref.at[pl.ds(pl.multiple_of(places[n] * WIDE, WIDE), WIDE), :],
                weights.at[n // GROUP % 2, pl.ds(n % GROUP * WIDE, WIDE), :],
                sems.at[n],
            )

        for n in range(min(count, 2 * GROUP)):
            fetch(n).start()
        s_ref[...] = jnp.zeros_like(s_ref) if first else refs[n_arrays + 3][...]
        for low in range(0, count, GROUP):
            members = range(low, min(low + GROUP, count))
            for n in members:
                own = g_ref[pl.ds(places[n], 1), :]
                lanes_at = pl.ds((n - low) * WIDE, WIDE)
                for which, start, target, size in blocks[n][1]:

                    @pl.loop(0, size // CHUNK)
                    def _(step, which=which, start=start, target=target, own=own, lanes_at=lanes_at):
                        row = pl.multiple_of(step * CHUNK, CHUNK)
                        values = a_refs[which][pl.ds(start + row, CHUNK), :].astype(F32)
                        squares = values * values
                        lanes = squares[:, :HD]
                        for k in range(1, WIDE // HD):
                            lanes = lanes + squares[:, k * HD : (k + 1) * HD]
                        s_ref[pl.ds(target + row, CHUNK), :] += lanes
                        scaled[pl.ds(target + row, CHUNK), lanes_at] = (values * own).astype(BF16)

            for n in members:
                fetch(n).wait()
            depth = len(members) * WIDE
            for half in range(2):
                rows = slice(half * HALF, (half + 1) * HALF)
                product = jnp.dot(
                    scaled[rows, :depth], weights[low // GROUP % 2, :depth, :], preferred_element_type=F32
                )
                if low:
                    q_ref[rows, :] += product
                else:
                    q_ref[rows, :] = product if first else refs[n_arrays + 2][rows, :] + product
            for n in range(low + 2 * GROUP, min(low + 3 * GROUP, count)):
                fetch(n).start()

    carried = [] if first else list(carry)
    return pl.pallas_call(
        body,
        out_shape=(
            jax.ShapeDtypeStruct((WIDE, WIDE), F32),
            jax.ShapeDtypeStruct((WIDE, HD), F32),
        ),
        in_specs=[SMEM] + [VMEM] * n_arrays + [VMEM, FIXED] + [VMEM] * len(carried),
        out_specs=(VMEM, VMEM),
        scratch_shapes=[
            pltpu.VMEM((WIDE, GROUP * WIDE), BF16),
            pltpu.VMEM((2, GROUP * WIDE, WIDE), BF16),
            pltpu.SemaphoreType.DMA((count,)),
        ],
        input_output_aliases={} if first else {n_arrays + 3: 0, n_arrays + 4: 1},
        compiler_params=params(8),
        cost_estimate=estimate(0, 0),
        name="query_part",
    )(order, *in_vmem(arrays), gain, w_query, *in_vmem(carried))


def in_hbm(arrays):
    return [pltpu.with_memory_space_constraint(a, pltpu.HBM) for a in arrays]


def cut_cache(cache, head):
    shape = (*cache.shape[:3], HD)

    def body(head_ref, c_ref, o_ref, sem):
        column = pl.multiple_of(head_ref[0] * HD, HD)
        copy = pltpu.make_async_copy(c_ref.at[:, :, :, pl.ds(column, HD)], o_ref, sem)
        copy.start()
        copy.wait()

    return pl.pallas_call(
        body,
        out_shape=pltpu.HBM(shape, BF16),
        in_specs=[SMEM, FIXED],
        out_specs=FIXED,
        scratch_shapes=[pltpu.SemaphoreType.DMA],
        compiler_params=params(2),
        cost_estimate=estimate(0, 0),
        name="cut_cache",
    )(head, *in_hbm([cache]))


def join_cache(parts):
    def body(one_ref, two_ref, o_ref, sems):
        copies = [
            pltpu.make_async_copy(ref, o_ref.at[n], sems.at[n])
            for n, ref in enumerate((one_ref, two_ref))
        ]
        for copy in copies:
            copy.start()
        for copy in copies:
            copy.wait()

    return pl.pallas_call(
        body,
        out_shape=pltpu.HBM((2, *parts[0].shape), BF16),
        in_specs=[FIXED, FIXED],
        out_specs=FIXED,
        scratch_shapes=[pltpu.SemaphoreType.DMA((2,))],
        compiler_params=params(2),
        cost_estimate=estimate(0, 0),
        name="join_cache",
    )(*in_hbm(parts))


def gather_blocks(pools, codes):
    branches = codes.shape[0]
    span = PDEPTH * PB + PB

    def body(code_ref, *refs):
        pool_refs, (o_ref, sems) = refs[:4], refs[4:]
        for b in range(branches):
            for d in range(PDEPTH):
                code = code_ref[b, d]
                slot, block = lax.rem(lax.div(code, 16), 2), lax.rem(code, 16)
                for which, source in enumerate(pool_refs):

                    @pl.when(lax.div(code, 32) == which)
                    def _(source=source):
                        pltpu.make_async_copy(
                            source.at[slot, :, block], o_ref.at[b, :, pl.ds(d * PB, PB), :], sems.at[b, d]
                        ).start()

        for b in range(branches):
            for d in range(PDEPTH):
                pltpu.make_async_copy(
                    pool_refs[0].at[0, :, 0], o_ref.at[b, :, pl.ds(d * PB, PB), :], sems.at[b, d]
                ).wait()

    return pl.pallas_call(
        body,
        out_shape=jax.ShapeDtypeStruct((branches, 2, span, HD), BF16),
        in_specs=[SMEM] + [ANYWHERE] * 4,
        out_specs=VMEM,
        scratch_shapes=[pltpu.SemaphoreType.DMA((branches, PDEPTH))],
        compiler_params=params(6),
        cost_estimate=estimate(0, 0),
        name="gather_blocks",
    )(codes, *pools)


def middle(query, squares, order, keyvalue, tables, prefix, lengths, w_output):
    branches = WIDE // PB
    heads = WIDE // HD
    span = PDEPTH * PB + PB
    scale = 1.0 / math.sqrt(HD)
    spots = [(2, 2), (1, 2), (3, 2), (0, 2)]

    def body(
        order_ref, len_ref, q_ref, s_ref, mine_ref, other_ref, cos_ref, sin_ref, prefix_ref, wo_ref,
        heads_ref, far_ref, kv_ref,
        wo, qb, wsems,
    ):
        copies = []
        for n, (i, j) in enumerate(spots):
            column = pl.multiple_of(place_of(order_ref, i, j) * WIDE, WIDE)
            copies.append(
                pltpu.make_async_copy(wo_ref.at[:, pl.ds(column, WIDE)], wo.at[n], wsems.at[n])
            )
        for copy in copies:
            copy.start()
        total = jnp.sum(s_ref[...], axis=1, keepdims=True)
        factor = lax.rsqrt(total * (1.0 / 8192.0) + 1e-06)
        cos_part = cos_ref[...] * factor
        sin_part = sin_ref[...] * factor

        def rope(v, cos_part, sin_part):
            return (v * cos_part + pltpu.roll(v, HD // 2, 1) * sin_part).astype(BF16)

        even = lax.rem(place_of(order_ref, 0, 0), 2) == 0
        mine, other = mine_ref[...].astype(F32), other_ref[...].astype(F32)
        new_keys = rope(jnp.where(even, mine, other), cos_part, sin_part)
        new_values = (jnp.where(even, other, mine) * factor).astype(BF16)
        for b in range(branches):
            kv_ref[b, 0, PDEPTH * PB :, :] = new_keys[b * PB : (b + 1) * PB]
            kv_ref[b, 1, PDEPTH * PB :, :] = new_values[b * PB : (b + 1) * PB]
        cos_part, sin_part = cos_part * scale, sin_part * scale
        for h in range(heads):
            qb[h] = rope(q_ref[:, h * HD : (h + 1) * HD], cos_part, sin_part)
        column = lax.broadcasted_iota(jnp.int32, (heads * PB, span), 1)
        within = lax.rem(lax.broadcasted_iota(jnp.int32, (heads * PB, span), 0), PB)
        own_seen = (column >= PDEPTH * PB) & (column - PDEPTH * PB <= within)
        for b in range(branches):
            queries = qb[:, b * PB : (b + 1) * PB, :].reshape(heads * PB, HD)
            scores = lax.dot_general(
                queries, kv_ref[b, 0], (((1,), (1,)), ((), ())), preferred_element_type=F32
            )
            seen = (column < len_ref[b] * PB) | own_seen
            scores = jnp.where(seen, scores, -1e30)
            highest = jnp.max(scores, axis=1, keepdims=True)
            expo = jnp.exp(scores - highest)
            inverse = 1.0 / jnp.sum(expo, axis=1, keepdims=True)
            mixed = jnp.dot(expo.astype(BF16), kv_ref[b, 1], preferred_element_type=F32)
            mixed = (mixed * inverse).astype(BF16)
            for h in range(heads):
                heads_ref[b * PB : (b + 1) * PB, h * HD : (h + 1) * HD] = mixed[
                    h * PB : (h + 1) * PB
                ]
        for n, copy in enumerate(copies):
            copy.wait()
            far_ref[n] = jnp.dot(heads_ref[...], wo[n], preferred_element_type=F32).astype(BF16)

    return pl.pallas_call(
        body,
        out_shape=(
            jax.ShapeDtypeStruct((WIDE, WIDE), BF16),
            jax.ShapeDtypeStruct((len(spots), WIDE, WIDE), BF16),
            jax.ShapeDtypeStruct(prefix.shape, BF16),
        ),
        in_specs=[SMEM] * 2 + [VMEM] * 7 + [FIXED],
        out_specs=(VMEM, VMEM, VMEM),
        scratch_shapes=[
            pltpu.VMEM((len(spots), WIDE, WIDE), BF16),
            pltpu.VMEM((heads, WIDE, HD), BF16),
            pltpu.SemaphoreType.DMA((len(spots),)),
        ],
        input_output_aliases={8: 2},
        compiler_params=params(8),
        cost_estimate=estimate(0, 0),
        name="middle",
    )(
        order, lengths, *in_vmem([query, squares, *keyvalue, *tables, prefix]), w_output
    )[:2]


def output_part(heads_out, w_output, order, spots):
    count = len(spots)

    def body(order_ref, h_ref, w_ref, o_ref, weights, sems):
        copies = []
        for n, (i, j) in enumerate(spots):
            column = pl.multiple_of(place_of(order_ref, i, j) * WIDE, WIDE)
            copies.append(
                pltpu.make_async_copy(w_ref.at[:, pl.ds(column, WIDE)], weights.at[n], sems.at[n])
            )
        for copy in copies:
            copy.start()
        for n, copy in enumerate(copies):
            copy.wait()
            o_ref[n] = jnp.dot(h_ref[...], weights[n], preferred_element_type=F32).astype(BF16)

    return pl.pallas_call(
        body,
        out_shape=jax.ShapeDtypeStruct((count, WIDE, WIDE), BF16),
        in_specs=[SMEM, VMEM, FIXED],
        out_specs=VMEM,
        scratch_shapes=[
            pltpu.VMEM((count, WIDE, WIDE), BF16),
            pltpu.SemaphoreType.DMA((count,)),
        ],
        compiler_params=params(6),
        cost_estimate=estimate(0, 0),
        name="output_part",
    )(order, heads_out, w_output)


def local(tokens, gain, w_query, w_keyvalue, w_output, cache, parents, lengths):
    bar = lax.optimization_barrier
    group = lax.axis_index("branch")
    place = lax.axis_index("tensor")
    x, y = place // 4, place % 4
    z, core = group // 2, group % 2
    row_count = tokens.shape[0]
    branch_count = row_count // PB

    count = jnp.arange(16, dtype=jnp.int32)
    i_step, j_step = count // 4, count % 4
    dx = jnp.where(core == 0, j_step, i_step)
    dy = jnp.where(core == 0, i_step, j_step)
    order = ((x + dx) % 4) * 4 + (y + dy) % 4
    gains = gain.astype(F32).reshape(16, WIDE)
    w_query, w_keyvalue, w_output = [
        pltpu.with_memory_space_constraint(w, pltpu.HBM) for w in (w_query, w_keyvalue, w_output)
    ]

    s1 = both(tokens, tokens, "first")
    kv_far, *kv = kv_partial(tokens, gains, w_keyvalue, order, (2, 0, 1, 3))
    k_far = both(kv_far[:HALF], kv_far[HALF:], "first")
    b1m, b1p, k_m, k_p, cache, kv_0, kv_1, kv_3 = bar((*s1, *k_far, cache, *kv))
    (near,) = assemble(
        [tokens, b1p, b1m],
        [((3 * WIDE, WIDE), [rows_piece(n * WIDE, WIDE, (n, 0)) for n in range(3)])],
    )
    s2 = both(near, near, "second")
    s3 = both(
        *assemble(
            [b1m, b1p, kv_1, kv_3, k_m, k_p],
            [
                (
                    (3 * HALF, WIDE),
                    [
                        rows_piece(0, HALF, (0, 0)),
                        rows_piece(HALF, HALF, (2, 0), (4, 0)),
                        rows_piece(2 * HALF, HALF, (2, HALF)),
                    ],
                ),
                (
                    (3 * HALF, WIDE),
                    [
                        rows_piece(0, HALF, (1, HALF)),
                        rows_piece(HALF, HALF, (3, 0)),
                        rows_piece(2 * HALF, HALF, (3, HALF), (5, 0)),
                    ],
                ),
            ],
        ),
        "first",
    )
    kv_head = place * (w_query.shape[1] // HD) // (HEADS // KVH)
    cache_head = cut_cache(cache, kv_head.reshape(1))
    z_one = hop(cache_head, "z_one", 1)
    part = query_part(
        [((0, 0), [(0, 0, 0, WIDE)]), ((1, 0), [(1, 0, 0, WIDE)]), ((3, 0), [(2, 0, 0, WIDE)])],
        [tokens, b1p, b1m],
        order,
        gains,
        w_query,
        None,
    )
    pool = join_cache([cache_head, z_one])
    b3m, b3p, b2m, b2p, pool, *part = bar((*s3, *s2, pool, *part))
    (to_next,) = assemble(
        [b3m, b3p, kv_0, b2m],
        [
            (
                (5 * HALF + HALF // 4, WIDE),
                [rows_piece(0, HALF, (0, 0)), rows_piece(HALF, HALF, (1, 0))]
                + [rows_piece(WIDE + n * HALF, HALF, (3, n * WIDE)) for n in range(3)]
                + packed(5 * HALF, HALF, (2, 0, 2 * HD), (0, HALF, 2 * HD), (1, HALF, 2 * HD)),
            )
        ],
    )
    (to_last,) = assemble(
        [b3m, b3p, kv_0, b2p],
        [
            (
                (5 * HALF + HALF // 4, WIDE),
                [rows_piece(0, HALF, (0, 0)), rows_piece(HALF, HALF, (1, 0))]
                + [rows_piece(WIDE + n * HALF, HALF, (3, n * WIDE + HALF)) for n in range(3)]
                + packed(5 * HALF, HALF, (2, HALF, 2 * HD), (0, WIDE, 2 * HD), (1, WIDE, 2 * HD)),
            )
        ],
    )
    s5 = both(to_next, to_last, "second")
    (ksum,) = assemble(
        [kv_0, b3m, b3p],
        [((WIDE, WIDE), [(0, 0, WIDE, WIDE, [(0, 0, 0), (1, HALF, 0), (2, HALF, 0)])])],
    )
    z_two, near_twin = hop(pool, "z_two", 1), hop(pool, "core", 1)
    my_lengths = lax.dynamic_slice_in_dim(lengths, group * branch_count, branch_count, 0)
    my_parents = lax.dynamic_slice_in_dim(parents, group * branch_count, branch_count, 0)
    owner = my_parents // 16
    owner_z, owner_core = owner // 2, owner % 2
    across = z + 1 - 2 * (z % 2)
    partner = jnp.where(owner_core == 0, across, 3 - z)
    slot = jnp.where(
        owner_z == z, 0, jnp.where(owner_z == partner, 1, jnp.where(owner_z == (z + 2) % 4, 3, 2))
    )
    codes = jnp.where(owner_core == core, 0, 64) + slot * 16 + my_parents % 16

    positions = jnp.repeat(my_lengths, PB) * PB + jnp.tile(
        jnp.arange(PB, dtype=jnp.int32), branch_count
    )
    halfway = HD // 2
    frequency = jnp.exp(jnp.arange(halfway, dtype=F32) * (-2.0 * math.log(1000000.0) / HD))
    angles = positions.astype(F32)[:, None] * frequency[None, :]
    cosine, sine = jnp.cos(angles), jnp.sin(angles)
    cosine = jnp.concatenate([cosine, cosine], axis=1)
    sine = jnp.concatenate([-sine, sine], axis=1)

    part = query_part(
        [
            ((2, 0), [(0, 0, 0, HALF), (1, 0, HALF, HALF)]),
            ((0, 1), [(2, 0, 0, WIDE)]),
            ((1, 1), [(2, WIDE, 0, WIDE)]),
            ((3, 1), [(2, 2 * WIDE, 0, WIDE)]),
            ((0, 3), [(3, 0, 0, WIDE)]),
            ((1, 3), [(3, WIDE, 0, WIDE)]),
            ((3, 3), [(3, 2 * WIDE, 0, WIDE)]),
        ],
        [b3m, b3p, b2p, b2m],
        order,
        gains,
        w_query,
        part,
    )
    b5m, b5p, z_two, near_twin, cosine, sine, ksum, codes, *part = bar(
        (*s5, z_two, near_twin, cosine, sine, ksum, codes, *part)
    )
    quarter = HALF // 4
    s7 = both(
        *assemble(
            [b5m, b5p, ksum],
            [
                (
                    (HALF + WIDE // 4, WIDE),
                    [rows_piece(0, HALF, (0, 0))]
                    + [
                        piece
                        for k in range(4)
                        for piece in [
                            (
                                HALF,
                                k * HD,
                                2 * quarter,
                                HD,
                                [(2, k * 2 * quarter, HD)],
                            )
                        ]
                        if k >= 2
                    ]
                    + [
                        (
                            HALF + t * quarter,
                            k * HD,
                            quarter,
                            HD,
                            [(2, (2 * k + t) * quarter, HD), (0, 5 * HALF, (2 * k + t) * HD)],
                        )
                        for k in range(2)
                        for t in range(2)
                    ],
                ),
                (
                    (HALF + WIDE // 4, WIDE),
                    [rows_piece(0, HALF, (1, HALF))]
                    + [
                        (HALF, k * HD, 2 * quarter, HD, [(2, k * 2 * quarter, 3 * HD)])
                        for k in range(2)
                    ]
                    + [
                        (
                            HALF + t * quarter,
                            k * HD,
                            quarter,
                            HD,
                            [(2, (2 * k + t) * quarter, 3 * HD), (1, 5 * HALF, (2 * k + t - 4) * HD)],
                        )
                        for k in range(2, 4)
                        for t in range(2)
                    ],
                ),
            ],
        ),
        "second",
    )
    far_twin = hop(z_two, "core", 1)
    pools = [
        pltpu.with_memory_space_constraint(a, pltpu.HBM) for a in (pool, z_two, near_twin, far_twin)
    ]
    prefix = gather_blocks(pools, codes)
    part = query_part(
        [
            ((2, 1), [(0, 0, 0, WIDE)]),
            ((2, 3), [(1, 0, 0, WIDE)]),
            ((0, 2), [(1, WIDE, 0, HALF), (0, WIDE, HALF, HALF)]),
            ((1, 2), [(1, WIDE + HALF, 0, HALF), (0, WIDE + HALF, HALF, HALF)]),
            ((3, 2), [(1, 2 * WIDE, 0, HALF), (0, 2 * WIDE, HALF, HALF)]),
        ],
        [b5p, b5m],
        order,
        gains,
        w_query,
        part,
    )
    b7m, b7p, prefix, *part = bar((*s7, prefix, *part))
    (mine,) = assemble(
        [ksum, b7m, b7p],
        [
            (
                (WIDE, HD),
                [
                    (k * 128, 0, 128, HD, [(0, k * 128, 0), (1, HALF, k * HD), (2, HALF, k * HD)])
                    for k in range(4)
                ],
            )
        ],
    )
    other = hop(mine, "twin", 1)
    part = query_part(
        [
            ((2, 2), [(0, 0, 0, HALF), (1, 0, HALF, HALF)]),
        ],
        [b7m, b7p],
        order,
        gains,
        w_query,
        part,
    )
    heads_out, far = middle(
        *part, order, (mine, other), (cosine, sine), prefix, my_lengths, w_output
    )

    ra = both(far[0, :HALF], far[0, HALF:], "second")
    rb = both(
        stack_rows(far[1, :HALF], far[2, :HALF], far[3, :HALF]),
        stack_rows(far[1, HALF:], far[2, HALF:], far[3, HALF:]),
        "second",
    )
    spots = [(2, 1), (2, 3), (1, 1), (3, 1), (1, 3), (3, 3)]
    rest = output_part(heads_out, w_output, order, spots)
    ra_m, ra_p, rest = bar((*ra, rest))
    q21, q23, q11, q31, q13, q33 = [rest[n] for n in range(6)]
    rc = both(
        stack_rows(plus(q21[:HALF], ra_m), q21[HALF:]),
        stack_rows(q23[:HALF], plus(q23[HALF:], ra_p)),
        "second",
    )
    rb_m, rb_p = bar(rb)
    rd = both(
        stack_rows(
            plus(q11[:HALF], rb_m[:HALF]), q11[HALF:], plus(q31[:HALF], rb_m[HALF:WIDE]), q31[HALF:]
        ),
        stack_rows(
            q13[:HALF], plus(q13[HALF:], rb_p[:HALF]), q33[:HALF], plus(q33[HALF:], rb_p[HALF:WIDE])
        ),
        "second",
    )
    spots = [(2, 0), (0, 1), (0, 3), (1, 0), (3, 0), (0, 0)]
    heads_late, rb_m = bar((heads_out, rb_m))
    rest = output_part(heads_late, w_output, order, spots)
    rc_m, rc_p, rest = bar((*rc, rest))
    q20, q01, q03, q10, q30, q00 = [rest[n] for n in range(6)]
    sum2 = plus(q20, rc_m, rc_p)
    re = both(sum2[:HALF], sum2[HALF:], "first")
    re_m, re_p, rb_m, rb_p = bar((*re, rb_m, rb_p))
    rf = both(
        stack_rows(plus(q01[:HALF], rb_m[WIDE:]), q01[HALF:]),
        stack_rows(q03[:HALF], plus(q03[HALF:], rb_p[WIDE:])),
        "second",
    )
    rd_m, rd_p = bar(rd)
    sum1 = stack_rows(
        plus(q10[:HALF], rd_m[:HALF], rd_p[:HALF], re_m), plus(q10[HALF:], rd_m[HALF:WIDE], rd_p[HALF:WIDE])
    )
    sum3 = stack_rows(
        plus(q30[:HALF], rd_m[WIDE : WIDE + HALF], rd_p[WIDE : WIDE + HALF]),
        plus(q30[HALF:], rd_m[WIDE + HALF :], rd_p[WIDE + HALF :], re_p),
    )
    rg = both(sum1, sum3, "first")
    return plus(q00, *rf, *rg)


def solution(mesh):
    return jax.shard_map(
        local,
        mesh=mesh,
        in_specs=(
            P("branch", "tensor"),
            P(),
            P(None, "tensor"),
            P(None, "tensor", None),
            P("tensor", None),
            P(None, "branch", None, None),
            P(),
            P(),
        ),
        out_specs=P("branch", "tensor"),
        check_vma=False,
    )
```

```python
import math

import jax
import jax.numpy as jnp
from jax import lax
from jax.experimental import pallas as pl
from jax.experimental.pallas import tpu as pltpu
from jax.sharding import PartitionSpec as P

HEADS = 64
KVH = 8
HD = 128
PB = 64
PDEPTH = 4
HALF = 256
AXES = ("branch", "tensor")
F32 = jnp.float32
BF16 = jnp.bfloat16
MIB = 1024 * 1024


def pairs(move):
    table = []
    for z in range(4):
        for c in range(2):
            for x in range(4):
                for y in range(4):
                    z2, c2, x2, y2 = move(z, c, x, y)
                    target = ((z2 % 4) * 2 + c2 % 2) * 16 + (x2 % 4) * 4 + y2 % 4
                    table.append(((z * 2 + c) * 16 + x * 4 + y, target))
    return table


HOPS = {}
for step in (1, -1):
    HOPS["first", step] = pairs(
        lambda z, c, x, y, s=step: (z, c, x, y + s) if c == 0 else (z, c, x + s, y)
    )
    HOPS["second", step] = pairs(
        lambda z, c, x, y, s=step: (z, c, x + s, y) if c == 0 else (z, c, x, y + s)
    )
HOPS["twin", 1] = pairs(lambda z, c, x, y: (z, c, x, y ^ 1))
HOPS["z_one", 1] = pairs(lambda z, c, x, y: (z ^ 1 if c == 0 else 3 - z, c, x, y))
HOPS["z_two", 1] = pairs(lambda z, c, x, y: (3 - z if c == 0 else z ^ 1, c, x, y))
HOPS["core", 1] = pairs(lambda z, c, x, y: (z, c + 1, x, y))


def hop(value, axis, step):
    return lax.ppermute(value, AXES, HOPS[axis, step])


def both(forward, backward, axis):
    return hop(forward, axis, 1), hop(backward, axis, -1)


def stack_rows(*parts):
    return jnp.concatenate(parts, axis=0)


def plus(base, *terms):
    total = base.astype(F32)
    for term in terms:
        total = total + term.astype(F32)
    return total.astype(BF16)


def pack(block):
    quarter = block.shape[0] // 4
    return jnp.concatenate([block[k * quarter : (k + 1) * quarter] for k in range(4)], axis=1)


def unpack(block):
    return jnp.concatenate([block[:, k * HD : (k + 1) * HD] for k in range(4)], axis=0)


def params(mebibytes):
    return pltpu.CompilerParams(vmem_limit_bytes=mebibytes * MIB)


def estimate(flops, moved):
    return pl.CostEstimate(flops=flops, bytes_accessed=moved, transcendentals=0)


VMEM = pl.BlockSpec(memory_space=pltpu.VMEM)
SMEM = pl.BlockSpec(memory_space=pltpu.SMEM)
FIXED = pl.BlockSpec(memory_space=pltpu.HBM)
ANYWHERE = pl.BlockSpec(memory_space=pl.ANY)
GROUP = 2
CHUNK = 64
WIDE = 512


def in_vmem(arrays):
    return [pltpu.with_memory_space_constraint(a, pltpu.VMEM) for a in arrays]


def place_of(order_ref, i, j):
    return order_ref[i * 4 + j]


def assemble(arrays, outputs):
    n_arrays, n_outputs = len(arrays), len(outputs)
    needed, plans = {}, []
    for shape, pieces in outputs:
        direct, summed = [], []
        for piece in pieces:
            _, _, rows, columns, terms = piece
            whole = columns == shape[1] == arrays[terms[0][0]].shape[1]
            if len(terms) == 1 and whole:
                direct.append(piece)
                continue
            summed.append(piece)
            for a, r, _ in terms:
                low, high = needed.get(a, (r, r + rows))
                needed[a] = (min(low, r), max(high, r + rows))
        plans.append((direct, summed))
    staged = sorted(needed)
    n_copies = len(staged) + sum(len(plan[0]) for plan in plans)

    def body(*refs):
        a_refs, o_refs = refs[:n_arrays], refs[n_arrays : n_arrays + n_outputs]
        stage = dict(zip(staged, refs[n_arrays + n_outputs :]))
        sems = refs[-1]
        inward, outward = [], []
        for n, a in enumerate(staged):
            low, high = needed[a]
            inward.append(
                pltpu.make_async_copy(a_refs[a].at[pl.ds(low, high - low), :], stage[a], sems.at[n])
            )
        count = len(staged)
        for o_ref, (direct, _) in zip(o_refs, plans):
            for row, _, rows, _, terms in direct:
                source, start, _ = terms[0]
                outward.append(
                    pltpu.make_async_copy(
                        a_refs[source].at[pl.ds(start, rows), :], o_ref.at[pl.ds(row, rows), :], sems.at[count]
                    )
                )
                count += 1
        for copy in inward + outward:
            copy.start()
        for copy in inward:
            copy.wait()
        for o_ref, (_, summed) in zip(o_refs, plans):
            for row, column, rows, columns, terms in summed:
                total = None
                for a, r, c in terms:
                    r -= needed[a][0]
                    part = stage[a][r : r + rows, c : c + columns]
                    if len(terms) > 1:
                        part = part.astype(F32)
                    total = part if total is None else total + part
                o_ref[row : row + rows, column : column + columns] = total.astype(BF16)
        for copy in outward:
            copy.wait()

    scratch = [pltpu.VMEM((needed[a][1] - needed[a][0], arrays[a].shape[1]), BF16) for a in staged]
    return pl.pallas_call(
        body,
        out_shape=[jax.ShapeDtypeStruct(shape, BF16) for shape, _ in outputs],
        in_specs=[ANYWHERE] * n_arrays,
        out_specs=[VMEM] * n_outputs,
        scratch_shapes=[*scratch, pltpu.SemaphoreType.DMA((n_copies,))],
        compiler_params=params(6),
        cost_estimate=estimate(0, 0),
        name="assemble",
    )(*arrays)


def rows_piece(row, rows, *terms):
    return (row, 0, rows, WIDE, [(a, r, 0) for a, r in terms])


def packed(row, rows, *terms):
    quarter = rows // 4
    pieces = []
    for k in range(4):
        places = [(a, start + k * quarter, column) for a, start, column in terms]
        pieces.append((row, k * HD, quarter, HD, places))
    return pieces


def kv_partial(tokens, gain, w_keyvalue, order, steps):
    spots = [(i, j) for i in steps for j in range(4)]
    count = len(spots)

    def body(order_ref, t_ref, g_ref, w_ref, *refs):
        o_refs, (weights, sems) = refs[:-2], refs[-2:]
        copies = []
        for n, (i, j) in enumerate(spots):
            target = place_of(order_ref, i, j)
            column = pl.multiple_of(lax.div(target, 2) * HD, HD)
            copies.append(
                pltpu.make_async_copy(
                    w_ref.at[lax.rem(target, 2), :, pl.ds(column, HD)],
                    weights.at[:, pl.ds(n * HD, HD)],
                    sems.at[n],
                )
            )
        for copy in copies:
            copy.start()
        own = g_ref[pl.ds(place_of(order_ref, 0, 0), 1), :]
        scaled = (t_ref[...].astype(F32) * own).astype(BF16)
        for copy in copies:
            copy.wait()
        for n, o_ref in enumerate(o_refs):
            o_ref[...] = jnp.dot(
                scaled, weights[:, n * WIDE : (n + 1) * WIDE], preferred_element_type=F32
            ).astype(BF16)

    return pl.pallas_call(
        body,
        out_shape=[jax.ShapeDtypeStruct((WIDE, WIDE), BF16)] * len(steps),
        in_specs=[SMEM, VMEM, VMEM, FIXED],
        out_specs=[VMEM] * len(steps),
        scratch_shapes=[
            pltpu.VMEM((WIDE, count * HD), BF16),
            pltpu.SemaphoreType.DMA((count,)),
        ],
        compiler_params=params(6),
        cost_estimate=estimate(0, 0),
        name="kv_partial",
    )(order, tokens, gain, w_keyvalue)


def query_part(blocks, arrays, order, gain, w_query, carry):
    count = len(blocks)
    n_arrays = len(arrays)
    first = carry is None

    def body(order_ref, *refs):
        a_refs = refs[:n_arrays]
        g_ref, w_ref = refs[n_arrays : n_arrays + 2]
        q_ref, s_ref, scaled, weights, sems = refs[-5:]
        places = [place_of(order_ref, *spot) for spot, _ in blocks]

        def fetch(n):
            return pltpu.make_async_copy(
                w_ref.at[pl.ds(pl.multiple_of(places[n] * WIDE, WIDE), WIDE), :],
                weights.at[n // GROUP % 2, pl.ds(n % GROUP * WIDE, WIDE), :],
                sems.at[n],
            )

        for n in range(min(count, 2 * GROUP)):
            fetch(n).start()
        s_ref[...] = jnp.zeros_like(s_ref) if first else refs[n_arrays + 3][...]
        for low in range(0, count, GROUP):
            members = range(low, min(low + GROUP, count))
            for n in members:
                own = g_ref[pl.ds(places[n], 1), :]
                lanes_at = pl.ds((n - low) * WIDE, WIDE)
                for which, start, target, size in blocks[n][1]:

                    @pl.loop(0, size // CHUNK)
                    def _(step, which=which, start=start, target=target, own=own, lanes_at=lanes_at):
                        row = pl.multiple_of(step * CHUNK, CHUNK)
                        values = a_refs[which][pl.ds(start + row, CHUNK), :].astype(F32)
                        squares = values * values
                        lanes = squares[:, :HD]
                        for k in range(1, WIDE // HD):
                            lanes = lanes + squares[:, k * HD : (k + 1) * HD]
                        s_ref[pl.ds(target + row, CHUNK), :] += lanes
                        scaled[pl.ds(target + row, CHUNK), lanes_at] = (values * own).astype(BF16)

            for n in members:
                fetch(n).wait()
            depth = len(members) * WIDE
            for half in range(2):
                rows = slice(half * HALF, (half + 1) * HALF)
                product = jnp.dot(
                    scaled[rows, :depth], weights[low // GROUP % 2, :depth, :], preferred_element_type=F32
                )
                if low:
                    q_ref[rows, :] += product
                else:
                    q_ref[rows, :] = product if first else refs[n_arrays + 2][rows, :] + product
            for n in range(low + 2 * GROUP, min(low + 3 * GROUP, count)):
                fetch(n).start()

    carried = [] if first else list(carry)
    return pl.pallas_call(
        body,
        out_shape=(
            jax.ShapeDtypeStruct((WIDE, WIDE), F32),
            jax.ShapeDtypeStruct((WIDE, HD), F32),
        ),
        in_specs=[SMEM] + [VMEM] * n_arrays + [VMEM, FIXED] + [VMEM] * len(carried),
        out_specs=(VMEM, VMEM),
        scratch_shapes=[
            pltpu.VMEM((WIDE, GROUP * WIDE), BF16),
            pltpu.VMEM((2, GROUP * WIDE, WIDE), BF16),
            pltpu.SemaphoreType.DMA((count,)),
        ],
        input_output_aliases={} if first else {n_arrays + 3: 0, n_arrays + 4: 1},
        compiler_params=params(8),
        cost_estimate=estimate(0, 0),
        name="query_part",
    )(order, *in_vmem(arrays), gain, w_query, *in_vmem(carried))


def gather_blocks(pools, codes):
    branches = codes.shape[0]
    span = PDEPTH * PB + PB

    def body(code_ref, *refs):
        pool_refs, (o_ref, sems) = refs[:4], refs[4:]
        for b in range(branches):
            for d in range(PDEPTH):
                code = code_ref[b, d]
                slot, block = lax.rem(lax.div(code, 16), 2), lax.rem(code, 16)
                for which, source in enumerate(pool_refs):

                    @pl.when(lax.div(code, 32) == which)
                    def _(source=source):
                        pltpu.make_async_copy(
                            source.at[slot, :, block], o_ref.at[b, :, pl.ds(d * PB, PB), :], sems.at[b, d]
                        ).start()

        for b in range(branches):
            for d in range(PDEPTH):
                pltpu.make_async_copy(
                    pool_refs[0].at[0, :, 0], o_ref.at[b, :, pl.ds(d * PB, PB), :], sems.at[b, d]
                ).wait()

    return pl.pallas_call(
        body,
        out_shape=jax.ShapeDtypeStruct((branches, 2, span, HD), BF16),
        in_specs=[SMEM] + [ANYWHERE] * 4,
        out_specs=VMEM,
        scratch_shapes=[pltpu.SemaphoreType.DMA((branches, PDEPTH))],
        compiler_params=params(6),
        cost_estimate=estimate(0, 0),
        name="gather_blocks",
    )(codes, *pools)


def middle(query, squares, order, keyvalue, tables, prefix, lengths, w_output):
    branches = WIDE // PB
    heads = WIDE // HD
    span = PDEPTH * PB + PB
    scale = 1.0 / math.sqrt(HD)
    spots = [(2, 2), (1, 2), (3, 2), (0, 2)]

    def body(
        order_ref, len_ref, q_ref, s_ref, mine_ref, other_ref, cos_ref, sin_ref, prefix_ref, wo_ref,
        heads_ref, far_ref, kv_ref,
        wo, qb, wsems,
    ):
        copies = []
        for n, (i, j) in enumerate(spots):
            column = pl.multiple_of(place_of(order_ref, i, j) * WIDE, WIDE)
            copies.append(
                pltpu.make_async_copy(wo_ref.at[:, pl.ds(column, WIDE)], wo.at[n], wsems.at[n])
            )
        for copy in copies:
            copy.start()
        total = jnp.sum(s_ref[...], axis=1, keepdims=True)
        factor = lax.rsqrt(total * (1.0 / 8192.0) + 1e-06)
        cos_part = cos_ref[...] * factor
        sin_part = sin_ref[...] * factor

        def rope(v, cos_part, sin_part):
            return (v * cos_part + pltpu.roll(v, HD // 2, 1) * sin_part).astype(BF16)

        even = lax.rem(place_of(order_ref, 0, 0), 2) == 0
        mine, other = mine_ref[...].astype(F32), other_ref[...].astype(F32)
        new_keys = rope(jnp.where(even, mine, other), cos_part, sin_part)
        new_values = (jnp.where(even, other, mine) * factor).astype(BF16)
        for b in range(branches):
            kv_ref[b, 0, PDEPTH * PB :, :] = new_keys[b * PB : (b + 1) * PB]
            kv_ref[b, 1, PDEPTH * PB :, :] = new_values[b * PB : (b + 1) * PB]
        cos_part, sin_part = cos_part * scale, sin_part * scale
        for h in range(heads):
            qb[h] = rope(q_ref[:, h * HD : (h + 1) * HD], cos_part, sin_part)
        column = lax.broadcasted_iota(jnp.int32, (heads * PB, span), 1)
        within = lax.rem(lax.broadcasted_iota(jnp.int32, (heads * PB, span), 0), PB)
        own_seen = (column >= PDEPTH * PB) & (column - PDEPTH * PB <= within)
        for b in range(branches):
            queries = qb[:, b * PB : (b + 1) * PB, :].reshape(heads * PB, HD)
            scores = lax.dot_general(
                queries, kv_ref[b, 0], (((1,), (1,)), ((), ())), preferred_element_type=F32
            )
            seen = (column < len_ref[b] * PB) | own_seen
            scores = jnp.where(seen, scores, -1e30)
            highest = jnp.max(scores, axis=1, keepdims=True)
            expo = jnp.exp(scores - highest)
            inverse = 1.0 / jnp.sum(expo, axis=1, keepdims=True)
            mixed = jnp.dot(expo.astype(BF16), kv_ref[b, 1], preferred_element_type=F32)
            mixed = (mixed * inverse).astype(BF16)
            for h in range(heads):
                heads_ref[b * PB : (b + 1) * PB, h * HD : (h + 1) * HD] = mixed[
                    h * PB : (h + 1) * PB
                ]
        for n, copy in enumerate(copies):
            copy.wait()
            far_ref[n] = jnp.dot(heads_ref[...], wo[n], preferred_element_type=F32).astype(BF16)

    return pl.pallas_call(
        body,
        out_shape=(
            jax.ShapeDtypeStruct((WIDE, WIDE), BF16),
            jax.ShapeDtypeStruct((len(spots), WIDE, WIDE), BF16),
            jax.ShapeDtypeStruct(prefix.shape, BF16),
        ),
        in_specs=[SMEM] * 2 + [VMEM] * 7 + [FIXED],
        out_specs=(VMEM, VMEM, VMEM),
        scratch_shapes=[
            pltpu.VMEM((len(spots), WIDE, WIDE), BF16),
            pltpu.VMEM((heads, WIDE, HD), BF16),
            pltpu.SemaphoreType.DMA((len(spots),)),
        ],
        input_output_aliases={8: 2},
        compiler_params=params(8),
        cost_estimate=estimate(0, 0),
        name="middle",
    )(
        order, lengths, *in_vmem([query, squares, *keyvalue, *tables, prefix]), w_output
    )[:2]


def output_part(heads_out, w_output, order, spots):
    count = len(spots)

    def body(order_ref, h_ref, w_ref, o_ref, weights, sems):
        copies = []
        for n, (i, j) in enumerate(spots):
            column = pl.multiple_of(place_of(order_ref, i, j) * WIDE, WIDE)
            copies.append(
                pltpu.make_async_copy(w_ref.at[:, pl.ds(column, WIDE)], weights.at[n], sems.at[n])
            )
        for copy in copies:
            copy.start()
        for n, copy in enumerate(copies):
            copy.wait()
            o_ref[n] = jnp.dot(h_ref[...], weights[n], preferred_element_type=F32).astype(BF16)

    return pl.pallas_call(
        body,
        out_shape=jax.ShapeDtypeStruct((count, WIDE, WIDE), BF16),
        in_specs=[SMEM, VMEM, FIXED],
        out_specs=VMEM,
        scratch_shapes=[
            pltpu.VMEM((count, WIDE, WIDE), BF16),
            pltpu.SemaphoreType.DMA((count,)),
        ],
        compiler_params=params(6),
        cost_estimate=estimate(0, 0),
        name="output_part",
    )(order, heads_out, w_output)


def local(tokens, gain, w_query, w_keyvalue, w_output, cache, parents, lengths):
    bar = lax.optimization_barrier
    group = lax.axis_index("branch")
    place = lax.axis_index("tensor")
    x, y = place // 4, place % 4
    z, core = group // 2, group % 2
    row_count = tokens.shape[0]
    branch_count = row_count // PB

    count = jnp.arange(16, dtype=jnp.int32)
    i_step, j_step = count // 4, count % 4
    dx = jnp.where(core == 0, j_step, i_step)
    dy = jnp.where(core == 0, i_step, j_step)
    order = ((x + dx) % 4) * 4 + (y + dy) % 4
    gains = gain.astype(F32).reshape(16, WIDE)
    w_query, w_keyvalue, w_output = [
        pltpu.with_memory_space_constraint(w, pltpu.HBM) for w in (w_query, w_keyvalue, w_output)
    ]

    s1 = both(tokens, tokens, "first")
    kv_far, *kv = kv_partial(tokens, gains, w_keyvalue, order, (2, 0, 1, 3))
    k_far = both(kv_far[:HALF], kv_far[HALF:], "first")
    b1m, b1p, k_m, k_p, cache, kv_0, kv_1, kv_3 = bar((*s1, *k_far, cache, *kv))
    (near,) = assemble(
        [tokens, b1p, b1m],
        [((3 * WIDE, WIDE), [rows_piece(n * WIDE, WIDE, (n, 0)) for n in range(3)])],
    )
    s2 = both(near, near, "second")
    s3 = both(
        *assemble(
            [b1m, b1p, kv_1, kv_3, k_m, k_p],
            [
                (
                    (3 * HALF, WIDE),
                    [
                        rows_piece(0, HALF, (0, 0)),
                        rows_piece(HALF, HALF, (2, 0), (4, 0)),
                        rows_piece(2 * HALF, HALF, (2, HALF)),
                    ],
                ),
                (
                    (3 * HALF, WIDE),
                    [
                        rows_piece(0, HALF, (1, HALF)),
                        rows_piece(HALF, HALF, (3, 0)),
                        rows_piece(2 * HALF, HALF, (3, HALF), (5, 0)),
                    ],
                ),
            ],
        ),
        "first",
    )
    kv_head = place * (w_query.shape[1] // HD) // (HEADS // KVH)
    cache_head = lax.dynamic_slice_in_dim(cache, kv_head * HD, HD, 3)
    z_one = hop(cache_head, "z_one", 1)
    part = query_part(
        [((0, 0), [(0, 0, 0, WIDE)]), ((1, 0), [(1, 0, 0, WIDE)]), ((3, 0), [(2, 0, 0, WIDE)])],
        [tokens, b1p, b1m],
        order,
        gains,
        w_query,
        None,
    )
    pool = jnp.stack([cache_head, z_one])
    b3m, b3p, b2m, b2p, pool, *part = bar((*s3, *s2, pool, *part))
    (to_next,) = assemble(
        [b3m, b3p, kv_0, b2m],
        [
            (
                (5 * HALF + HALF // 4, WIDE),
                [rows_piece(0, HALF, (0, 0)), rows_piece(HALF, HALF, (1, 0))]
                + [rows_piece(WIDE + n * HALF, HALF, (3, n * WIDE)) for n in range(3)]
                + packed(5 * HALF, HALF, (2, 0, 2 * HD), (0, HALF, 2 * HD), (1, HALF, 2 * HD)),
            )
        ],
    )
    (to_last,) = assemble(
        [b3m, b3p, kv_0, b2p],
        [
            (
                (5 * HALF + HALF // 4, WIDE),
                [rows_piece(0, HALF, (0, 0)), rows_piece(HALF, HALF, (1, 0))]
                + [rows_piece(WIDE + n * HALF, HALF, (3, n * WIDE + HALF)) for n in range(3)]
                + packed(5 * HALF, HALF, (2, HALF, 2 * HD), (0, WIDE, 2 * HD), (1, WIDE, 2 * HD)),
            )
        ],
    )
    s5 = both(to_next, to_last, "second")
    (ksum,) = assemble(
        [kv_0, b3m, b3p],
        [((WIDE, WIDE), [(0, 0, WIDE, WIDE, [(0, 0, 0), (1, HALF, 0), (2, HALF, 0)])])],
    )
    z_two, near_twin = hop(pool, "z_two", 1), hop(pool, "core", 1)
    my_lengths = lax.dynamic_slice_in_dim(lengths, group * branch_count, branch_count, 0)
    my_parents = lax.dynamic_slice_in_dim(parents, group * branch_count, branch_count, 0)
    owner = my_parents // 16
    owner_z, owner_core = owner // 2, owner % 2
    across = z + 1 - 2 * (z % 2)
    partner = jnp.where(owner_core == 0, across, 3 - z)
    slot = jnp.where(
        owner_z == z, 0, jnp.where(owner_z == partner, 1, jnp.where(owner_z == (z + 2) % 4, 3, 2))
    )
    codes = jnp.where(owner_core == core, 0, 64) + slot * 16 + my_parents % 16

    positions = jnp.repeat(my_lengths, PB) * PB + jnp.tile(
        jnp.arange(PB, dtype=jnp.int32), branch_count
    )
    halfway = HD // 2
    frequency = jnp.exp(jnp.arange(halfway, dtype=F32) * (-2.0 * math.log(1000000.0) / HD))
    angles = positions.astype(F32)[:, None] * frequency[None, :]
    cosine, sine = jnp.cos(angles), jnp.sin(angles)
    cosine = jnp.concatenate([cosine, cosine], axis=1)
    sine = jnp.concatenate([-sine, sine], axis=1)

    part = query_part(
        [
            ((2, 0), [(0, 0, 0, HALF), (1, 0, HALF, HALF)]),
            ((0, 1), [(2, 0, 0, WIDE)]),
            ((1, 1), [(2, WIDE, 0, WIDE)]),
            ((3, 1), [(2, 2 * WIDE, 0, WIDE)]),
            ((0, 3), [(3, 0, 0, WIDE)]),
            ((1, 3), [(3, WIDE, 0, WIDE)]),
            ((3, 3), [(3, 2 * WIDE, 0, WIDE)]),
        ],
        [b3m, b3p, b2p, b2m],
        order,
        gains,
        w_query,
        part,
    )
    b5m, b5p, z_two, near_twin, cosine, sine, ksum, codes, *part = bar(
        (*s5, z_two, near_twin, cosine, sine, ksum, codes, *part)
    )
    quarter = HALF // 4
    s7 = both(
        *assemble(
            [b5m, b5p, ksum],
            [
                (
                    (HALF + WIDE // 4, WIDE),
                    [rows_piece(0, HALF, (0, 0))]
                    + [
                        piece
                        for k in range(4)
                        for piece in [
                            (
                                HALF,
                                k * HD,
                                2 * quarter,
                                HD,
                                [(2, k * 2 * quarter, HD)],
                            )
                        ]
                        if k >= 2
                    ]
                    + [
                        (
                            HALF + t * quarter,
                            k * HD,
                            quarter,
                            HD,
                            [(2, (2 * k + t) * quarter, HD), (0, 5 * HALF, (2 * k + t) * HD)],
                        )
                        for k in range(2)
                        for t in range(2)
                    ],
                ),
                (
                    (HALF + WIDE // 4, WIDE),
                    [rows_piece(0, HALF, (1, HALF))]
                    + [
                        (HALF, k * HD, 2 * quarter, HD, [(2, k * 2 * quarter, 3 * HD)])
                        for k in range(2)
                    ]
                    + [
                        (
                            HALF + t * quarter,
                            k * HD,
                            quarter,
                            HD,
                            [(2, (2 * k + t) * quarter, 3 * HD), (1, 5 * HALF, (2 * k + t - 4) * HD)],
                        )
                        for k in range(2, 4)
                        for t in range(2)
                    ],
                ),
            ],
        ),
        "second",
    )
    far_twin = hop(z_two, "core", 1)
    pools = [
        pltpu.with_memory_space_constraint(a, pltpu.HBM) for a in (pool, z_two, near_twin, far_twin)
    ]
    prefix = gather_blocks(pools, codes)
    part = query_part(
        [
            ((2, 1), [(0, 0, 0, WIDE)]),
            ((2, 3), [(1, 0, 0, WIDE)]),
            ((0, 2), [(1, WIDE, 0, HALF), (0, WIDE, HALF, HALF)]),
            ((1, 2), [(1, WIDE + HALF, 0, HALF), (0, WIDE + HALF, HALF, HALF)]),
            ((3, 2), [(1, 2 * WIDE, 0, HALF), (0, 2 * WIDE, HALF, HALF)]),
        ],
        [b5p, b5m],
        order,
        gains,
        w_query,
        part,
    )
    b7m, b7p, prefix, *part = bar((*s7, prefix, *part))
    (mine,) = assemble(
        [ksum, b7m, b7p],
        [
            (
                (WIDE, HD),
                [
                    (k * 128, 0, 128, HD, [(0, k * 128, 0), (1, HALF, k * HD), (2, HALF, k * HD)])
                    for k in range(4)
                ],
            )
        ],
    )
    other = hop(mine, "twin", 1)
    part = query_part(
        [
            ((2, 2), [(0, 0, 0, HALF), (1, 0, HALF, HALF)]),
        ],
        [b7m, b7p],
        order,
        gains,
        w_query,
        part,
    )
    heads_out, far = middle(
        *part, order, (mine, other), (cosine, sine), prefix, my_lengths, w_output
    )

    ra = both(far[0, :HALF], far[0, HALF:], "second")
    rb = both(
        stack_rows(far[1, :HALF], far[2, :HALF], far[3, :HALF]),
        stack_rows(far[1, HALF:], far[2, HALF:], far[3, HALF:]),
        "second",
    )
    spots = [(2, 1), (2, 3), (1, 1), (3, 1), (1, 3), (3, 3)]
    rest = output_part(heads_out, w_output, order, spots)
    ra_m, ra_p, rest = bar((*ra, rest))
    q21, q23, q11, q31, q13, q33 = [rest[n] for n in range(6)]
    rc = both(
        stack_rows(plus(q21[:HALF], ra_m), q21[HALF:]),
        stack_rows(q23[:HALF], plus(q23[HALF:], ra_p)),
        "second",
    )
    rb_m, rb_p = bar(rb)
    rd = both(
        stack_rows(
            plus(q11[:HALF], rb_m[:HALF]), q11[HALF:], plus(q31[:HALF], rb_m[HALF:WIDE]), q31[HALF:]
        ),
        stack_rows(
            q13[:HALF], plus(q13[HALF:], rb_p[:HALF]), q33[:HALF], plus(q33[HALF:], rb_p[HALF:WIDE])
        ),
        "second",
    )
    spots = [(2, 0), (0, 1), (0, 3), (1, 0), (3, 0), (0, 0)]
    heads_late, rb_m = bar((heads_out, rb_m))
    rest = output_part(heads_late, w_output, order, spots)
    rc_m, rc_p, rest = bar((*rc, rest))
    q20, q01, q03, q10, q30, q00 = [rest[n] for n in range(6)]
    sum2 = plus(q20, rc_m, rc_p)
    re = both(sum2[:HALF], sum2[HALF:], "first")
    re_m, re_p, rb_m, rb_p = bar((*re, rb_m, rb_p))
    rf = both(
        stack_rows(plus(q01[:HALF], rb_m[WIDE:]), q01[HALF:]),
        stack_rows(q03[:HALF], plus(q03[HALF:], rb_p[WIDE:])),
        "second",
    )
    rd_m, rd_p = bar(rd)
    sum1 = stack_rows(
        plus(q10[:HALF], rd_m[:HALF], rd_p[:HALF], re_m), plus(q10[HALF:], rd_m[HALF:WIDE], rd_p[HALF:WIDE])
    )
    sum3 = stack_rows(
        plus(q30[:HALF], rd_m[WIDE : WIDE + HALF], rd_p[WIDE : WIDE + HALF]),
        plus(q30[HALF:], rd_m[WIDE + HALF :], rd_p[WIDE + HALF :], re_p),
    )
    rg = both(sum1, sum3, "first")
    return plus(q00, *rf, *rg)


def solution(mesh):
    return jax.shard_map(
        local,
        mesh=mesh,
        in_specs=(
            P("branch", "tensor"),
            P(),
            P(None, "tensor"),
            P(None, "tensor", None),
            P("tensor", None),
            P(None, "branch", None, None),
            P(),
            P(),
        ),
        out_specs=P("branch", "tensor"),
        check_vma=False,
    )
```

```python
import math

import jax
import jax.numpy as jnp
from jax import lax
from jax.experimental import pallas as pl
from jax.experimental.pallas import tpu as pltpu
from jax.sharding import PartitionSpec as P

HEADS = 64
KVH = 8
HD = 128
PB = 64
PDEPTH = 4
HALF = 256
AXES = ("branch", "tensor")
F32 = jnp.float32
BF16 = jnp.bfloat16
MIB = 1024 * 1024


def pairs(move):
    table = []
    for z in range(4):
        for c in range(2):
            for x in range(4):
                for y in range(4):
                    z2, c2, x2, y2 = move(z, c, x, y)
                    target = ((z2 % 4) * 2 + c2 % 2) * 16 + (x2 % 4) * 4 + y2 % 4
                    table.append(((z * 2 + c) * 16 + x * 4 + y, target))
    return table


HOPS = {}
for step in (1, -1):
    HOPS["first", step] = pairs(
        lambda z, c, x, y, s=step: (z, c, x, y + s) if c == 0 else (z, c, x + s, y)
    )
    HOPS["second", step] = pairs(
        lambda z, c, x, y, s=step: (z, c, x + s, y) if c == 0 else (z, c, x, y + s)
    )
HOPS["twin", 1] = pairs(lambda z, c, x, y: (z, c, x, y ^ 1))
HOPS["z_one", 1] = pairs(lambda z, c, x, y: (z ^ 1 if c == 0 else 3 - z, c, x, y))
HOPS["z_two", 1] = pairs(lambda z, c, x, y: (3 - z if c == 0 else z ^ 1, c, x, y))
HOPS["core", 1] = pairs(lambda z, c, x, y: (z, c + 1, x, y))


def hop(value, axis, step):
    return lax.ppermute(value, AXES, HOPS[axis, step])


def both(forward, backward, axis):
    return hop(forward, axis, 1), hop(backward, axis, -1)


def stack_rows(*parts):
    return jnp.concatenate(parts, axis=0)


def plus(base, *terms):
    total = base.astype(F32)
    for term in terms:
        total = total + term.astype(F32)
    return total.astype(BF16)


def pack(block):
    quarter = block.shape[0] // 4
    return jnp.concatenate([block[k * quarter : (k + 1) * quarter] for k in range(4)], axis=1)


def unpack(block):
    return jnp.concatenate([block[:, k * HD : (k + 1) * HD] for k in range(4)], axis=0)


def params(mebibytes):
    return pltpu.CompilerParams(vmem_limit_bytes=mebibytes * MIB)


def estimate(flops, moved):
    return pl.CostEstimate(flops=flops, bytes_accessed=moved, transcendentals=0)


VMEM = pl.BlockSpec(memory_space=pltpu.VMEM)
SMEM = pl.BlockSpec(memory_space=pltpu.SMEM)
FIXED = pl.BlockSpec(memory_space=pltpu.HBM)
ANYWHERE = pl.BlockSpec(memory_space=pl.ANY)
GROUP = 2
CHUNK = 64
WIDE = 512


def in_vmem(arrays):
    return [pltpu.with_memory_space_constraint(a, pltpu.VMEM) for a in arrays]


def place_of(order_ref, i, j):
    return order_ref[i * 4 + j]


def assemble(arrays, outputs):
    n_arrays = len(arrays)

    def body(*refs):
        for o_ref, (_, pieces) in zip(refs[n_arrays:], outputs, strict=True):
            for row, column, rows, columns, terms in pieces:
                parts = [refs[a][r : r + rows, c : c + columns] for a, r, c in terms]
                if len(parts) > 1:
                    total = parts[0].astype(F32)
                    for part in parts[1:]:
                        total = total + part.astype(F32)
                    parts = [total.astype(BF16)]
                o_ref[row : row + rows, column : column + columns] = parts[0]

    return pl.pallas_call(
        body,
        out_shape=[pltpu.VMEM(shape, BF16) for shape, _ in outputs],
        in_specs=[VMEM] * n_arrays,
        out_specs=[VMEM] * len(outputs),
        compiler_params=params(4),
        cost_estimate=estimate(0, 0),
        name="assemble",
    )(*in_vmem(arrays))


def rows_piece(row, rows, *terms):
    return (row, 0, rows, WIDE, [(a, r, 0) for a, r in terms])


def packed(row, lanes, rows, *terms):
    quarter = rows // 4
    pieces = []
    for k in range(4):
        places = []
        for a, start, column in terms:
            if column is None:
                places.append((a, start, k * HD))
            else:
                places.append((a, start + k * quarter, column))
        pieces.append((row, k * HD, quarter, HD, places))
    return pieces


def kv_partial(tokens, gain, w_keyvalue, order, steps):
    spots = [(i, j) for i in steps for j in range(4)]
    count = len(spots)

    def body(order_ref, t_ref, g_ref, w_ref, o_ref, weights, sems):
        copies = []
        for n, (i, j) in enumerate(spots):
            target = place_of(order_ref, i, j)
            column = pl.multiple_of(lax.div(target, 2) * HD, HD)
            copies.append(
                pltpu.make_async_copy(
                    w_ref.at[lax.rem(target, 2), :, pl.ds(column, HD)],
                    weights.at[:, pl.ds(n * HD, HD)],
                    sems.at[n],
                )
            )
        for copy in copies:
            copy.start()
        own = g_ref[pl.ds(place_of(order_ref, 0, 0), 1), :]
        scaled = (t_ref[...].astype(F32) * own).astype(BF16)
        for copy in copies:
            copy.wait()
        for n in range(0, count * HD, WIDE):
            o_ref[:, n : n + WIDE] = jnp.dot(
                scaled, weights[:, n : n + WIDE], preferred_element_type=F32
            ).astype(BF16)

    return pl.pallas_call(
        body,
        out_shape=jax.ShapeDtypeStruct((WIDE, count * HD), BF16),
        in_specs=[SMEM, VMEM, VMEM, FIXED],
        out_specs=VMEM,
        scratch_shapes=[
            pltpu.VMEM((WIDE, count * HD), BF16),
            pltpu.SemaphoreType.DMA((count,)),
        ],
        compiler_params=params(5),
        cost_estimate=estimate(0, 0),
        name="kv_partial",
    )(order, tokens, gain, w_keyvalue)


def query_part(blocks, arrays, order, gain, w_query, carry):
    count = len(blocks)
    n_arrays = len(arrays)
    first = carry is None

    def body(order_ref, *refs):
        a_refs = refs[:n_arrays]
        g_ref, w_ref = refs[n_arrays : n_arrays + 2]
        q_ref, s_ref, scaled, weights, sems = refs[-5:]
        places = [place_of(order_ref, *spot) for spot, _ in blocks]

        def fetch(n):
            return pltpu.make_async_copy(
                w_ref.at[pl.ds(pl.multiple_of(places[n] * WIDE, WIDE), WIDE), :],
                weights.at[n // GROUP % 2, pl.ds(n % GROUP * WIDE, WIDE), :],
                sems.at[n],
            )

        for n in range(min(count, 2 * GROUP)):
            fetch(n).start()
        s_ref[...] = jnp.zeros_like(s_ref) if first else refs[n_arrays + 3][...]
        for low in range(0, count, GROUP):
            members = range(low, min(low + GROUP, count))
            for n in members:
                own = g_ref[pl.ds(places[n], 1), :]
                lanes_at = pl.ds((n - low) * WIDE, WIDE)
                for which, start, target, size in blocks[n][1]:

                    @pl.loop(0, size // CHUNK)
                    def _(step, which=which, start=start, target=target, own=own, lanes_at=lanes_at):
                        row = pl.multiple_of(step * CHUNK, CHUNK)
                        values = a_refs[which][pl.ds(start + row, CHUNK), :].astype(F32)
                        squares = values * values
                        lanes = squares[:, :HD]
                        for k in range(1, WIDE // HD):
                            lanes = lanes + squares[:, k * HD : (k + 1) * HD]
                        s_ref[pl.ds(target + row, CHUNK), :] += lanes
                        scaled[pl.ds(target + row, CHUNK), lanes_at] = (values * own).astype(BF16)

            for n in members:
                fetch(n).wait()
            depth = len(members) * WIDE
            for half in range(2):
                rows = slice(half * HALF, (half + 1) * HALF)
                product = jnp.dot(
                    scaled[rows, :depth], weights[low // GROUP % 2, :depth, :], preferred_element_type=F32
                )
                if low:
                    q_ref[rows, :] += product
                else:
                    q_ref[rows, :] = product if first else refs[n_arrays + 2][rows, :] + product
            for n in range(low + 2 * GROUP, min(low + 3 * GROUP, count)):
                fetch(n).start()

    carried = [] if first else list(carry)
    return pl.pallas_call(
        body,
        out_shape=(
            jax.ShapeDtypeStruct((WIDE, WIDE), F32),
            jax.ShapeDtypeStruct((WIDE, HD), F32),
        ),
        in_specs=[SMEM] + [VMEM] * n_arrays + [VMEM, FIXED] + [VMEM] * len(carried),
        out_specs=(VMEM, VMEM),
        scratch_shapes=[
            pltpu.VMEM((WIDE, GROUP * WIDE), BF16),
            pltpu.VMEM((2, GROUP * WIDE, WIDE), BF16),
            pltpu.SemaphoreType.DMA((count,)),
        ],
        input_output_aliases={} if first else {n_arrays + 3: 0, n_arrays + 4: 1},
        compiler_params=params(14),
        cost_estimate=estimate(0, 0),
        name="query_part",
    )(order, *in_vmem(arrays), gain, w_query, *in_vmem(carried))


def gather_blocks(pools, codes):
    branches = codes.shape[0]
    span = PDEPTH * PB + PB

    def body(code_ref, *refs):
        pool_refs, (o_ref, sems) = refs[:4], refs[4:]
        for b in range(branches):
            for d in range(PDEPTH):
                code = code_ref[b, d]
                slot, block = lax.rem(lax.div(code, 16), 2), lax.rem(code, 16)
                for which, source in enumerate(pool_refs):

                    @pl.when(lax.div(code, 32) == which)
                    def _(source=source):
                        pltpu.make_async_copy(
                            source.at[slot, :, block], o_ref.at[b, :, pl.ds(d * PB, PB), :], sems.at[b, d]
                        ).start()

        for b in range(branches):
            for d in range(PDEPTH):
                pltpu.make_async_copy(
                    pool_refs[0].at[0, :, 0], o_ref.at[b, :, pl.ds(d * PB, PB), :], sems.at[b, d]
                ).wait()

    return pl.pallas_call(
        body,
        out_shape=jax.ShapeDtypeStruct((branches, 2, span, HD), BF16),
        in_specs=[SMEM] + [ANYWHERE] * 4,
        out_specs=VMEM,
        scratch_shapes=[pltpu.SemaphoreType.DMA((branches, PDEPTH))],
        compiler_params=params(4),
        cost_estimate=estimate(0, 0),
        name="gather_blocks",
    )(codes, *pools)


def middle(query, squares, order, keyvalue, tables, prefix, lengths, w_output):
    branches = WIDE // PB
    heads = WIDE // HD
    span = PDEPTH * PB + PB
    scale = 1.0 / math.sqrt(HD)
    spots = [(2, 2), (1, 2), (3, 2), (0, 2)]

    def body(
        order_ref, len_ref, q_ref, s_ref, mine_ref, other_ref, cos_ref, sin_ref, prefix_ref, wo_ref,
        heads_ref, far_ref, kv_ref,
        wo, qb, wsems,
    ):
        copies = []
        for n, (i, j) in enumerate(spots):
            column = pl.multiple_of(place_of(order_ref, i, j) * WIDE, WIDE)
            copies.append(
                pltpu.make_async_copy(wo_ref.at[:, pl.ds(column, WIDE)], wo.at[n], wsems.at[n])
            )
        for copy in copies:
            copy.start()
        total = jnp.sum(s_ref[...], axis=1, keepdims=True)
        factor = lax.rsqrt(total * (1.0 / 8192.0) + 1e-06)
        cos_part = cos_ref[...] * factor
        sin_part = sin_ref[...] * factor

        def rope(v, cos_part, sin_part):
            return (v * cos_part + pltpu.roll(v, HD // 2, 1) * sin_part).astype(BF16)

        even = lax.rem(place_of(order_ref, 0, 0), 2) == 0
        mine, other = mine_ref[...].astype(F32), other_ref[...].astype(F32)
        new_keys = rope(jnp.where(even, mine, other), cos_part, sin_part)
        new_values = (jnp.where(even, other, mine) * factor).astype(BF16)
        for b in range(branches):
            kv_ref[b, 0, PDEPTH * PB :, :] = new_keys[b * PB : (b + 1) * PB]
            kv_ref[b, 1, PDEPTH * PB :, :] = new_values[b * PB : (b + 1) * PB]
        cos_part, sin_part = cos_part * scale, sin_part * scale
        for h in range(heads):
            qb[h] = rope(q_ref[:, h * HD : (h + 1) * HD], cos_part, sin_part)
        column = lax.broadcasted_iota(jnp.int32, (heads * PB, span), 1)
        within = lax.rem(lax.broadcasted_iota(jnp.int32, (heads * PB, span), 0), PB)
        own_seen = (column >= PDEPTH * PB) & (column - PDEPTH * PB <= within)
        for b in range(branches):
            queries = qb[:, b * PB : (b + 1) * PB, :].reshape(heads * PB, HD)
            scores = lax.dot_general(
                queries, kv_ref[b, 0], (((1,), (1,)), ((), ())), preferred_element_type=F32
            )
            seen = (column < len_ref[b] * PB) | own_seen
            scores = jnp.where(seen, scores, -1e30)
            highest = jnp.max(scores, axis=1, keepdims=True)
            expo = jnp.exp(scores - highest)
            inverse = 1.0 / jnp.sum(expo, axis=1, keepdims=True)
            mixed = jnp.dot(expo.astype(BF16), kv_ref[b, 1], preferred_element_type=F32)
            mixed = (mixed * inverse).astype(BF16)
            for h in range(heads):
                heads_ref[b * PB : (b + 1) * PB, h * HD : (h + 1) * HD] = mixed[
                    h * PB : (h + 1) * PB
                ]
        for n, copy in enumerate(copies):
            copy.wait()
            far_ref[n] = jnp.dot(heads_ref[...], wo[n], preferred_element_type=F32).astype(BF16)

    return pl.pallas_call(
        body,
        out_shape=(
            jax.ShapeDtypeStruct((WIDE, WIDE), BF16),
            jax.ShapeDtypeStruct((len(spots), WIDE, WIDE), BF16),
            jax.ShapeDtypeStruct(prefix.shape, BF16),
        ),
        in_specs=[SMEM] * 2 + [VMEM] * 7 + [FIXED],
        out_specs=(VMEM, VMEM, VMEM),
        scratch_shapes=[
            pltpu.VMEM((len(spots), WIDE, WIDE), BF16),
            pltpu.VMEM((heads, WIDE, HD), BF16),
            pltpu.SemaphoreType.DMA((len(spots),)),
        ],
        input_output_aliases={8: 2},
        compiler_params=params(9),
        cost_estimate=estimate(0, 0),
        name="middle",
    )(
        order, lengths, *in_vmem([query, squares, *keyvalue, *tables, prefix]), w_output
    )[:2]


def output_part(heads_out, w_output, order, spots):
    count = len(spots)

    def body(order_ref, h_ref, w_ref, o_ref, weights, sems):
        copies = []
        for n, (i, j) in enumerate(spots):
            column = pl.multiple_of(place_of(order_ref, i, j) * WIDE, WIDE)
            copies.append(
                pltpu.make_async_copy(w_ref.at[:, pl.ds(column, WIDE)], weights.at[n], sems.at[n])
            )
        for copy in copies:
            copy.start()
        for n, copy in enumerate(copies):
            copy.wait()
            o_ref[n] = jnp.dot(h_ref[...], weights[n], preferred_element_type=F32).astype(BF16)

    return pl.pallas_call(
        body,
        out_shape=jax.ShapeDtypeStruct((count, WIDE, WIDE), BF16),
        in_specs=[SMEM, VMEM, FIXED],
        out_specs=VMEM,
        scratch_shapes=[
            pltpu.VMEM((count, WIDE, WIDE), BF16),
            pltpu.SemaphoreType.DMA((count,)),
        ],
        compiler_params=params(6),
        cost_estimate=estimate(0, 0),
        name="output_part",
    )(order, heads_out, w_output)


def local(tokens, gain, w_query, w_keyvalue, w_output, cache, parents, lengths):
    bar = lax.optimization_barrier
    group = lax.axis_index("branch")
    place = lax.axis_index("tensor")
    x, y = place // 4, place % 4
    z, core = group // 2, group % 2
    row_count = tokens.shape[0]
    branch_count = row_count // PB

    count = jnp.arange(16, dtype=jnp.int32)
    i_step, j_step = count // 4, count % 4
    dx = jnp.where(core == 0, j_step, i_step)
    dy = jnp.where(core == 0, i_step, j_step)
    order = ((x + dx) % 4) * 4 + (y + dy) % 4
    gains = gain.astype(F32).reshape(16, WIDE)
    w_query, w_keyvalue, w_output = [
        pltpu.with_memory_space_constraint(w, pltpu.HBM) for w in (w_query, w_keyvalue, w_output)
    ]

    s1 = both(tokens, tokens, "first")
    kv_far = kv_partial(tokens, gains, w_keyvalue, order, (2,))
    k_far = both(kv_far[:HALF], kv_far[HALF:], "first")
    kv_near = kv_partial(tokens, gains, w_keyvalue, order, (0, 1, 3))
    kv_head = place * (w_query.shape[1] // HD) // (HEADS // KVH)
    cache_head = lax.dynamic_slice_in_dim(cache, kv_head * HD, HD, 3)
    z_one = hop(cache_head, "z_one", 1)
    b1m, b1p = bar(s1)
    (near,) = assemble(
        [tokens, b1p, b1m],
        [((3 * WIDE, WIDE), [rows_piece(n * WIDE, WIDE, (n, 0)) for n in range(3)])],
    )
    s2 = both(near, near, "second")
    k_m, k_p, kv_near, z_one, b1m, b1p = bar((*k_far, kv_near, z_one, b1m, b1p))
    s3 = both(
        *assemble(
            [b1m, b1p, kv_near, k_m, k_p],
            [
                (
                    (3 * HALF, WIDE),
                    [
                        rows_piece(0, HALF, (0, 0)),
                        (HALF, 0, HALF, WIDE, [(2, 0, WIDE), (3, 0, 0)]),
                        (2 * HALF, 0, HALF, WIDE, [(2, HALF, WIDE)]),
                    ],
                ),
                (
                    (3 * HALF, WIDE),
                    [
                        rows_piece(0, HALF, (1, HALF)),
                        (HALF, 0, HALF, WIDE, [(2, 0, 2 * WIDE)]),
                        (2 * HALF, 0, HALF, WIDE, [(2, HALF, 2 * WIDE), (4, 0, 0)]),
                    ],
                ),
            ],
        ),
        "first",
    )
    part = query_part(
        [((0, 0), [(0, 0, 0, WIDE)]), ((1, 0), [(1, 0, 0, WIDE)]), ((3, 0), [(2, 0, 0, WIDE)])],
        [tokens, b1p, b1m],
        order,
        gains,
        w_query,
        None,
    )
    pool = jnp.stack([cache_head, z_one])
    z_two = hop(pool, "z_two", 1)
    b3m, b3p, *part = bar((*s3, *part))
    ksum, to_next, to_last = assemble(
        [b3m, b3p, kv_near],
        [
            ((WIDE, WIDE), [(0, 0, WIDE, WIDE, [(2, 0, 0), (0, HALF, 0), (1, HALF, 0)])]),
            (
                (WIDE + HALF // 4, WIDE),
                [rows_piece(0, HALF, (0, 0)), rows_piece(HALF, HALF, (1, 0))]
                + packed(WIDE, 0, HALF, (2, 0, 2 * HD), (0, HALF, 2 * HD), (1, HALF, 2 * HD)),
            ),
            (
                (WIDE + HALF // 4, WIDE),
                [rows_piece(0, HALF, (0, 0)), rows_piece(HALF, HALF, (1, 0))]
                + packed(WIDE, 0, HALF, (2, HALF, 2 * HD), (0, 2 * HALF, 2 * HD), (1, 2 * HALF, 2 * HD)),
            ),
        ],
    )
    s5 = both(to_next, to_last, "second")
    near_twin = hop(pool, "core", 1)
    my_lengths = lax.dynamic_slice_in_dim(lengths, group * branch_count, branch_count, 0)
    my_parents = lax.dynamic_slice_in_dim(parents, group * branch_count, branch_count, 0)
    owner = my_parents // 16
    owner_z, owner_core = owner // 2, owner % 2
    across = z + 1 - 2 * (z % 2)
    partner = jnp.where(owner_core == 0, across, 3 - z)
    slot = jnp.where(
        owner_z == z, 0, jnp.where(owner_z == partner, 1, jnp.where(owner_z == (z + 2) % 4, 3, 2))
    )
    codes = jnp.where(owner_core == core, 0, 64) + slot * 16 + my_parents % 16

    positions = jnp.repeat(my_lengths, PB) * PB + jnp.tile(
        jnp.arange(PB, dtype=jnp.int32), branch_count
    )
    halfway = HD // 2
    frequency = jnp.exp(jnp.arange(halfway, dtype=F32) * (-2.0 * math.log(1000000.0) / HD))
    angles = positions.astype(F32)[:, None] * frequency[None, :]
    cosine, sine = jnp.cos(angles), jnp.sin(angles)
    cosine = jnp.concatenate([cosine, cosine], axis=1)
    sine = jnp.concatenate([-sine, sine], axis=1)

    b2m, b2p = bar(s2)
    s6 = both(
        *assemble(
            [b2m, b2p],
            [
                ((3 * HALF, WIDE), [rows_piece(n * HALF, HALF, (0, n * WIDE)) for n in range(3)]),
                ((3 * HALF, WIDE), [rows_piece(n * HALF, HALF, (1, n * WIDE + HALF)) for n in range(3)]),
            ],
        ),
        "second",
    )
    b5m, b5p, b2m, b2p, z_two, near_twin, cosine, sine, codes, *part = bar(
        (*s5, b2m, b2p, z_two, near_twin, cosine, sine, codes, *part)
    )
    quarter = HALF // 4
    s7 = both(
        *assemble(
            [b5m, b5p, ksum],
            [
                (
                    (HALF + WIDE // 4, WIDE),
                    [rows_piece(0, HALF, (0, 0))]
                    + [
                        piece
                        for k in range(4)
                        for piece in [
                            (
                                HALF,
                                k * HD,
                                2 * quarter,
                                HD,
                                [(2, k * 2 * quarter, HD)],
                            )
                        ]
                        if k >= 2
                    ]
                    + [
                        (
                            HALF + t * quarter,
                            k * HD,
                            quarter,
                            HD,
                            [(2, (2 * k + t) * quarter, HD), (0, WIDE, (2 * k + t) * HD)],
                        )
                        for k in range(2)
                        for t in range(2)
                    ],
                ),
                (
                    (HALF + WIDE // 4, WIDE),
                    [rows_piece(0, HALF, (1, HALF))]
                    + [
                        (HALF, k * HD, 2 * quarter, HD, [(2, k * 2 * quarter, 3 * HD)])
                        for k in range(2)
                    ]
                    + [
                        (
                            HALF + t * quarter,
                            k * HD,
                            quarter,
                            HD,
                            [(2, (2 * k + t) * quarter, 3 * HD), (1, WIDE, (2 * k + t - 4) * HD)],
                        )
                        for k in range(2, 4)
                        for t in range(2)
                    ],
                ),
            ],
        ),
        "second",
    )
    far_twin = hop(z_two, "core", 1)
    part = query_part(
        [
            ((2, 0), [(0, 0, 0, HALF), (1, 0, HALF, HALF)]),
            ((0, 1), [(2, 0, 0, WIDE)]),
            ((1, 1), [(2, WIDE, 0, WIDE)]),
            ((3, 1), [(2, 2 * WIDE, 0, WIDE)]),
            ((0, 3), [(3, 0, 0, WIDE)]),
            ((1, 3), [(3, WIDE, 0, WIDE)]),
            ((3, 3), [(3, 2 * WIDE, 0, WIDE)]),
            ((2, 1), [(4, 0, 0, WIDE)]),
            ((2, 3), [(5, 0, 0, WIDE)]),
        ],
        [b3m, b3p, b2p, b2m, b5p, b5m],
        order,
        gains,
        w_query,
        part,
    )
    b7m, b7p, b6m, b6p, far_twin, *part = bar((*s7, *s6, far_twin, *part))
    (mine,) = assemble(
        [ksum, b7m, b7p],
        [
            (
                (WIDE, HD),
                [
                    (k * 128, 0, 128, HD, [(0, k * 128, 0), (1, HALF, k * HD), (2, HALF, k * HD)])
                    for k in range(4)
                ],
            )
        ],
    )
    other = hop(mine, "twin", 1)
    pools = [
        pltpu.with_memory_space_constraint(a, pltpu.HBM) for a in (pool, z_two, near_twin, far_twin)
    ]
    prefix = gather_blocks(pools, codes)
    part = query_part(
        [
            ((0, 2), [(0, 0, 0, HALF), (1, 0, HALF, HALF)]),
            ((1, 2), [(0, HALF, 0, HALF), (1, HALF, HALF, HALF)]),
            ((3, 2), [(0, 2 * HALF, 0, HALF), (1, 2 * HALF, HALF, HALF)]),
            ((2, 2), [(2, 0, 0, HALF), (3, 0, HALF, HALF)]),
        ],
        [b6m, b6p, b7m, b7p],
        order,
        gains,
        w_query,
        part,
    )
    heads_out, far = middle(
        *part, order, (mine, other), (cosine, sine), prefix, my_lengths, w_output
    )

    ra = both(far[0, :HALF], far[0, HALF:], "second")
    rb = both(
        stack_rows(far[1, :HALF], far[2, :HALF], far[3, :HALF]),
        stack_rows(far[1, HALF:], far[2, HALF:], far[3, HALF:]),
        "second",
    )
    spots = [(2, 1), (2, 3), (1, 1), (3, 1), (1, 3), (3, 3)]
    rest = output_part(heads_out, w_output, order, spots)
    ra_m, ra_p, rest = bar((*ra, rest))
    q21, q23, q11, q31, q13, q33 = [rest[n] for n in range(6)]
    rc = both(
        stack_rows(plus(q21[:HALF], ra_m), q21[HALF:]),
        stack_rows(q23[:HALF], plus(q23[HALF:], ra_p)),
        "second",
    )
    rb_m, rb_p = bar(rb)
    rd = both(
        stack_rows(
            plus(q11[:HALF], rb_m[:HALF]), q11[HALF:], plus(q31[:HALF], rb_m[HALF:WIDE]), q31[HALF:]
        ),
        stack_rows(
            q13[:HALF], plus(q13[HALF:], rb_p[:HALF]), q33[:HALF], plus(q33[HALF:], rb_p[HALF:WIDE])
        ),
        "second",
    )
    spots = [(2, 0), (0, 1), (0, 3), (1, 0), (3, 0), (0, 0)]
    heads_late, rb_m = bar((heads_out, rb_m))
    rest = output_part(heads_late, w_output, order, spots)
    rc_m, rc_p, rest = bar((*rc, rest))
    q20, q01, q03, q10, q30, q00 = [rest[n] for n in range(6)]
    sum2 = plus(q20, rc_m, rc_p)
    re = both(sum2[:HALF], sum2[HALF:], "first")
    rf = both(
        stack_rows(plus(q01[:HALF], rb_m[WIDE:]), q01[HALF:]),
        stack_rows(q03[:HALF], plus(q03[HALF:], rb_p[WIDE:])),
        "second",
    )
    rd_m, rd_p, re_m, re_p = bar((*rd, *re))
    sum1 = stack_rows(
        plus(q10[:HALF], rd_m[:HALF], rd_p[:HALF], re_m), plus(q10[HALF:], rd_m[HALF:WIDE], rd_p[HALF:WIDE])
    )
    sum3 = stack_rows(
        plus(q30[:HALF], rd_m[WIDE : WIDE + HALF], rd_p[WIDE : WIDE + HALF]),
        plus(q30[HALF:], rd_m[WIDE + HALF :], rd_p[WIDE + HALF :], re_p),
    )
    rg = both(sum1, sum3, "first")
    return plus(q00, *rf, *rg)


def solution(mesh):
    return jax.shard_map(
        local,
        mesh=mesh,
        in_specs=(
            P("branch", "tensor"),
            P(),
            P(None, "tensor"),
            P(None, "tensor", None),
            P("tensor", None),
            P(None, "branch", None, None),
            P(),
            P(),
        ),
        out_specs=P("branch", "tensor"),
        check_vma=False,
    )
```
